32 devices in a mesh: batch: 4 (over y, x), seq: 8 (over z, core).
Axes of the slice: x: 2, y: 2, z: 4, core: 2. Of those that a mesh axis runs over, the one named last changes fastest.
Arguments:
- frames: float32 [16, 1024, 512], P('batch', 'seq'), may hold values from -6 to 6
- out_grad: float32 [16, 1024, 512], P('batch', 'seq'), may hold values from -6 to 6
- lengths: int32 [16], P('batch'), may hold values from 512 to 1024, as said below
- routing: int32 [16, 1024, 2], P('batch', 'seq'), may hold values from 0 to 7, all different within a row
- norm_gains: float32 [5, 512], replicated, may hold values from 0.25 to 1.75
- routers: float32 [2, 512, 8], replicated, may hold values from -0.1875 to 0.1875
- expert_in: float32 [2, 512, 16384], P(None, None, 'seq'), may hold values from -0.25 to 0.25
- expert_out: float32 [2, 16384, 512], P(None, 'seq'), may hold values from -1.5 to 1.5
- attn_qkv: float32 [512, 1536], replicated, may hold values from -0.25 to 0.25
- attn_out: float32 [512, 512], replicated, may hold values from -6 to 6
- conv_in: float32 [512, 1024], replicated, may hold values from -0.25 to 0.25
- depthwise: float32 [15, 512], replicated, may hold values from -1.5 to 1.5
- bn_gain: float32 [512], replicated, may hold values from 0.25 to 1.75
- bn_bias: float32 [512], replicated, may hold values from -3 to 3
- conv_out: float32 [512, 512], replicated, may hold values from -0.25 to 0.25
- running_mean: float32 [512], replicated, may hold values from -3 to 3
- running_var: float32 [512], replicated, may hold values from 0.5 to 2
Outputs:
- layer_out: float32 [16, 1024, 512], P('batch', 'seq')
- frames_grad: float32 [16, 1024, 512], P('batch', 'seq')
- norm_gains_grad: float32 [5, 512], replicated
- routers_grad: float32 [2, 512, 8], replicated
- expert_in_grad: float32 [2, 512, 16384], P(None, None, 'seq')
- expert_out_grad: float32 [2, 16384, 512], P(None, 'seq')
- attn_qkv_grad: float32 [512, 1536], replicated
- attn_out_grad: float32 [512, 512], replicated
- conv_in_grad: float32 [512, 1024], replicated
- depthwise_grad: float32 [15, 512], replicated
- bn_gain_grad: float32 [512], replicated
- bn_bias_grad: float32 [512], replicated
- conv_out_grad: float32 [512, 512], replicated
- new_mean: float32 [512], replicated
- new_var: float32 [512], replicated
The draws below stay inside these ranges and needn't reach their ends.
Inputs may be any that keep to these rules, and one draw needn't show every extreme that they name: `lengths`: of every 4 consecutive utterances, one has exactly 1024 live frames.
All inputs are finite; a program needn't handle non-finite values.
Results may differ from the reference program's by a relative error of at most 0.0003.
Values sent between devices are 32-bit elements; how exact they have to be, the bound alone decides.
A program may use at most 448 MiB of HBM per device.

```python
import math
import jax
import jax.numpy as jnp
from jax import lax

D = 512
FF = 2048
HEADS = 8
EXPERTS = 8
KERNEL = 15
FR_DEV = 128
UTT_DEV = 4
HEAD = 64
CAP = 64
UTTS = 16
LENGTH = 1024
N_BATCH = 4
N_SEQ = 8


def draw_lengths(key, part):
    key = jax.random.fold_in(key, 11)
    key_lengths, key_choice = jax.random.split(key)
    drawn = jax.random.randint(key_lengths, (UTTS,), LENGTH // 2, LENGTH + 1)
    picked = jax.random.randint(key_choice, (UTTS // UTT_DEV,), 0, UTT_DEV)
    full_mask = jnp.arange(UTTS) % UTT_DEV == jnp.repeat(picked, UTT_DEV)
    return jnp.where(full_mask, LENGTH, drawn).astype(jnp.int32)


def block_levels(key, dims, shards, smallest, top_value):
    factor_of = 1.0
    for dim, parts in shards:
        draws = jax.random.uniform(jax.random.fold_in(jax.random.fold_in(key, 6), dim), (parts,), jnp.float32, smallest / len(shards), top_value / len(shards))
        factor_of = factor_of * jnp.repeat(jnp.exp(draws), dims[dim] // parts).reshape((-1,) + (1,) * (len(dims) - 1 - dim))
    return factor_of


def distinct(rng, rows, number_of, top, lift):
    ranking = jax.random.permutation(jax.random.fold_in(rng, 1), number_of)
    boost = ranking
    for power in range(3):
        boost = boost * boost // number_of
    boost = boost * lift // number_of
    lots = jax.random.randint(jax.random.fold_in(rng, 2), (rows, number_of), 0, 4096) + boost
    holders = jax.random.permutation(jax.random.fold_in(rng, 3), rows)[jnp.arange(number_of) % rows]
    lots = jnp.where(jnp.arange(rows)[:, None] == holders[None, :], 1 << 14, lots)
    score = lots * number_of + jnp.arange(number_of)
    return lax.top_k(score.astype(jnp.int32), top)[1].astype(jnp.int32)


def scatter_about(stream_key, shape, spread, limit, shards=(), kind=jnp.bfloat16):
    values = jax.random.normal(stream_key, shape, jnp.float32) * spread
    if len(shards) > 0:
        values = block_levels(stream_key, shape, shards, -0.22, 0.18) * values
    return jnp.clip(values, min=-limit, max=limit).astype(kind)


def setup_inputs(seed: int = 0) -> dict:
    splits = jax.random.split(jax.random.key(seed), 18)
    frames = scatter_about(splits[0], (UTTS, LENGTH, D), 1.0, 6.0, ((0, 4), (1, 8)), jnp.float32)
    out_grad = scatter_about(splits[1], (UTTS, LENGTH, D), 1.0, 6.0, ((0, 4), (1, 8)), jnp.float32)
    lengths = draw_lengths(jax.random.fold_in(splits[17], 71), 0)
    routing = distinct(splits[3], UTTS * LENGTH, EXPERTS, 2, 4096).reshape((UTTS, LENGTH, 2))
    norm_gains = jnp.clip(1.0 + 0.15 * jax.random.normal(splits[4], (5, D), jnp.float32), 0.25, 1.75)
    routers = scatter_about(splits[5], (2, D, EXPERTS), (2 * D) ** -0.5, 0.1875, (), jnp.float32)
    expert_in = scatter_about(splits[6], (2, D, EXPERTS * FF), D ** -0.5, 0.25, ((2, 8),), jnp.float32)
    expert_out = scatter_about(splits[7], (2, EXPERTS * FF, D), (max(FF // 128, 1)) ** -0.5, 1.5, ((1, 8),), jnp.float32)
    attn_qkv = scatter_about(splits[8], (D, 3 * D), D ** -0.5, 0.25, (), jnp.float32)
    attn_out = scatter_about(splits[9], (D, D), (max(D // 512, 1)) ** -0.5, 6.0, (), jnp.float32)
    conv_in = scatter_about(splits[10], (D, 2 * D), D ** -0.5, 0.25, (), jnp.float32)
    depthwise = scatter_about(splits[11], (KERNEL, D), KERNEL ** -0.5, 1.5, (), jnp.float32)
    bn_gain = jnp.clip(1.0 + 0.15 * jax.random.normal(splits[12], (D,), jnp.float32), 0.25, 1.75)
    bn_bias = scatter_about(splits[13], (D,), 0.5, 3.0, (), jnp.float32)
    conv_out = scatter_about(splits[14], (D, D), D ** -0.5, 0.25, (), jnp.float32)
    running_mean = scatter_about(splits[15], (D,), 0.5, 3.0, (), jnp.float32)
    running_var = jnp.clip(jnp.exp(jax.random.uniform(splits[16], (D,), jnp.float32, math.log(0.5), math.log(2.0))), 0.5, 2.0)
    return dict(frames=frames, out_grad=out_grad, lengths=lengths, routing=routing, norm_gains=norm_gains, routers=routers, expert_in=expert_in, expert_out=expert_out, attn_qkv=attn_qkv, attn_out=attn_out, conv_in=conv_in, depthwise=depthwise, bn_gain=bn_gain, bn_bias=bn_bias, conv_out=conv_out, running_mean=running_mean, running_var=running_var)


HIGHEST_PRECISION = lax.Precision.HIGHEST
EPSILON = 1e-05
MOMENTUM = 0.1
NEGATIVE_FILL = -1e+30

@jax.custom_vjp
def low(v):
    return lax.optimization_barrier(v.astype(jnp.bfloat16)).astype(jnp.float32)

@jax.custom_vjp
def low_back(v):
    return v

def low_keep(v):
    return (low(v), None)

def low_pass(kept, grad):
    return (grad,)

def back_keep(v):
    return (v, None)

def back_low(kept, grad):
    return (low(grad),)
low.defvjp(low_keep, low_pass)
low_back.defvjp(back_keep, back_low)

def matmul(left_side, right_side):
    return jnp.dot(left_side, right_side, precision=HIGHEST_PRECISION, preferred_element_type=jnp.float32)

def layer_norm(values, gain_row):
    centered = values - lax.optimization_barrier(jnp.mean(values, axis=-1, keepdims=True))
    inverse_scale = lax.rsqrt(lax.optimization_barrier(jnp.mean(centered * centered, axis=-1, keepdims=True)) + EPSILON)
    return centered * inverse_scale * gain_row

def apply_swish(values):
    return values * jax.nn.sigmoid(values)

def rotate(values, positions):
    half_head = HEAD // 2
    frequency = 10000.0 ** (-jnp.arange(half_head, dtype=jnp.float32) / half_head)
    angles = positions.astype(jnp.float32)[:, None] * frequency[None, :]
    cosine = jnp.cos(angles)[:, None, :]
    sine_part = jnp.sin(angles)[:, None, :]
    shaped = values.reshape(values.shape[:-1] + (HEADS, HEAD))
    front_half = shaped[..., :half_head]
    back_half = shaped[..., half_head:]
    turned = jnp.concatenate([front_half * cosine - back_half * sine_part, back_half * cosine + front_half * sine_part], -1)
    return turned.reshape(values.shape)

def gate_of(tokens, router, routes):
    logits = matmul(tokens, router)
    probability = jax.nn.softmax(logits, axis=-1)
    chosen = routes[:, None] == jnp.arange(router.shape[1], dtype=jnp.int32)[None, :]
    return lax.optimization_barrier(jnp.sum(jnp.where(chosen, probability, 0.0), axis=-1))

def route_slots(routes, live_mask, experts, capacity):
    matches_expert = (routes[:, None] == jnp.arange(experts, dtype=jnp.int32)[None, :]) & live_mask[:, None]
    running_rank = jnp.cumsum(matches_expert.astype(jnp.int32), axis=0) - 1
    slot_rank = lax.optimization_barrier(jnp.sum(jnp.where(matches_expert, running_rank, 0), axis=-1))
    kept_mask = live_mask & (slot_rank < capacity)
    slot_index = jnp.where(kept_mask, routes * capacity + slot_rank, 0).astype(jnp.int32)
    slot_match = kept_mask[:, None] & (slot_index[:, None] == jnp.arange(experts * capacity, dtype=jnp.int32)[None, :])
    filled = jnp.any(slot_match, axis=0)
    source = lax.optimization_barrier(jnp.sum(jnp.where(slot_match, jnp.arange(routes.shape[0], dtype=jnp.int32)[:, None], 0), axis=0)).astype(jnp.int32)
    return (kept_mask, slot_index, filled, source)

def grouped(values):
    tail_shape = values.shape[2:]
    shaped = values.reshape((N_BATCH, UTT_DEV, N_SEQ, FR_DEV) + tail_shape)
    order = (0, 2, 1, 3) + tuple(range(4, 4 + len(tail_shape)))
    return shaped.transpose(order).reshape((N_BATCH * N_SEQ, UTT_DEV * FR_DEV) + tail_shape)

def ungrouped(values):
    tail_shape = values.shape[2:]
    shaped = values.reshape((N_BATCH, N_SEQ, UTT_DEV, FR_DEV) + tail_shape)
    order = (0, 2, 1, 3) + tuple(range(4, 4 + len(tail_shape)))
    return shaped.transpose(order).reshape((UTTS, LENGTH) + tail_shape)

def expert_apply(expert_args):
    slot_rows, inward, outward = expert_args
    flat_rows = slot_rows.reshape(-1, D)
    return matmul(apply_swish(matmul(flat_rows, inward)), outward).reshape(slot_rows.shape)

def mixture(normed, router, inward_all, outward_all, routes, live_mask):
    tokens = grouped(normed)
    group_routes = grouped(routes)
    group_live = grouped(live_mask)
    gate_values = gate_of(tokens.reshape(-1, D), router, group_routes.reshape(-1)).reshape(group_routes.shape)
    kept_mask, slot_index, filled, source = jax.vmap(lambda route_row, live_row: route_slots(route_row, live_row, EXPERTS, CAP))(group_routes, group_live)
    dispatched = jax.vmap(lambda token_rows, picks: token_rows[picks])(tokens, source) * filled[..., None].astype(jnp.float32)
    dispatched = dispatched.reshape(-1, EXPERTS, CAP, D).transpose(1, 0, 2, 3)
    inward_split = inward_all.reshape(D, EXPERTS, FF).transpose(1, 0, 2)
    outward_split = outward_all.reshape(EXPERTS, FF, D)
    returned = lax.map(jax.checkpoint(expert_apply), (dispatched, inward_split, outward_split))
    returned = returned.transpose(1, 0, 2, 3).reshape(-1, EXPERTS * CAP, D)
    gathered = jax.vmap(lambda slot_rows, picks: slot_rows[picks])(returned, slot_index)
    result = gathered * (gate_values * kept_mask.astype(jnp.float32))[..., None]
    return ungrouped(result)

def attend_one(inputs):
    query_rows, key_rows, value_rows, length = inputs
    usable = jnp.arange(LENGTH, dtype=jnp.int32) < length
    query_heads = query_rows.reshape(LENGTH, HEADS, HEAD)
    key_heads = key_rows.reshape(LENGTH, HEADS, HEAD)
    value_heads = value_rows.reshape(LENGTH, HEADS, HEAD)
    scores = jnp.einsum('qhc,khc->hqk', query_heads, key_heads, precision=HIGHEST_PRECISION, preferred_element_type=jnp.float32) * HEAD ** (-0.5)
    scores = jnp.where(usable[None, None, :], scores, NEGATIVE_FILL)
    weights = jax.nn.softmax(scores, axis=-1)
    attended = jnp.einsum('hqk,khc->qhc', weights, value_heads, precision=HIGHEST_PRECISION, preferred_element_type=jnp.float32)
    return attended.reshape(LENGTH, D)

def forward(frames, norm_gains, routers, expert_in, expert_out, attn_qkv, attn_out, conv_in, depthwise, bn_gain, bn_bias, conv_out, lengths, routing):
    positions = jnp.arange(LENGTH, dtype=jnp.int32)
    live_mask = positions[None, :] < lengths[:, None]
    live_float = live_mask.astype(jnp.float32)
    normed = layer_norm(frames, norm_gains[0])
    section_one = frames + 0.5 * mixture(normed, routers[0], expert_in[0], expert_out[0], routing[..., 0], live_mask)
    normed = layer_norm(section_one, norm_gains[1])
    projected = matmul(normed, attn_qkv)
    queries = rotate(projected[..., :D], positions)
    key_rows = rotate(projected[..., D:2 * D], positions)
    value_rows = projected[..., 2 * D:]
    attended = lax.map(jax.checkpoint(attend_one), (queries, key_rows, value_rows, lengths))
    section_two = section_one + matmul(attended, attn_out)
    normed = layer_norm(section_two, norm_gains[2])
    gate_input = matmul(normed, conv_in)
    glu_out = gate_input[..., :D] * jax.nn.sigmoid(gate_input[..., D:]) * live_float[..., None]
    rim_width = KERNEL // 2
    padded = jnp.pad(glu_out, ((0, 0), (rim_width, rim_width), (0, 0)))
    convolved = padded[:, 0:LENGTH] * depthwise[0]
    for offset in range(1, KERNEL):
        convolved = convolved + padded[:, offset:offset + LENGTH] * depthwise[offset]
    frame_count = jnp.sum(live_float)
    averaged = lax.optimization_barrier(jnp.sum(live_float[..., None] * convolved, axis=(0, 1))) / frame_count
    variance = lax.optimization_barrier(jnp.sum(live_float[..., None] * convolved * convolved, axis=(0, 1))) / frame_count - averaged * averaged
    normed_bn = (convolved - averaged) * lax.rsqrt(variance + EPSILON) * bn_gain + bn_bias
    section_three = section_two + matmul(apply_swish(normed_bn), conv_out)
    normed = layer_norm(section_three, norm_gains[3])
    section_four = section_three + 0.5 * mixture(normed, routers[1], expert_in[1], expert_out[1], routing[..., 1], live_mask)
    return (layer_norm(section_four, norm_gains[4]), (averaged, variance))

def reference(frames, out_grad, lengths, routing, norm_gains, routers, expert_in, expert_out, attn_qkv, attn_out, conv_in, depthwise, bn_gain, bn_bias, conv_out, running_mean, running_var):

    def whole_layer(*primals):
        return forward(*primals, lengths, routing)
    primals = (frames, norm_gains, routers, expert_in, expert_out, attn_qkv, attn_out, conv_in, depthwise, bn_gain, bn_bias, conv_out)
    layer_out, pullback, statistics = jax.vjp(whole_layer, *primals, has_aux=True)
    gradients = pullback(out_grad)
    averaged, variance = statistics
    frame_count = jnp.sum((jnp.arange(LENGTH, dtype=jnp.int32)[None, :] < lengths[:, None]).astype(jnp.float32))
    new_mean = (1.0 - MOMENTUM) * running_mean + MOMENTUM * averaged
    new_var = (1.0 - MOMENTUM) * running_var + MOMENTUM * variance * frame_count / (frame_count - 1.0)
    return (layer_out, gradients[0], gradients[1], gradients[2], gradients[3], gradients[4], gradients[5], gradients[6], gradients[7], gradients[8], gradients[9], gradients[10], gradients[11], new_mean, new_var)
```

```python
import jax
import jax.numpy as jnp
from jax import lax
from jax.sharding import PartitionSpec as P

HEADS = 8
EXPERTS = 8
KERNEL = 15
HEAD = 64
EPSILON = 1e-05
MOMENTUM = 0.1
NEGATIVE_FILL = -1e30
HIGH = lax.Precision.HIGH


def mm(left_side, right_side):
    return jnp.dot(left_side, right_side, precision=HIGH, preferred_element_type=jnp.float32)


def mm_tn(left_side, right_side):
    return lax.dot_general(
        left_side, right_side, (((0,), (0,)), ((), ())), precision=HIGH,
        preferred_element_type=jnp.float32,
    )


def mm_nt(left_side, right_side):
    return lax.dot_general(
        left_side, right_side, (((1,), (1,)), ((), ())), precision=HIGH,
        preferred_element_type=jnp.float32,
    )


def einsum_high(pattern, left_side, right_side):
    return jnp.einsum(
        pattern, left_side, right_side, precision=HIGH, preferred_element_type=jnp.float32
    )


def norm_stats(values):
    centered = values - jnp.mean(values, axis=-1, keepdims=True)
    inverse = lax.rsqrt(jnp.mean(centered * centered, axis=-1, keepdims=True) + EPSILON)
    return centered * inverse, inverse


def norm_back(grad, gain_row, unit, inverse):
    scaled = grad * gain_row
    return inverse * (
        scaled
        - jnp.mean(scaled, axis=-1, keepdims=True)
        - unit * jnp.mean(scaled * unit, axis=-1, keepdims=True)
    )


def swish(values):
    return values * jax.nn.sigmoid(values)


def swish_slope(values):
    gate = jax.nn.sigmoid(values)
    return gate * (1.0 + values * (1.0 - gate))


def seq_exchange(blocks):
    return lax.all_to_all(blocks, "seq", split_axis=0, concat_axis=0, tiled=True)


def frame_exchange(blocks):
    parts = blocks.shape[0]
    step = lax.axis_size("seq") // parts
    rings = [[part * step + low for part in range(parts)] for low in range(step)]
    return lax.all_to_all(
        blocks, "seq", split_axis=0, concat_axis=0, axis_index_groups=rings, tiled=True
    )


def near_pairs(step, shift):
    count = lax.axis_size("seq")
    return [(i, i // step * step + (i % step + shift) % step) for i in range(count)]


def near_gather(rows, step):
    return [rows] + [
        lax.ppermute(rows, "seq", near_pairs(step, step - shift)) for shift in range(1, step)
    ]


def near_sum(pieces, step):
    total = pieces[0]
    for shift in range(1, step):
        total = total + lax.ppermute(pieces[shift], "seq", near_pairs(step, shift))
    return total


def group_sum(rows, groups):
    total = rows
    for shift in range(1, groups):
        total = total + lax.ppermute(rows, "seq", near_pairs(groups, shift))
    return total


def batch_gather(rows):
    return lax.all_gather(rows, "batch", axis=0, tiled=False)


def slot_matrix(routes, live_flat, capacity):
    experts = jnp.arange(EXPERTS, dtype=jnp.int32)
    match = (routes[:, None] == experts[None, :]) & live_flat[:, None]
    rank = jnp.cumsum(match.astype(jnp.int32), axis=0) - 1
    rank = jnp.sum(jnp.where(match, rank, 0), axis=-1)
    kept = live_flat & (rank < capacity)
    slot = jnp.where(kept, routes * capacity + rank, -1)
    slots = jnp.arange(EXPERTS * capacity, dtype=jnp.int32)
    return kept, (slots[:, None] == slot[None, :]).astype(jnp.bfloat16)


def split_two(values):
    high = lax.reduce_precision(values, exponent_bits=8, mantissa_bits=7)
    return high.astype(jnp.bfloat16), (values - high).astype(jnp.bfloat16)


def pick(matrix, rows):
    width = rows.shape[-1]
    both = jnp.concatenate(split_two(rows), axis=-1)
    out = jnp.dot(matrix, both, preferred_element_type=jnp.float32)
    return out[:, :width] + out[:, width:]


def put(matrix, rows):
    width = rows.shape[-1]
    both = jnp.concatenate(split_two(rows), axis=-1)
    out = lax.dot_general(
        matrix, both, (((0,), (0,)), ((), ())), preferred_element_type=jnp.float32
    )
    return out[:, :width] + out[:, width:]


def dispatch(matrix, rows, capacity, groups):
    slots = pick(matrix, rows).reshape(EXPERTS, 1, capacity, -1)
    copies = jnp.broadcast_to(slots, (EXPERTS, groups, capacity, slots.shape[-1]))
    out = seq_exchange(copies.reshape(EXPERTS * groups, capacity, -1))
    return out.reshape(-1, out.shape[-1])


def give_back(matrix, rows, capacity, groups):
    out = seq_exchange(rows.reshape(EXPERTS * groups, capacity, -1))
    out = out.reshape(EXPERTS, groups, capacity, -1)[:, 0].reshape(EXPERTS * capacity, -1)
    return put(matrix, out)


def gate_rows(hidden, router, expert):
    logits = mm(hidden, router)
    prob = jax.nn.softmax(logits, axis=-1)
    chosen = (jnp.arange(EXPERTS, dtype=jnp.int32) == expert).astype(jnp.float32)[None, :]
    return prob, chosen, jnp.sum(prob * chosen, axis=-1, keepdims=True)


def expert_back(branch_grad, hidden, prob, chosen, gate, pre, branch, router, inward, outward, groups):
    gate_grad = jnp.sum(branch_grad * branch, axis=-1, keepdims=True)
    out_grad = branch_grad * gate
    pre_grad = mm_nt(out_grad, outward) * swish_slope(pre)
    logit_grad = gate_grad * gate * (chosen - prob)
    hidden_grad = group_sum(mm_nt(pre_grad, inward), groups) + mm_nt(logit_grad, router)
    return out_grad, hidden_grad, mm_tn(hidden, logit_grad)


def weight_grads(hidden_all, out_grad_all, inward, outward):
    members = lax.axis_size("batch")
    width = inward.shape[1] // members
    first = lax.axis_index("batch") * width
    inward_part = lax.dynamic_slice_in_dim(inward, first, width, axis=1)
    outward_part = lax.dynamic_slice_in_dim(outward, first, width, axis=0)
    hidden_all = hidden_all.reshape(-1, hidden_all.shape[-1])
    out_grad_all = out_grad_all.reshape(-1, out_grad_all.shape[-1])
    pre = mm(hidden_all, inward_part)
    outward_grad = mm_tn(swish(pre), out_grad_all)
    pre_grad = mm_nt(out_grad_all, outward_part) * swish_slope(pre)
    inward_grad = mm_tn(hidden_all, pre_grad)
    gathered = batch_gather(jnp.stack([inward_grad.T, outward_grad]))
    return (
        gathered[:, 0].reshape(-1, gathered.shape[-1]).T,
        gathered[:, 1].reshape(-1, gathered.shape[-1]),
    )


def turn(values, cosine, sine):
    shaped = values.reshape(values.shape[0], HEADS, HEAD)
    front, back = shaped[..., : HEAD // 2], shaped[..., HEAD // 2 :]
    turned = jnp.concatenate([front * cosine - back * sine, back * cosine + front * sine], -1)
    return turned.reshape(values.shape)


def heads_of(rows):
    return rows.reshape(rows.shape[0], HEADS, HEAD)


def attend(queries, keys, values, usable):
    scores = einsum_high("qhc,khc->hqk", heads_of(queries), heads_of(keys)) * HEAD ** (-0.5)
    scores = jnp.where(usable[None, None, :], scores, NEGATIVE_FILL)
    top = jnp.max(scores, axis=-1, keepdims=True)
    weights = jnp.exp(scores - top)
    total = jnp.sum(weights, axis=-1, keepdims=True)
    out = einsum_high("hqk,khc->hqc", weights, heads_of(values)) / total
    return out.transpose(1, 0, 2).reshape(queries.shape), top + jnp.log(total)


def attend_back(grad, attended, queries, keys, values, log_total, usable):
    scores = einsum_high("qhc,khc->hqk", heads_of(queries), heads_of(keys)) * HEAD ** (-0.5)
    scores = jnp.where(usable[None, None, :], scores, NEGATIVE_FILL)
    prob = jnp.exp(scores - log_total)
    out_dot = jnp.sum(heads_of(grad * attended), axis=-1).T[..., None]
    prob_grad = einsum_high("qhc,khc->hqk", heads_of(grad), heads_of(values))
    score_grad = prob * (prob_grad - out_dot) * HEAD ** (-0.5)
    query_grad = einsum_high("hqk,khc->qhc", score_grad, heads_of(keys)).reshape(queries.shape)
    key_grad = einsum_high("hqk,qhc->khc", score_grad, heads_of(queries)).reshape(keys.shape)
    value_grad = einsum_high("hqk,qhc->khc", prob, heads_of(grad)).reshape(keys.shape)
    return query_grad, key_grad, value_grad


def with_rims(blocks, step, rim):
    low = lax.axis_index("seq") % step
    none = jnp.zeros_like(blocks[:1, :rim])
    before = lax.ppermute(blocks[:, -rim:], "seq", near_pairs(step, 1))
    after = lax.ppermute(blocks[:, :rim], "seq", near_pairs(step, step - 1))
    before = jnp.where(low == 0, jnp.concatenate([none, before[:-1]], axis=0), before)
    after = jnp.where(low == step - 1, jnp.concatenate([after[1:], none], axis=0), after)
    return jnp.concatenate([before, blocks, after], axis=1)


def per_device(
    frames, out_grad, lengths, routing, norm_gains, routers, expert_in, expert_out,
    attn_qkv, attn_out, conv_in, depthwise, bn_gain, bn_bias, conv_out, running_mean, running_var,
):
    utter_count, frame_rows, width = frames.shape
    members = lax.axis_size("seq")
    step = members // utter_count
    groups = members // EXPERTS
    capacity = utter_count * frame_rows // EXPERTS
    place = lax.axis_index("seq")
    expert = place // groups
    first_copy = (place % groups == 0).astype(jnp.float32)
    row_ids = jnp.arange(frame_rows, dtype=jnp.int32)
    live_here = (place * frame_rows + row_ids)[None, :] < lengths[:, None]
    flat_frames = frames.reshape(-1, width)
    flat_grad = out_grad.reshape(-1, width)
    kept_one, slots_one = slot_matrix(routing[..., 0].reshape(-1), live_here.reshape(-1), capacity)
    kept_two, slots_two = slot_matrix(routing[..., 1].reshape(-1), live_here.reshape(-1), capacity)

    rows_one = dispatch(slots_one, flat_frames, capacity, groups)
    out_grad_rows = dispatch(slots_two, flat_grad, capacity, groups)
    unit_one, inverse_one = norm_stats(rows_one)
    hidden_one = unit_one * norm_gains[0]
    prob_one, chosen, gate_one = gate_rows(hidden_one, routers[0], expert)
    pre_one = mm(hidden_one, expert_in[0])
    branch_one = group_sum(mm(swish(pre_one), expert_out[0]), groups)
    hidden_one_all = batch_gather(hidden_one)
    section_one = flat_frames + give_back(slots_one, 0.5 * gate_one * branch_one, capacity, groups)

    section_one = frame_exchange(section_one.reshape(frames.shape)).reshape(-1, width)
    utter = place // step
    low = place % step
    length = lax.dynamic_index_in_dim(lengths, utter, keepdims=False)
    parts = jnp.arange(utter_count, dtype=jnp.int32)

    def positions_of(offset):
        other = (low + offset) % step
        return ((parts * step + other)[:, None] * frame_rows + row_ids[None, :]).reshape(-1)

    positions = positions_of(0)
    live = (positions < length).astype(jnp.float32)[:, None]
    half = HEAD // 2
    frequency = 10000.0 ** (-jnp.arange(half, dtype=jnp.float32) / half)
    angles = positions.astype(jnp.float32)[:, None] * frequency[None, :]
    cosine, sine = jnp.cos(angles)[:, None, :], jnp.sin(angles)[:, None, :]
    unit_two, inverse_two = norm_stats(section_one)
    hidden_two = unit_two * norm_gains[1]
    projected = mm(hidden_two, attn_qkv)
    queries = turn(projected[:, :width], cosine, sine)
    key_values = jnp.concatenate(
        [turn(projected[:, width : 2 * width], cosine, sine), projected[:, 2 * width :]], axis=-1
    )
    key_values = jnp.concatenate(near_gather(key_values, step), axis=0)
    keys, values = key_values[:, :width], key_values[:, width:]
    usable = jnp.concatenate([positions_of(i) for i in range(step)]) < length
    attended, log_total = attend(queries, keys, values, usable)
    section_two = section_one + mm(attended, attn_out)
    unit_three, inverse_three = norm_stats(section_two)
    hidden_three = unit_three * norm_gains[2]
    glu_in = mm(hidden_three, conv_in)
    glu_gate = jax.nn.sigmoid(glu_in[:, width:])
    glu = glu_in[:, :width] * glu_gate * live
    rim = KERNEL // 2
    block_shape = (utter_count, frame_rows, width)
    padded = with_rims(glu.reshape(block_shape), step, rim)
    convolved = padded[:, 0:frame_rows] * depthwise[0]
    for offset in range(1, KERNEL):
        convolved = convolved + padded[:, offset : offset + frame_rows] * depthwise[offset]
    convolved = convolved.reshape(-1, width)
    sums = lax.psum(
        jnp.stack(
            [
                jnp.sum(live * convolved, axis=0),
                jnp.sum(live * convolved * convolved, axis=0),
                jnp.broadcast_to(jnp.sum(live), (width,)),
            ]
        ),
        ("batch", "seq"),
    )
    frame_count = sums[2]
    averaged = sums[0] / frame_count
    variance = sums[1] / frame_count - averaged * averaged
    bn_inverse = lax.rsqrt(variance + EPSILON)
    bn_unit = (convolved - averaged) * bn_inverse
    normed = bn_unit * bn_gain + bn_bias
    activated = swish(normed)
    section_three = section_two + mm(activated, conv_out)

    section_three = frame_exchange(section_three.reshape(block_shape)).reshape(-1, width)
    rows_two = dispatch(slots_two, section_three, capacity, groups)
    unit_four, inverse_four = norm_stats(rows_two)
    hidden_four = unit_four * norm_gains[3]
    prob_two, chosen, gate_two = gate_rows(hidden_four, routers[1], expert)
    pre_two = mm(hidden_four, expert_in[1])
    branch_two = group_sum(mm(swish(pre_two), expert_out[1]), groups)
    unit_five, inverse_five = norm_stats(rows_two + 0.5 * gate_two * branch_two)
    last_rows = unit_five * norm_gains[4]
    gain_five = first_copy * jnp.sum(out_grad_rows * unit_five, axis=0)
    rows_four_grad = norm_back(out_grad_rows, norm_gains[4], unit_five, inverse_five)
    hidden_two_all = batch_gather(hidden_four)
    branch_grad_two, hidden_four_grad, router_two = expert_back(
        0.5 * rows_four_grad, hidden_four, prob_two, chosen, gate_two, pre_two, branch_two,
        routers[1], expert_in[1], expert_out[1], groups,
    )
    gain_four = first_copy * jnp.sum(hidden_four_grad * unit_four, axis=0)
    rows_three_grad = rows_four_grad + norm_back(
        hidden_four_grad, norm_gains[3], unit_four, inverse_four
    )
    back_rows = give_back(slots_two, rows_three_grad, capacity, groups)
    last_back = give_back(slots_two, last_rows, capacity, groups)
    drop_two = 1.0 - kept_two.astype(jnp.float32)[:, None]
    unit_plain, inverse_plain = norm_stats(section_three)
    layer_out = last_back + drop_two * (unit_plain * norm_gains[4])
    gain_five = gain_five + jnp.sum(drop_two * flat_grad * unit_plain, axis=0)
    grad_three = back_rows + drop_two * norm_back(
        flat_grad, norm_gains[4], unit_plain, inverse_plain
    )
    inward_two, outward_two = weight_grads(
        hidden_two_all, batch_gather(branch_grad_two), expert_in[1], expert_out[1]
    )

    grad_three = frame_exchange(grad_three.reshape(block_shape)).reshape(-1, width)
    conv_out_grad = mm_tn(activated, grad_three)
    normed_grad = mm_nt(grad_three, conv_out) * swish_slope(normed)
    parts_sum = lax.psum(
        jnp.stack([jnp.sum(normed_grad * bn_unit, axis=0), jnp.sum(normed_grad, axis=0)]),
        ("batch", "seq"),
    )
    bn_gain_grad, bn_bias_grad = parts_sum[0], parts_sum[1]
    mean_grad = -bn_inverse * bn_gain * bn_bias_grad
    var_grad = -0.5 * bn_inverse * bn_inverse * bn_gain * bn_gain_grad
    conv_grad = bn_inverse * bn_gain * normed_grad + live * (
        (mean_grad - 2.0 * averaged * var_grad) / frame_count
        + convolved * (2.0 * var_grad / frame_count)
    )
    conv_blocks = conv_grad.reshape(block_shape)
    padded_grad = with_rims(conv_blocks, step, rim)
    glu_grad = padded_grad[:, 2 * rim : 2 * rim + frame_rows] * depthwise[0]
    for offset in range(1, KERNEL):
        first = 2 * rim - offset
        glu_grad = glu_grad + padded_grad[:, first : first + frame_rows] * depthwise[offset]
    depthwise_grad = jnp.stack(
        [
            jnp.sum(padded[:, offset : offset + frame_rows] * conv_blocks, axis=(0, 1))
            for offset in range(KERNEL)
        ]
    )
    glu_grad = glu_grad.reshape(-1, width) * live
    glu_in_grad = jnp.concatenate(
        [
            glu_grad * glu_gate,
            glu_grad * glu_in[:, :width] * glu_gate * (1.0 - glu_gate),
        ],
        axis=-1,
    )
    conv_in_grad = mm_tn(hidden_three, glu_in_grad)
    hidden_three_grad = mm_nt(glu_in_grad, conv_in)
    gain_three = jnp.sum(hidden_three_grad * unit_three, axis=0)
    grad_two = grad_three + norm_back(hidden_three_grad, norm_gains[2], unit_three, inverse_three)
    attn_out_grad = mm_tn(attended, grad_two)
    attended_grad = mm_nt(grad_two, attn_out)
    query_grad, key_grad, value_grad = attend_back(
        attended_grad, attended, queries, keys, values, log_total, usable
    )
    key_value_grad = jnp.concatenate([key_grad, value_grad], axis=-1)
    rows = key_value_grad.shape[0] // step
    key_value_grad = near_sum(
        [key_value_grad[i * rows : (i + 1) * rows] for i in range(step)], step
    )
    projected_grad = jnp.concatenate(
        [
            turn(query_grad, cosine, -sine),
            turn(key_value_grad[:, :width], cosine, -sine),
            key_value_grad[:, width:],
        ],
        axis=-1,
    )
    qkv_grad = mm_tn(hidden_two, projected_grad)
    hidden_two_grad = mm_nt(projected_grad, attn_qkv)
    gain_two = jnp.sum(hidden_two_grad * unit_two, axis=0)
    grad_one = grad_two + norm_back(hidden_two_grad, norm_gains[1], unit_two, inverse_two)

    grad_one = frame_exchange(grad_one.reshape(block_shape)).reshape(-1, width)
    grad_rows = dispatch(slots_one, grad_one, capacity, groups)
    branch_grad_one, hidden_one_grad, router_one = expert_back(
        0.5 * grad_rows, hidden_one, prob_one, chosen, gate_one, pre_one, branch_one,
        routers[0], expert_in[0], expert_out[0], groups,
    )
    gain_one = first_copy * jnp.sum(hidden_one_grad * unit_one, axis=0)
    extra = norm_back(hidden_one_grad, norm_gains[0], unit_one, inverse_one)
    frames_grad = grad_one + give_back(slots_one, extra, capacity, groups)
    inward_one, outward_one = weight_grads(
        hidden_one_all, batch_gather(branch_grad_one), expert_in[0], expert_out[0]
    )
    gains_grad = jnp.stack([gain_one, gain_two, gain_three, gain_four, gain_five])
    routers_grad = first_copy * jnp.stack([router_one, router_two])
    (gains_grad, routers_grad, qkv_grad, attn_out_grad, conv_in_grad, depthwise_grad, conv_out_grad) = (
        lax.psum(
            (gains_grad, routers_grad, qkv_grad, attn_out_grad, conv_in_grad, depthwise_grad, conv_out_grad),
            ("batch", "seq"),
        )
    )
    new_mean = (1.0 - MOMENTUM) * running_mean + MOMENTUM * averaged
    new_var = (1.0 - MOMENTUM) * running_var + MOMENTUM * variance * frame_count / (
        frame_count - 1.0
    )
    return (
        layer_out.reshape(frames.shape), frames_grad.reshape(frames.shape), gains_grad, routers_grad,
        jnp.stack([inward_one, inward_two]), jnp.stack([outward_one, outward_two]),
        qkv_grad, attn_out_grad, conv_in_grad, depthwise_grad, bn_gain_grad, bn_bias_grad,
        conv_out_grad, new_mean, new_var,
    )


def solution(mesh):
    frame_spec = P("batch", "seq", None)
    in_specs = (
        frame_spec, frame_spec, P("batch"), frame_spec, P(), P(),
        P(None, None, "seq"), P(None, "seq", None),
    ) + (P(),) * 9
    out_specs = (
        frame_spec, frame_spec, P(), P(), P(None, None, "seq"), P(None, "seq", None),
    ) + (P(),) * 9
    return jax.shard_map(
        per_device, mesh=mesh, in_specs=in_specs, out_specs=out_specs, check_vma=False
    )
```

```python
import functools
import math

import jax
import jax.numpy as jnp
from jax import lax
from jax.experimental import pallas as pl
from jax.experimental.pallas import tpu as pltpu
from jax.sharding import PartitionSpec as P

HEADS = 8
EXPERTS = 8
KERNEL = 15
HEAD = 64
EPSILON = 1e-05
MOMENTUM = 0.1
NEGATIVE_FILL = -1e30
HIGH = lax.Precision.HIGH
MESH = pl.DeviceIdType.MESH
F32 = jnp.float32
BF16 = jnp.bfloat16
LANES = 128
SCORE_SCALE = HEAD ** (-0.5) / math.log(2.0)
VMEM_BYTES = 52 * 1024 * 1024


def mm(left_side, right_side):
    return jnp.dot(left_side, right_side, precision=HIGH, preferred_element_type=jnp.float32)


def mm_tn(left_side, right_side):
    return lax.dot_general(
        left_side, right_side, (((0,), (0,)), ((), ())), precision=HIGH,
        preferred_element_type=jnp.float32,
    )


def mm_nt(left_side, right_side):
    return lax.dot_general(
        left_side, right_side, (((1,), (1,)), ((), ())), precision=HIGH,
        preferred_element_type=jnp.float32,
    )


def einsum_high(pattern, left_side, right_side):
    return jnp.einsum(
        pattern, left_side, right_side, precision=HIGH, preferred_element_type=jnp.float32
    )


def norm_stats(values):
    centered = values - jnp.mean(values, axis=-1, keepdims=True)
    inverse = lax.rsqrt(jnp.mean(centered * centered, axis=-1, keepdims=True) + EPSILON)
    return centered * inverse, inverse


def norm_back(grad, gain_row, unit, inverse):
    scaled = grad * gain_row
    return inverse * (
        scaled
        - jnp.mean(scaled, axis=-1, keepdims=True)
        - unit * jnp.mean(scaled * unit, axis=-1, keepdims=True)
    )


def swish(values):
    return values * jax.nn.sigmoid(values)


def swish_slope(values):
    gate = jax.nn.sigmoid(values)
    return gate * (1.0 + values * (1.0 - gate))


def seq_exchange(blocks):
    return lax.all_to_all(blocks, "seq", split_axis=0, concat_axis=0, tiled=True)


def frame_exchange(blocks):
    parts = blocks.shape[0]
    step = lax.axis_size("seq") // parts
    rings = [[part * step + low for part in range(parts)] for low in range(step)]
    return lax.all_to_all(
        blocks, "seq", split_axis=0, concat_axis=0, axis_index_groups=rings, tiled=True
    )


def near_pairs(step, shift):
    count = lax.axis_size("seq")
    return [(i, i // step * step + (i % step + shift) % step) for i in range(count)]


def near_gather(rows, step):
    return [rows] + [
        lax.ppermute(rows, "seq", near_pairs(step, step - shift)) for shift in range(1, step)
    ]


def near_sum(pieces, step):
    total = pieces[0]
    for shift in range(1, step):
        total = total + lax.ppermute(pieces[shift], "seq", near_pairs(step, shift))
    return total


def group_sum(rows, groups):
    total = rows
    for shift in range(1, groups):
        total = total + lax.ppermute(rows, "seq", near_pairs(groups, shift))
    return total


def batch_gather(rows):
    return lax.all_gather(rows, "batch", axis=0, tiled=False)


def slot_matrix(routes, live_flat, capacity):
    experts = jnp.arange(EXPERTS, dtype=jnp.int32)
    match = (routes[:, None] == experts[None, :]) & live_flat[:, None]
    rank = jnp.cumsum(match.astype(jnp.int32), axis=0) - 1
    rank = jnp.sum(jnp.where(match, rank, 0), axis=-1)
    kept = live_flat & (rank < capacity)
    slot = jnp.where(kept, routes * capacity + rank, -1)
    slots = jnp.arange(EXPERTS * capacity, dtype=jnp.int32)
    return kept, (slots[:, None] == slot[None, :]).astype(jnp.bfloat16)


def split_two(values):
    high = lax.reduce_precision(values, exponent_bits=8, mantissa_bits=7)
    return high.astype(jnp.bfloat16), (values - high).astype(jnp.bfloat16)


def pick(matrix, rows):
    width = rows.shape[-1]
    both = jnp.concatenate(split_two(rows), axis=-1)
    out = jnp.dot(matrix, both, preferred_element_type=jnp.float32)
    return out[:, :width] + out[:, width:]


def put(matrix, rows):
    width = rows.shape[-1]
    both = jnp.concatenate(split_two(rows), axis=-1)
    out = lax.dot_general(
        matrix, both, (((0,), (0,)), ((), ())), preferred_element_type=jnp.float32
    )
    return out[:, :width] + out[:, width:]


def dispatch(matrix, rows, capacity, groups):
    slots = pick(matrix, rows).reshape(EXPERTS, 1, capacity, -1)
    copies = jnp.broadcast_to(slots, (EXPERTS, groups, capacity, slots.shape[-1]))
    out = seq_exchange(copies.reshape(EXPERTS * groups, capacity, -1))
    return out.reshape(-1, out.shape[-1])


def give_back(matrix, rows, capacity, groups):
    out = seq_exchange(rows.reshape(EXPERTS * groups, capacity, -1))
    out = out.reshape(EXPERTS, groups, capacity, -1)[:, 0].reshape(EXPERTS * capacity, -1)
    return put(matrix, out)


def gate_rows(hidden, router, expert):
    logits = mm(hidden, router)
    prob = jax.nn.softmax(logits, axis=-1)
    chosen = (jnp.arange(EXPERTS, dtype=jnp.int32) == expert).astype(jnp.float32)[None, :]
    return prob, chosen, jnp.sum(prob * chosen, axis=-1, keepdims=True)


def expert_back(branch_grad, hidden, prob, chosen, gate, pre, branch, router, inward, outward, groups):
    gate_grad = jnp.sum(branch_grad * branch, axis=-1, keepdims=True)
    out_grad = branch_grad * gate
    pre_grad = mm_nt(out_grad, outward) * swish_slope(pre)
    logit_grad = gate_grad * gate * (chosen - prob)
    hidden_grad = group_sum(mm_nt(pre_grad, inward), groups) + mm_nt(logit_grad, router)
    return out_grad, hidden_grad, mm_tn(hidden, logit_grad)


def weight_grads(hidden_all, out_grad_all, inward, outward):
    members = lax.axis_size("batch")
    width = inward.shape[1] // members
    first = lax.axis_index("batch") * width
    inward_part = lax.dynamic_slice_in_dim(inward, first, width, axis=1)
    outward_part = lax.dynamic_slice_in_dim(outward, first, width, axis=0)
    hidden_all = hidden_all.reshape(-1, hidden_all.shape[-1])
    out_grad_all = out_grad_all.reshape(-1, out_grad_all.shape[-1])
    pre = mm(hidden_all, inward_part)
    outward_grad = mm_tn(swish(pre), out_grad_all)
    pre_grad = mm_nt(out_grad_all, outward_part) * swish_slope(pre)
    inward_grad = mm_tn(hidden_all, pre_grad)
    gathered = batch_gather(jnp.stack([inward_grad.T, outward_grad]))
    return (
        gathered[:, 0].reshape(-1, gathered.shape[-1]).T,
        gathered[:, 1].reshape(-1, gathered.shape[-1]),
    )


def whole(shape):
    rank = len(shape)
    return pl.BlockSpec(shape, lambda *ids: (0,) * rank)


def plain_call(kernel, outs, args, scratch=(), flops=0):
    moved = sum(math.prod(a.shape) * 4 for a in args) + sum(math.prod(o) * 4 for o in outs)
    return pl.pallas_call(
        kernel,
        out_shape=[jax.ShapeDtypeStruct(o, F32) for o in outs],
        scratch_shapes=list(scratch),
        compiler_params=pltpu.CompilerParams(vmem_limit_bytes=VMEM_BYTES),
        cost_estimate=pl.CostEstimate(flops=flops, bytes_accessed=moved, transcendentals=0),
    )(*args)


def halves(values):
    high = values.astype(BF16)
    return high, (values - high.astype(F32)).astype(BF16)


NN = (((1,), (0,)), ((), ()))
NT = (((1,), (1,)), ((), ()))
TN = (((0,), (0,)), ((), ()))


def dot3(left, right, dims=NN):
    left_high, left_low = left
    right_high, right_low = right
    return (
        lax.dot_general(left_high, right_high, dims, preferred_element_type=F32)
        + lax.dot_general(left_high, right_low, dims, preferred_element_type=F32)
        + lax.dot_general(left_low, right_high, dims, preferred_element_type=F32)
    )


def dot2(left, right, dims=NN):
    left_high, left_low = left
    return lax.dot_general(left_high, right, dims, preferred_element_type=F32) + lax.dot_general(
        left_low, right, dims, preferred_element_type=F32
    )


def rotated(values, cosine, sine, lane):
    ahead = pltpu.roll(values, LANES - HEAD // 2, 1)
    behind = pltpu.roll(values, HEAD // 2, 1)
    other = jnp.where(lane % HEAD < HEAD // 2, ahead, behind)
    return values * cosine + other * sine


def project_kernel(x_ref, gain_ref, weight_ref, cos_ref, sin_ref, q_ref, kv_ref):
    width = x_ref.shape[1]
    unit, _ = norm_stats(x_ref[...])
    hidden = halves(unit * gain_ref[...])
    lane = lax.broadcasted_iota(jnp.int32, (1, LANES), 1)
    cosine, sine = cos_ref[...], sin_ref[...]
    for part in range(3):
        out = dot3(hidden, halves(weight_ref[:, part * width : (part + 1) * width]))
        for first in range(0, width, LANES):
            piece = out[:, first : first + LANES]
            if part < 2:
                piece = rotated(piece, cosine, sine, lane)
            if part == 0:
                q_ref[:, first : first + LANES] = piece
            else:
                start = (part - 1) * width + first
                kv_ref[:, start : start + LANES] = piece


def one_head(values, head, lane):
    return jnp.where((lane < HEAD) == (head == 0), values, pltpu.roll(values, HEAD, 1))


def high_low(values):
    high = values.astype(BF16).astype(F32)
    return high, values - high


def query_side(values, extra, lane):
    high, low = high_low(values)
    return jnp.concatenate([high, jnp.where(lane < HEAD, low, extra)], axis=1).astype(BF16)


def key_side(values, extra, lane):
    high, low = high_low(values)
    first = jnp.where(lane < HEAD, high, low)
    return jnp.concatenate([first, jnp.where(lane < HEAD, high, extra)], axis=1).astype(BF16)


def both_parts(values, lane):
    high, low = high_low(values)
    return jnp.where(lane < HEAD, high, low).astype(BF16)


def in_parts(column, lane, first):
    high, rest = high_low(column)
    middle, low = high_low(rest)
    return jnp.where(
        lane == first,
        high,
        jnp.where(lane == first + 1, middle, jnp.where(lane == first + 2, low, 0.0)),
    )


def attention_kernel(
    q_ref, k_ref, v_ref, extra_ref, x_ref, out_weight_ref, gain_ref, in_weight_ref, live_ref,
    att_ref, lse_ref, x2_ref, glu_in_ref, glu_ref, att_all,
):
    pair = pl.program_id(0)
    rows = q_ref.shape[0]
    width = x_ref.shape[1]
    tile = min(256, rows)
    lane = lax.broadcasted_iota(jnp.int32, (1, LANES), 1)
    one_at = jnp.where(lane == HEAD, 1.0, 0.0).astype(F32)
    ones_column = jnp.where(lane == 0, 1.0, 0.0).astype(F32)
    keys_count = k_ref.shape[0]
    outs = []
    for head in range(2):
        key_pack = key_side(one_head(k_ref[...], head, lane), extra_ref[...], lane)
        value_high, value_low = high_low(one_head(v_ref[...], head, lane))
        value_pack = jnp.concatenate(
            [
                jnp.where(lane < HEAD, value_high, value_low),
                jnp.broadcast_to(ones_column, (keys_count, LANES)),
            ],
            axis=1,
        ).astype(BF16)
        per_tile = []
        for first in range(0, rows, tile):
            queries = one_head(q_ref[first : first + tile, :] * SCORE_SCALE, head, lane)
            query_pack = query_side(queries, one_at, lane)
            scores = lax.dot_general(query_pack, key_pack, NT, preferred_element_type=F32)
            top = jnp.max(scores, axis=1, keepdims=True)
            weights = halves(jnp.exp2(scores - top))
            summed = dot2(weights, value_pack)
            total = summed[:, LANES : LANES + 1]
            mixed = summed[:, :LANES]
            mixed = (mixed + pltpu.roll(mixed, HEAD, 1)) / total
            log_total = jnp.broadcast_to(top + jnp.log2(total), mixed.shape)
            per_tile.append((mixed, log_total))
        outs.append(per_tile)
    for index, first in enumerate(range(0, rows, tile)):
        (mixed_a, log_a), (mixed_b, log_b) = outs[0][index], outs[1][index]
        mixed = jnp.where(lane < HEAD, mixed_a, mixed_b)
        att_ref[first : first + tile, :] = mixed
        lse_ref[first : first + tile, :] = jnp.where(lane < HEAD, log_a, log_b)
        att_all[pair, first : first + tile, :] = mixed

    @pl.when(pair == pl.num_programs(0) - 1)
    def _():
        pairs = att_all.shape[0]
        attended = jnp.concatenate([att_all[i] for i in range(pairs)], axis=1)
        x2 = x_ref[...] + dot3(halves(attended), halves(out_weight_ref[...]))
        x2_ref[...] = x2
        unit, _ = norm_stats(x2)
        hidden = halves(unit * gain_ref[...])
        left = dot3(hidden, halves(in_weight_ref[:, :width]))
        right = dot3(hidden, halves(in_weight_ref[:, width:]))
        glu_in_ref[:, :width] = left
        glu_in_ref[:, width:] = right
        glu_ref[...] = left * jax.nn.sigmoid(right) * live_ref[...]


def attention_block(queries, keys, values, extra, x1, out_weight, gain_row, in_weight, live):
    rows, width = queries.shape
    count = keys.shape[0]
    pairs = width // LANES
    lanes_of = lambda height: pl.BlockSpec((height, LANES), lambda i: (0, i))
    return pl.pallas_call(
        attention_kernel,
        grid=(pairs,),
        in_specs=[
            lanes_of(rows), lanes_of(count), lanes_of(count), whole(extra.shape), whole(x1.shape),
            whole(out_weight.shape), whole(gain_row.shape), whole(in_weight.shape), whole(live.shape),
        ],
        out_specs=[
            lanes_of(rows), lanes_of(rows), whole((rows, width)), whole((rows, 2 * width)),
            whole((rows, width)),
        ],
        out_shape=[
            jax.ShapeDtypeStruct((rows, w), F32) for w in (width, width, width, 2 * width, width)
        ],
        scratch_shapes=[pltpu.VMEM((pairs, rows, LANES), F32)],
        compiler_params=pltpu.CompilerParams(vmem_limit_bytes=VMEM_BYTES),
        cost_estimate=pl.CostEstimate(
            flops=20_000_000_000, bytes_accessed=20_000_000, transcendentals=0
        ),
    )(queries, keys, values, extra, x1, out_weight, gain_row, in_weight, live)


def attention_back_kernel(
    q_ref, grad_ref, att_ref, k_ref, v_ref, lse_ref, extra_ref, dqt_ref, dk_ref, dv_ref, packs
):
    rows = q_ref.shape[0]
    count = k_ref.shape[0]
    tile = 256
    lane = lax.broadcasted_iota(jnp.int32, (1, LANES), 1)
    one_at = jnp.where(lane == HEAD, 1.0, 0.0).astype(F32)
    product = grad_ref[...] * att_ref[...]
    for head in range(2):
        mine = (lane < HEAD) == (head == 0)
        out_dot = jnp.sum(jnp.where(mine, product, 0.0), axis=1, keepdims=True)
        log_total = one_head(lse_ref[...], head, lane)
        queries = one_head(q_ref[...] * SCORE_SCALE, head, lane)
        grads = one_head(grad_ref[...], head, lane)
        query_pack = query_side(queries, one_at + in_parts(-log_total, lane, HEAD + 1), lane)
        dots = jnp.broadcast_to(-out_dot, grads.shape)
        grad_pack = query_side(grads, in_parts(dots, lane, HEAD + 1), lane)
        query_both = both_parts(queries, lane)
        grad_both = both_parts(grads, lane)
        packs[...] = jnp.zeros_like(packs)

        def step(index, carry):
            first = pl.multiple_of(index * tile, tile)
            extra = extra_ref[pl.ds(first, tile), :]
            keys = one_head(k_ref[pl.ds(first, tile), :], head, lane)
            values = one_head(v_ref[pl.ds(first, tile), :], head, lane)
            scores = lax.dot_general(
                key_side(keys, extra, lane), query_pack, NT, preferred_element_type=F32
            )
            prob = jnp.exp2(scores)
            score_grad = prob * lax.dot_general(
                key_side(values, extra, lane), grad_pack, NT, preferred_element_type=F32
            )
            value_grad = dot2(halves(prob), grad_both)
            parts = halves(score_grad)
            key_grad = dot2(parts, query_both) * math.log(2.0)
            value_grad = value_grad + pltpu.roll(value_grad, HEAD, 1)
            key_grad = key_grad + pltpu.roll(key_grad, HEAD, 1)
            if head == 0:
                dv_ref[pl.ds(first, tile), :] = value_grad
                dk_ref[pl.ds(first, tile), :] = key_grad
            else:
                dv_ref[pl.ds(first, tile), :] = jnp.where(
                    mine, value_grad, dv_ref[pl.ds(first, tile), :]
                )
                dk_ref[pl.ds(first, tile), :] = jnp.where(
                    mine, key_grad, dk_ref[pl.ds(first, tile), :]
                )
            key_both = both_parts(keys, lane)
            packs[...] += lax.dot_general(
                key_both, parts[0], TN, preferred_element_type=F32
            ) + lax.dot_general(key_both, parts[1], TN, preferred_element_type=F32)
            return carry

        lax.fori_loop(0, count // tile, step, 0)
        dqt_ref[head * HEAD : (head + 1) * HEAD, :] = (
            packs[:HEAD, :] + packs[HEAD:, :]
        ) * HEAD ** (-0.5)


def attention_back_block(queries, grad, attended, keys, values, lse, extra):
    rows, width = queries.shape
    count = keys.shape[0]
    pairs = width // LANES
    lanes_of = lambda height: pl.BlockSpec((height, LANES), lambda i: (0, i))
    return pl.pallas_call(
        attention_back_kernel,
        grid=(pairs,),
        in_specs=[
            lanes_of(rows), lanes_of(rows), lanes_of(rows), lanes_of(count), lanes_of(count),
            lanes_of(rows), whole(extra.shape),
        ],
        out_specs=[
            pl.BlockSpec((LANES, rows), lambda i: (i, 0)), lanes_of(count), lanes_of(count),
        ],
        out_shape=[
            jax.ShapeDtypeStruct((width, rows), F32),
            jax.ShapeDtypeStruct((count, width), F32),
            jax.ShapeDtypeStruct((count, width), F32),
        ],
        scratch_shapes=[pltpu.VMEM((LANES, rows), F32)],
        compiler_params=pltpu.CompilerParams(vmem_limit_bytes=VMEM_BYTES),
        cost_estimate=pl.CostEstimate(
            flops=40_000_000_000, bytes_accessed=20_000_000, transcendentals=0
        ),
    )(queries, grad, attended, keys, values, lse, extra)


def project_back_kernel(
    dqt_ref, dkv_ref, x_ref, gain_ref, weight_ref, cos_ref, sin_ref, upper_ref,
    dw_ref, gain_grad_ref, dx_ref,
):
    width = x_ref.shape[1]
    unit, inverse = norm_stats(x_ref[...])
    gain_row = gain_ref[...]
    hidden = halves(unit * gain_row)
    lane = lax.broadcasted_iota(jnp.int32, (1, LANES), 1)
    cosine, sine = cos_ref[...], -sin_ref[...]
    hidden_grad = jnp.zeros(x_ref.shape, F32)
    for part in range(3):
        if part == 0:
            grad = dqt_ref[...].T
        else:
            grad = dkv_ref[:, (part - 1) * width : part * width]
        if part < 2:
            grad = jnp.concatenate(
                [
                    rotated(grad[:, i : i + LANES], cosine, sine, lane)
                    for i in range(0, width, LANES)
                ],
                axis=1,
            )
        grad = halves(grad)
        dw_ref[:, part * width : (part + 1) * width] = dot3(hidden, grad, TN)
        hidden_grad += dot3(grad, halves(weight_ref[:, part * width : (part + 1) * width]), NT)
    gain_grad_ref[...] = jnp.sum(hidden_grad * unit, axis=0, keepdims=True)
    dx_ref[...] = upper_ref[...] + norm_back(hidden_grad, gain_row, unit, inverse)


RIM = 8


def pad_blocks(pad_ref, before_ref, block_ref, after_ref):
    rows = block_ref.shape[1]
    pad_ref[:, :RIM, :] = before_ref[...]
    pad_ref[:, RIM : RIM + rows, :] = block_ref[...]
    pad_ref[:, RIM + rows :, :] = after_ref[...]


def conv_kernel(before_ref, glu_ref, after_ref, taps_ref, live_ref, out_ref, sums_ref, pad_ref):
    parts, rows, width = glu_ref.shape
    pad_blocks(pad_ref, before_ref, glu_ref, after_ref)
    sums_ref[...] = jnp.zeros_like(sums_ref)

    def step(part, carry):
        alive = live_ref[part]
        for first in range(0, width, LANES):
            columns = slice(first, first + LANES)
            total = jnp.zeros((rows, LANES), F32)
            for tap in range(KERNEL):
                total = total + pad_ref[part, 1 + tap : 1 + tap + rows, columns] * taps_ref[
                    tap : tap + 1, columns
                ]
            out_ref[part, :, columns] = total
            kept = alive * total
            sums_ref[0:1, columns] += jnp.sum(kept, axis=0, keepdims=True)
            sums_ref[1:2, columns] += jnp.sum(kept * total, axis=0, keepdims=True)
            sums_ref[2:3, columns] += jnp.sum(
                jnp.broadcast_to(alive, (rows, LANES)), axis=0, keepdims=True
            )
        return carry

    lax.fori_loop(0, parts, step, 0)


def conv_stats(sums):
    count = sums[2:3]
    averaged = sums[0:1] / count
    return count, averaged, sums[1:2] / count - averaged * averaged


def conv_tail_kernel(conv_ref, sums_ref, gain_ref, bias_ref, weight_ref, x2_ref, x3_ref):
    count, averaged, variance = conv_stats(sums_ref[...])
    scale = lax.rsqrt(variance + EPSILON)
    normed = (conv_ref[...] - averaged) * scale * gain_ref[...] + bias_ref[...]
    x3_ref[...] = x2_ref[...] + dot3(halves(swish(normed)), halves(weight_ref[...]))


def conv_tail_back_kernel(
    grad_ref, conv_ref, sums_ref, gain_ref, bias_ref, weight_ref, ng_ref, dw_ref, out_sums_ref
):
    count, averaged, variance = conv_stats(sums_ref[...])
    scale = lax.rsqrt(variance + EPSILON)
    unit = (conv_ref[...] - averaged) * scale
    normed = unit * gain_ref[...] + bias_ref[...]
    grad = halves(grad_ref[...])
    dw_ref[...] = dot3(halves(swish(normed)), grad, TN)
    normed_grad = dot3(grad, halves(weight_ref[...]), NT) * swish_slope(normed)
    ng_ref[...] = normed_grad
    out_sums_ref[...] = jnp.zeros_like(out_sums_ref)
    out_sums_ref[0:1, :] = jnp.sum(normed_grad * unit, axis=0, keepdims=True)
    out_sums_ref[1:2, :] = jnp.sum(normed_grad, axis=0, keepdims=True)


def conv_back_kernel(
    cg_before_ref, cg_ref, cg_after_ref, glu_before_ref, glu_ref, glu_after_ref, taps_ref,
    live_ref, taps_grad_ref, dglu_ref, pad_ref, glu_pad_ref, sums_ref,
):
    parts, rows, width = cg_ref.shape
    pad_blocks(pad_ref, cg_before_ref, cg_ref, cg_after_ref)
    pad_blocks(glu_pad_ref, glu_before_ref, glu_ref, glu_after_ref)
    sums_ref[...] = jnp.zeros_like(sums_ref)

    def step(part, carry):
        alive = live_ref[part]
        for first in range(0, width, LANES):
            columns = slice(first, first + LANES)
            total = jnp.zeros((rows, LANES), F32)
            here = cg_ref[part, :, columns]
            for tap in range(KERNEL):
                start = KERNEL - tap
                total = total + pad_ref[part, start : start + rows, columns] * taps_ref[
                    tap : tap + 1, columns
                ]
                product = glu_pad_ref[part, 1 + tap : 1 + tap + rows, columns] * here
                sums_ref[tap, :, columns] += jnp.sum(
                    product.reshape(rows // 8, 8, LANES), axis=0
                )
            dglu_ref[part, :, columns] = total * alive
        return carry

    lax.fori_loop(0, parts, step, 0)
    for tap in range(KERNEL):
        taps_grad_ref[tap : tap + 1, :] = jnp.sum(sums_ref[tap], axis=0, keepdims=True)


def glu_back_kernel(
    dglu_ref, glu_in_ref, x2_ref, gain_ref, in_weight_ref, grad_ref, att_ref, out_weight_ref,
    dw_in_ref, gain_grad_ref, dx2_ref, dw_out_ref, datt_ref,
):
    width = x2_ref.shape[1]
    unit, inverse = norm_stats(x2_ref[...])
    gain_row = gain_ref[...]
    hidden = halves(unit * gain_row)
    dglu = dglu_ref[...]
    left, gate = glu_in_ref[:, :width], jax.nn.sigmoid(glu_in_ref[:, width:])
    left_grad = halves(dglu * gate)
    right_grad = halves(dglu * left * gate * (1.0 - gate))
    dw_in_ref[:, :width] = dot3(hidden, left_grad, TN)
    dw_in_ref[:, width:] = dot3(hidden, right_grad, TN)
    hidden_grad = dot3(left_grad, halves(in_weight_ref[:, :width]), NT) + dot3(
        right_grad, halves(in_weight_ref[:, width:]), NT
    )
    gain_grad_ref[...] = jnp.sum(hidden_grad * unit, axis=0, keepdims=True)
    dx2 = grad_ref[...] + norm_back(hidden_grad, gain_row, unit, inverse)
    dx2_ref[...] = dx2
    dx2 = halves(dx2)
    dw_out_ref[...] = dot3(halves(att_ref[...]), dx2, TN)
    datt_ref[...] = dot3(dx2, halves(out_weight_ref[...]), NT)


def small_sum_kernel(rows, columns, x_ref, o_ref, row_buf, col_buf, send_b, recv_b, send_s, recv_s):
    b, s = lax.axis_index("batch"), lax.axis_index("seq")
    barrier = pltpu.get_barrier_semaphore()
    row_peers = [(lax.rem(b + off, rows), s) for off in range(1, rows)]
    col_peers = [(b, lax.rem(s + off, columns)) for off in range(1, columns)]
    for peer in row_peers + col_peers:
        pl.semaphore_signal(barrier, inc=1, device_id=peer, device_id_type=MESH)
    pl.semaphore_wait(barrier, len(row_peers) + len(col_peers))

    def share(source, buf, send, recv, mine, peers, count, axis):
        buf[mine] = source
        copies = []
        for off, peer in enumerate(peers):
            copies.append(
                pltpu.make_async_remote_copy(
                    src_ref=buf.at[mine], dst_ref=buf.at[mine], send_sem=send.at[off],
                    recv_sem=recv.at[mine], device_id=peer, device_id_type=MESH,
                )
            )
        for copy in copies:
            copy.start()
        for off, peer in enumerate(peers):
            other = peer[axis]
            pltpu.make_async_remote_copy(
                src_ref=buf.at[other], dst_ref=buf.at[other], send_sem=send.at[off],
                recv_sem=recv.at[other], device_id=peer, device_id_type=MESH,
            ).wait_recv()
        for copy in copies:
            copy.wait_send()
        total = buf[0]
        for i in range(1, count):
            total = total + buf[i]
        return total

    total = share(x_ref[...], row_buf, send_b, recv_b, b, row_peers, rows, 0)
    o_ref[...] = share(total, col_buf, send_s, recv_s, s, col_peers, columns, 1)


def small_sum(values, collective_id):
    rows, columns = lax.axis_size("batch"), lax.axis_size("seq")
    return pl.pallas_call(
        functools.partial(small_sum_kernel, rows, columns),
        out_shape=jax.ShapeDtypeStruct(values.shape, F32),
        in_specs=[pl.BlockSpec(memory_space=pltpu.VMEM)],
        out_specs=pl.BlockSpec(memory_space=pltpu.VMEM),
        scratch_shapes=[
            pltpu.VMEM((rows,) + values.shape, F32),
            pltpu.VMEM((columns,) + values.shape, F32),
            pltpu.SemaphoreType.DMA((rows,)),
            pltpu.SemaphoreType.DMA((rows,)),
            pltpu.SemaphoreType.DMA((columns,)),
            pltpu.SemaphoreType.DMA((columns,)),
        ],
        compiler_params=pltpu.CompilerParams(collective_id=collective_id, has_side_effects=True),
    )(values)


def rims_of(blocks, step):
    low = lax.axis_index("seq") % step
    none = jnp.zeros_like(blocks[:1, :RIM])
    before = lax.ppermute(blocks[:, -RIM:], "seq", near_pairs(step, 1))
    after = lax.ppermute(blocks[:, :RIM], "seq", near_pairs(step, step - 1))
    before = jnp.where(low == 0, jnp.concatenate([none, before[:-1]], axis=0), before)
    after = jnp.where(low == step - 1, jnp.concatenate([after[1:], none], axis=0), after)
    return before, after


def after_of(values, first):
    return lax.optimization_barrier((values, first))[0]


def per_device(
    frames, out_grad, lengths, routing, norm_gains, routers, expert_in, expert_out,
    attn_qkv, attn_out, conv_in, depthwise, bn_gain, bn_bias, conv_out, running_mean, running_var,
):
    utter_count, frame_rows, width = frames.shape
    members = lax.axis_size("seq")
    step = members // utter_count
    groups = members // EXPERTS
    capacity = utter_count * frame_rows // EXPERTS
    place = lax.axis_index("seq")
    expert = place // groups
    first_copy = (place % groups == 0).astype(jnp.float32)
    row_ids = jnp.arange(frame_rows, dtype=jnp.int32)
    live_here = (place * frame_rows + row_ids)[None, :] < lengths[:, None]
    flat_frames = frames.reshape(-1, width)
    flat_grad = out_grad.reshape(-1, width)
    kept_one, slots_one = slot_matrix(routing[..., 0].reshape(-1), live_here.reshape(-1), capacity)
    kept_two, slots_two = slot_matrix(routing[..., 1].reshape(-1), live_here.reshape(-1), capacity)

    rows_one = dispatch(slots_one, flat_frames, capacity, groups)
    out_grad_rows = dispatch(slots_two, flat_grad, capacity, groups)
    unit_one, inverse_one = norm_stats(rows_one)
    hidden_one = unit_one * norm_gains[0]
    prob_one, chosen, gate_one = gate_rows(hidden_one, routers[0], expert)
    pre_one = mm(hidden_one, expert_in[0])
    branch_one = group_sum(mm(swish(pre_one), expert_out[0]), groups)
    hidden_one_all = batch_gather(hidden_one)
    section_one = flat_frames + give_back(slots_one, 0.5 * gate_one * branch_one, capacity, groups)

    section_one = frame_exchange(section_one.reshape(frames.shape)).reshape(-1, width)
    rows = utter_count * frame_rows
    utter = place // step
    low = place % step
    length = lax.dynamic_index_in_dim(lengths, utter, keepdims=False)
    parts = jnp.arange(utter_count, dtype=jnp.int32)

    def positions_of(offset):
        other = (low + offset) % step
        return ((parts * step + other)[:, None] * frame_rows + row_ids[None, :]).reshape(-1)

    positions = positions_of(0)
    live = (positions < length).astype(jnp.float32)[:, None]
    half = HEAD // 2
    frequency = 10000.0 ** (-jnp.arange(half, dtype=F32) / half)
    angles = positions.astype(F32)[:, None] * frequency[None, :]
    cosine, sine = jnp.cos(angles), jnp.sin(angles)
    cosine = jnp.concatenate([cosine] * (LANES // half), axis=1)
    sine = jnp.concatenate([-sine, sine] * (LANES // HEAD), axis=1)
    usable = jnp.concatenate([positions_of(i) for i in range(step)]) < length
    lane = jnp.arange(LANES)[None, :]
    extra = jnp.where(
        lane == HEAD,
        jnp.where(usable, 0.0, NEGATIVE_FILL)[:, None],
        ((lane > HEAD) & (lane < HEAD + 4)).astype(F32),
    )
    gain_rows = norm_gains.reshape(5, 1, width)
    queries, key_values = plain_call(
        project_kernel, [(rows, width), (rows, 2 * width)],
        [section_one, gain_rows[1], attn_qkv, cosine, sine], flops=2_500_000_000,
    )
    key_values = jnp.concatenate(near_gather(key_values, step), axis=0)
    keys, values = key_values[:, :width], key_values[:, width:]
    attended, log_total, section_two, glu_in, glu = attention_block(
        queries, keys, values, extra, section_one, attn_out, gain_rows[2], conv_in, live
    )
    block_shape = (utter_count, frame_rows, width)
    glu = glu.reshape(block_shape)
    glu_before, glu_after = rims_of(glu, step)
    taps = jnp.concatenate([depthwise, jnp.zeros((1, width), F32)], axis=0)
    live_blocks = live.reshape(utter_count, frame_rows, 1)
    pad_shape = pltpu.VMEM((utter_count, frame_rows + 2 * RIM, width), F32)
    convolved, sums = plain_call(
        conv_kernel, [block_shape, (8, width)], [glu_before, glu, glu_after, taps, live_blocks],
        scratch=[pad_shape],
    )
    convolved = convolved.reshape(rows, width)
    sums = small_sum(sums, 0)
    bn_rows = (bn_gain.reshape(1, width), bn_bias.reshape(1, width))
    (section_three,) = plain_call(
        conv_tail_kernel, [(rows, width)],
        [convolved, sums, *bn_rows, conv_out, section_two], flops=800_000_000,
    )
    frame_count = sums[2]
    averaged = sums[0] / frame_count
    variance = sums[1] / frame_count - averaged * averaged
    bn_inverse = lax.rsqrt(variance + EPSILON)

    section_three = frame_exchange(section_three.reshape(block_shape)).reshape(-1, width)
    rows_two = dispatch(slots_two, section_three, capacity, groups)
    unit_four, inverse_four = norm_stats(rows_two)
    hidden_four = unit_four * norm_gains[3]
    prob_two, chosen, gate_two = gate_rows(hidden_four, routers[1], expert)
    pre_two = mm(hidden_four, expert_in[1])
    branch_two = group_sum(mm(swish(pre_two), expert_out[1]), groups)
    unit_five, inverse_five = norm_stats(rows_two + 0.5 * gate_two * branch_two)
    last_rows = unit_five * norm_gains[4]
    gain_five = first_copy * jnp.sum(out_grad_rows * unit_five, axis=0)
    rows_four_grad = norm_back(out_grad_rows, norm_gains[4], unit_five, inverse_five)
    hidden_two_all = batch_gather(hidden_four)
    branch_grad_two, hidden_four_grad, router_two = expert_back(
        0.5 * rows_four_grad, hidden_four, prob_two, chosen, gate_two, pre_two, branch_two,
        routers[1], expert_in[1], expert_out[1], groups,
    )
    gain_four = first_copy * jnp.sum(hidden_four_grad * unit_four, axis=0)
    rows_three_grad = rows_four_grad + norm_back(
        hidden_four_grad, norm_gains[3], unit_four, inverse_four
    )
    back_rows = give_back(slots_two, rows_three_grad, capacity, groups)
    last_back = give_back(slots_two, last_rows, capacity, groups)
    drop_two = 1.0 - kept_two.astype(jnp.float32)[:, None]
    unit_plain, inverse_plain = norm_stats(section_three)
    layer_out = last_back + drop_two * (unit_plain * norm_gains[4])
    gain_five = gain_five + jnp.sum(drop_two * flat_grad * unit_plain, axis=0)
    grad_three = back_rows + drop_two * norm_back(
        flat_grad, norm_gains[4], unit_plain, inverse_plain
    )
    inward_two, outward_two = weight_grads(
        hidden_two_all, batch_gather(branch_grad_two), expert_in[1], expert_out[1]
    )

    grad_three = frame_exchange(grad_three.reshape(block_shape)).reshape(-1, width)
    normed_grad, conv_out_grad, parts_sum = plain_call(
        conv_tail_back_kernel, [(rows, width), (width, width), (8, width)],
        [grad_three, convolved, sums, *bn_rows, conv_out], flops=1_600_000_000,
    )
    parts_sum = small_sum(parts_sum, 1)
    bn_gain_grad, bn_bias_grad = parts_sum[0], parts_sum[1]
    mean_grad = -bn_inverse * bn_gain * bn_bias_grad
    var_grad = -0.5 * bn_inverse * bn_inverse * bn_gain * bn_gain_grad
    conv_grad = bn_inverse * bn_gain * normed_grad + live * (
        (mean_grad - 2.0 * averaged * var_grad) / frame_count
        + convolved * (2.0 * var_grad / frame_count)
    )
    conv_grad = conv_grad.reshape(block_shape)
    grad_before, grad_after = rims_of(conv_grad, step)
    depthwise_grad, glu_grad = plain_call(
        conv_back_kernel, [(KERNEL + 1, width), block_shape],
        [grad_before, conv_grad, grad_after, glu_before, glu, glu_after, taps, live_blocks],
        scratch=[pad_shape, pad_shape, pltpu.VMEM((KERNEL, 8, width), F32)],
    )
    depthwise_grad = depthwise_grad[:KERNEL]
    conv_in_grad, gain_three, grad_two, attn_out_grad, attended_grad = plain_call(
        glu_back_kernel,
        [(width, 2 * width), (1, width), (rows, width), (width, width), (rows, width)],
        [
            glu_grad.reshape(rows, width), glu_in, section_two, gain_rows[2], conv_in, grad_three,
            attended, attn_out,
        ],
        flops=5_000_000_000,
    )
    conv_out_grad, conv_in_grad, attn_out_grad = lax.psum(
        (conv_out_grad, conv_in_grad, attn_out_grad), ("batch", "seq")
    )
    query_grad, key_grad, value_grad = attention_back_block(
        queries, attended_grad, attended, keys, values, log_total, extra
    )
    key_value_grad = jnp.concatenate([key_grad, value_grad], axis=-1)
    key_value_grad = near_sum(
        [key_value_grad[i * rows : (i + 1) * rows] for i in range(step)], step
    )
    qkv_grad, gain_two, grad_one = plain_call(
        project_back_kernel, [(width, 3 * width), (1, width), (rows, width)],
        [query_grad, key_value_grad, section_one, gain_rows[1], attn_qkv, cosine, sine, grad_two],
        flops=5_000_000_000,
    )
    qkv_grad = lax.psum(
        after_of(qkv_grad, (conv_out_grad, conv_in_grad, attn_out_grad)), ("batch", "seq")
    )
    gain_two, gain_three = gain_two[0], gain_three[0]

    grad_one = frame_exchange(grad_one.reshape(block_shape)).reshape(-1, width)
    grad_rows = dispatch(slots_one, grad_one, capacity, groups)
    branch_grad_one, hidden_one_grad, router_one = expert_back(
        0.5 * grad_rows, hidden_one, prob_one, chosen, gate_one, pre_one, branch_one,
        routers[0], expert_in[0], expert_out[0], groups,
    )
    gain_one = first_copy * jnp.sum(hidden_one_grad * unit_one, axis=0)
    extra = norm_back(hidden_one_grad, norm_gains[0], unit_one, inverse_one)
    frames_grad = grad_one + give_back(slots_one, extra, capacity, groups)
    inward_one, outward_one = weight_grads(
        hidden_one_all, batch_gather(branch_grad_one), expert_in[0], expert_out[0]
    )
    gains_grad = jnp.stack([gain_one, gain_two, gain_three, gain_four, gain_five])
    routers_grad = first_copy * jnp.stack([router_one, router_two])
    gains_grad, routers_grad, depthwise_grad = lax.psum(
        after_of((gains_grad, routers_grad, depthwise_grad), qkv_grad), ("batch", "seq")
    )
    new_mean = (1.0 - MOMENTUM) * running_mean + MOMENTUM * averaged
    new_var = (1.0 - MOMENTUM) * running_var + MOMENTUM * variance * frame_count / (
        frame_count - 1.0
    )
    return (
        layer_out.reshape(frames.shape), frames_grad.reshape(frames.shape), gains_grad, routers_grad,
        jnp.stack([inward_one, inward_two]), jnp.stack([outward_one, outward_two]),
        qkv_grad, attn_out_grad, conv_in_grad, depthwise_grad, bn_gain_grad, bn_bias_grad,
        conv_out_grad, new_mean, new_var,
    )


def solution(mesh):
    frame_spec = P("batch", "seq", None)
    in_specs = (
        frame_spec, frame_spec, P("batch"), frame_spec, P(), P(),
        P(None, None, "seq"), P(None, "seq", None),
    ) + (P(),) * 9
    out_specs = (
        frame_spec, frame_spec, P(), P(), P(None, None, "seq"), P(None, "seq", None),
    ) + (P(),) * 9
    return jax.shard_map(
        per_device, mesh=mesh, in_specs=in_specs, out_specs=out_specs, check_vma=False
    )
```

```python
import functools
import math

import jax
import jax.numpy as jnp
from jax import lax
from jax.experimental import pallas as pl
from jax.experimental.pallas import tpu as pltpu
from jax.sharding import PartitionSpec as P

HEADS = 8
EXPERTS = 8
KERNEL = 15
HEAD = 64
EPSILON = 1e-05
MOMENTUM = 0.1
NEGATIVE_FILL = -1e30
HIGH = lax.Precision.HIGH
MESH = pl.DeviceIdType.MESH
F32 = jnp.float32
BF16 = jnp.bfloat16
LANES = 128
SCORE_SCALE = HEAD ** (-0.5) / math.log(2.0)
VMEM_BYTES = 52 * 1024 * 1024
PLAIN_BYTES = 36 * 1024 * 1024


def mm(left_side, right_side):
    return jnp.dot(left_side, right_side, precision=HIGH, preferred_element_type=jnp.float32)


def mm_tn(left_side, right_side):
    return lax.dot_general(
        left_side, right_side, (((0,), (0,)), ((), ())), precision=HIGH,
        preferred_element_type=jnp.float32,
    )


def mm_nt(left_side, right_side):
    return lax.dot_general(
        left_side, right_side, (((1,), (1,)), ((), ())), precision=HIGH,
        preferred_element_type=jnp.float32,
    )


def einsum_high(pattern, left_side, right_side):
    return jnp.einsum(
        pattern, left_side, right_side, precision=HIGH, preferred_element_type=jnp.float32
    )


def norm_stats(values):
    centered = values - jnp.mean(values, axis=-1, keepdims=True)
    inverse = lax.rsqrt(jnp.mean(centered * centered, axis=-1, keepdims=True) + EPSILON)
    return centered * inverse, inverse


def norm_back(grad, gain_row, unit, inverse):
    scaled = grad * gain_row
    return inverse * (
        scaled
        - jnp.mean(scaled, axis=-1, keepdims=True)
        - unit * jnp.mean(scaled * unit, axis=-1, keepdims=True)
    )


def swish(values):
    return values * jax.nn.sigmoid(values)


def swish_slope(values):
    gate = jax.nn.sigmoid(values)
    return gate * (1.0 + values * (1.0 - gate))


def remote(src, dst, send, recv, peer):
    return pltpu.make_async_remote_copy(
        src_ref=src, dst_ref=dst, send_sem=send, recv_sem=recv, device_id=peer, device_id_type=MESH
    )


def greet(peers):
    barrier = pltpu.get_barrier_semaphore()
    for peer in peers:
        pl.semaphore_signal(barrier, inc=1, device_id=peer, device_id_type=MESH)
    pl.semaphore_wait(barrier, len(peers))


class Ring:
    def __init__(self, src, dst, members, step, send, recv, local):
        b, s = lax.axis_index("batch"), lax.axis_index("seq")
        me, low = s // step, lax.rem(s, step)
        others = [lax.rem(me + off, members) for off in range(1, members)]
        self.peers = [(b, other * step + low) for other in others]
        self.own = pltpu.make_async_copy(src.at[me], dst.at[me], local)
        self.sends = [
            remote(src.at[other], dst.at[me], send.at[i], recv.at[me], self.peers[i])
            for i, other in enumerate(others)
        ]
        self.receives = [
            remote(src.at[other], dst.at[other], send.at[i], recv.at[other], self.peers[i])
            for i, other in enumerate(others)
        ]

    def start(self):
        for send in self.sends:
            send.start()
        self.own.start()

    def wait_receives(self):
        self.own.wait()
        for receive in self.receives:
            receive.wait_recv()

    def wait_sends(self):
        for send in self.sends:
            send.wait_send()


def ring_semaphores(members):
    dma = pltpu.SemaphoreType.DMA
    return [dma((members,)), dma((members,)), dma]


def square_mesh():
    return (lax.axis_size("batch"), lax.axis_size("seq")) == (4, 8)


class Spread:
    def __init__(self, src, dst, send, recv, local=None):
        b, s = lax.axis_index("batch"), lax.axis_index("seq")
        count = lax.axis_size("batch")
        self.square = square_mesh()
        if self.square:
            x, y = lax.rem(b, 2), b // 2
            across_x, across_y = (b + 1 - 2 * x, s), (b + 2 - 4 * y, s)
            half = src.shape[0] // 2
            low, high = pl.ds(0, half), pl.ds(half, half)
            self.peers = [across_x, across_y]
            plan = [
                (src.at[low], 1, low, across_x), (src.at[high], 2, high, across_y),
                (src.at[high], 1, high, across_x), (src.at[low], 2, low, across_y),
                (dst.at[1, low], 3, low, across_y), (dst.at[2, high], 3, high, across_x),
            ]
            self.copies = [
                remote(rows, dst.at[piece, part], send.at[i], recv.at[i], peer)
                for i, (rows, piece, part, peer) in enumerate(plan)
            ]
            self.needs = {1: (2,), 2: (3,), 3: (4, 5)}
            self.first = 4
        else:
            self.peers = [(lax.rem(b + k, count), s) for k in range(1, count)]
            self.copies = [
                remote(src, dst.at[k], send.at[k - 1], recv.at[k - 1], self.peers[k - 1])
                for k in range(1, count)
            ]
            self.needs = {k: (k - 1,) for k in range(1, count)}
            self.first = count - 1
        self.own = None if local is None else pltpu.make_async_copy(src, dst.at[0], local)

    @staticmethod
    def semaphores():
        count = 6 if square_mesh() else max(lax.axis_size("batch") - 1, 1)
        return [pltpu.SemaphoreType.DMA((count,)), pltpu.SemaphoreType.DMA((count,))]

    def start(self):
        for copy in self.copies[: self.first]:
            copy.start()
        if self.own is not None:
            self.own.start()

    def forward(self):
        if self.square:
            for i in range(2):
                self.copies[i].wait_recv()
                self.copies[4 + i].start()

    def wait_receive(self, piece):
        for i in self.needs[piece]:
            self.copies[i].wait_recv()

    def wait_receives(self):
        for piece in self.needs:
            self.wait_receive(piece)
        if self.own is not None:
            self.own.wait()

    def wait_sends(self):
        for copy in self.copies:
            copy.wait_send()


def near_pairs(step, shift):
    count = lax.axis_size("seq")
    return [(i, i // step * step + (i % step + shift) % step) for i in range(count)]


def near_gather(rows, step):
    return [rows] + [
        lax.ppermute(rows, "seq", near_pairs(step, step - shift)) for shift in range(1, step)
    ]


def near_back(pieces, step):
    return [pieces[0]] + [
        lax.ppermute(pieces[shift], "seq", near_pairs(step, shift)) for shift in range(1, step)
    ]


def slot_matrix(routes, live_flat, capacity):
    experts = jnp.arange(EXPERTS, dtype=jnp.int32)
    match = (routes[:, None] == experts[None, :]) & live_flat[:, None]
    rank = jnp.cumsum(match.astype(jnp.int32), axis=0) - 1
    rank = jnp.sum(jnp.where(match, rank, 0), axis=-1)
    kept = live_flat & (rank < capacity)
    slot = jnp.where(kept, routes * capacity + rank, -1)
    slots = jnp.arange(EXPERTS * capacity, dtype=jnp.int32)
    return kept, (slots[:, None] == slot[None, :]).astype(jnp.bfloat16)


def split_two(values):
    high = lax.reduce_precision(values, exponent_bits=8, mantissa_bits=7)
    return high.astype(jnp.bfloat16), (values - high).astype(jnp.bfloat16)


def pick(matrix, rows):
    width = rows.shape[-1]
    both = jnp.concatenate(split_two(rows), axis=-1)
    out = jnp.dot(matrix, both, preferred_element_type=jnp.float32)
    return out[:, :width] + out[:, width:]


def put(matrix, rows):
    width = rows.shape[-1]
    both = jnp.concatenate(split_two(rows), axis=-1)
    out = lax.dot_general(
        matrix, both, (((0,), (0,)), ((), ())), preferred_element_type=jnp.float32
    )
    return out[:, :width] + out[:, width:]


def slot_blocks(matrix, rows, capacity, groups):
    slots = pick(matrix, rows).reshape(EXPERTS, 1, capacity, -1)
    copies = jnp.broadcast_to(slots, (EXPERTS, groups, capacity, slots.shape[-1]))
    return copies.reshape(EXPERTS * groups, capacity, -1)


def fold_back(matrix, out, capacity, groups):
    out = out.reshape(EXPERTS, groups, capacity, -1)
    total = out[:, 0]
    for i in range(1, groups):
        total = total + out[:, i]
    return put(matrix, total.reshape(EXPERTS * capacity, -1))


def whole(shape):
    rank = len(shape)
    return pl.BlockSpec(shape, lambda *ids: (0,) * rank)


def plain_call(kernel, outs, args, scratch=(), flops=0):
    moved = sum(math.prod(a.shape) * 4 for a in args) + sum(math.prod(o) * 4 for o in outs)
    return pl.pallas_call(
        kernel,
        out_shape=[jax.ShapeDtypeStruct(o, F32) for o in outs],
        scratch_shapes=list(scratch),
        compiler_params=pltpu.CompilerParams(vmem_limit_bytes=PLAIN_BYTES),
        cost_estimate=pl.CostEstimate(flops=flops, bytes_accessed=moved, transcendentals=0),
    )(*args)


def halves(values):
    high = values.astype(BF16)
    return high, (values - high.astype(F32)).astype(BF16)


NN = (((1,), (0,)), ((), ()))
NT = (((1,), (1,)), ((), ()))
TN = (((0,), (0,)), ((), ()))


def dot3(left, right, dims=NN):
    left_high, left_low = left
    right_high, right_low = right
    return (
        lax.dot_general(left_high, right_high, dims, preferred_element_type=F32)
        + lax.dot_general(left_high, right_low, dims, preferred_element_type=F32)
        + lax.dot_general(left_low, right_high, dims, preferred_element_type=F32)
    )


def dot2(left, right, dims=NN):
    left_high, left_low = left
    return lax.dot_general(left_high, right, dims, preferred_element_type=F32) + lax.dot_general(
        left_low, right, dims, preferred_element_type=F32
    )


def rotated(values, cosine, sine, lane):
    ahead = pltpu.roll(values, LANES - HEAD // 2, 1)
    behind = pltpu.roll(values, HEAD // 2, 1)
    other = jnp.where(lane % HEAD < HEAD // 2, ahead, behind)
    return values * cosine + other * sine


def project_kernel(x_ref, gain_ref, weight_ref, cos_ref, sin_ref, q_ref, kv_ref):
    width = x_ref.shape[1]
    unit, _ = norm_stats(x_ref[...])
    hidden = halves(unit * gain_ref[...])
    lane = lax.broadcasted_iota(jnp.int32, (1, LANES), 1)
    cosine, sine = cos_ref[...], sin_ref[...]
    for part in range(3):
        out = dot3(hidden, halves(weight_ref[:, part * width : (part + 1) * width]))
        for first in range(0, width, LANES):
            piece = out[:, first : first + LANES]
            if part < 2:
                piece = rotated(piece, cosine, sine, lane)
            if part == 0:
                q_ref[:, first : first + LANES] = piece
            else:
                start = (part - 1) * width + first
                kv_ref[:, start : start + LANES] = piece


def one_head(values, head, lane):
    return jnp.where((lane < HEAD) == (head == 0), values, pltpu.roll(values, HEAD, 1))


def high_low(values):
    high = values.astype(BF16).astype(F32)
    return high, values - high


def query_side(values, extra, lane):
    high, low = high_low(values)
    return jnp.concatenate([high, jnp.where(lane < HEAD, low, extra)], axis=1).astype(BF16)


def key_side(values, extra, lane):
    high, low = high_low(values)
    first = jnp.where(lane < HEAD, high, low)
    return jnp.concatenate([first, jnp.where(lane < HEAD, high, extra)], axis=1).astype(BF16)


def both_parts(values, lane):
    high, low = high_low(values)
    return jnp.where(lane < HEAD, high, low).astype(BF16)


def in_parts(column, lane, first):
    high, rest = high_low(column)
    middle, low = high_low(rest)
    return jnp.where(
        lane == first,
        high,
        jnp.where(lane == first + 1, middle, jnp.where(lane == first + 2, low, 0.0)),
    )


def attention_kernel(
    members, near, q_ref, *refs,
):
    k_refs, v_refs, refs = refs[:near], refs[near : 2 * near], refs[2 * near :]
    (
        extra_ref, x_ref, out_weight_ref, gain_ref, in_weight_ref, live_ref, sent_ref, att_ref,
        lse_ref, x2_ref, glu_in_ref, glu_ref, landed_ref, att_all, *sems,
    ) = refs
    pair = pl.program_id(0)
    ring = Ring(sent_ref, landed_ref, members, 1, *sems)

    @pl.when(pair == 0)
    def _():
        greet(ring.peers)
        ring.start()

    rows = q_ref.shape[0]
    width = x_ref.shape[1]
    tile = min(256, rows)
    lane = lax.broadcasted_iota(jnp.int32, (1, LANES), 1)
    one_at = jnp.where(lane == HEAD, 1.0, 0.0).astype(F32)
    ones_column = jnp.where(lane == 0, 1.0, 0.0).astype(F32)
    keys = jnp.concatenate([k_ref[...] for k_ref in k_refs], axis=0)
    values = jnp.concatenate([v_ref[...] for v_ref in v_refs], axis=0)
    keys_count = keys.shape[0]
    outs = []
    for head in range(2):
        key_pack = key_side(one_head(keys, head, lane), extra_ref[...], lane)
        value_high, value_low = high_low(one_head(values, head, lane))
        value_pack = jnp.concatenate(
            [
                jnp.where(lane < HEAD, value_high, value_low),
                jnp.broadcast_to(ones_column, (keys_count, LANES)),
            ],
            axis=1,
        ).astype(BF16)
        per_tile = []
        for first in range(0, rows, tile):
            queries = one_head(q_ref[first : first + tile, :] * SCORE_SCALE, head, lane)
            query_pack = query_side(queries, one_at, lane)
            scores = lax.dot_general(query_pack, key_pack, NT, preferred_element_type=F32)
            top = jnp.max(scores, axis=1, keepdims=True)
            weights = halves(jnp.exp2(scores - top))
            summed = dot2(weights, value_pack)
            total = summed[:, LANES : LANES + 1]
            mixed = summed[:, :LANES]
            mixed = (mixed + pltpu.roll(mixed, HEAD, 1)) / total
            log_total = jnp.broadcast_to(top + jnp.log2(total), mixed.shape)
            per_tile.append((mixed, log_total))
        outs.append(per_tile)
    for index, first in enumerate(range(0, rows, tile)):
        (mixed_a, log_a), (mixed_b, log_b) = outs[0][index], outs[1][index]
        mixed = jnp.where(lane < HEAD, mixed_a, mixed_b)
        att_ref[first : first + tile, :] = mixed
        lse_ref[first : first + tile, :] = jnp.where(lane < HEAD, log_a, log_b)
        att_all[pair, first : first + tile, :] = mixed

    @pl.when(pair == pl.num_programs(0) - 1)
    def _():
        pairs = att_all.shape[0]
        attended = jnp.concatenate([att_all[i] for i in range(pairs)], axis=1)
        x2 = x_ref[...] + dot3(halves(attended), halves(out_weight_ref[...]))
        x2_ref[...] = x2
        unit, _ = norm_stats(x2)
        hidden = halves(unit * gain_ref[...])
        left = dot3(hidden, halves(in_weight_ref[:, :width]))
        right = dot3(hidden, halves(in_weight_ref[:, width:]))
        glu_in_ref[:, :width] = left
        glu_in_ref[:, width:] = right
        glu_ref[...] = left * jax.nn.sigmoid(right) * live_ref[...]
        ring.wait_receives()
        ring.wait_sends()


def attention_block(
    queries, key_values, extra, x1, out_weight, gain_row, in_weight, live, sent, collective_id
):
    rows, width = queries.shape
    near = len(key_values)
    pairs = width // LANES
    lanes_of = lambda height: pl.BlockSpec((height, LANES), lambda i: (0, i))
    values_of = pl.BlockSpec((rows, LANES), lambda i: (0, i + pairs))
    members = sent.shape[0]
    hbm = pl.BlockSpec(memory_space=pl.ANY)
    return pl.pallas_call(
        functools.partial(attention_kernel, members, near),
        grid=(pairs,),
        in_specs=[
            *[lanes_of(rows)] * (1 + near), *[values_of] * near, whole(extra.shape), whole(x1.shape),
            whole(out_weight.shape), whole(gain_row.shape), whole(in_weight.shape), whole(live.shape),
            hbm,
        ],
        out_specs=[
            lanes_of(rows), lanes_of(rows), whole((rows, width)), whole((rows, 2 * width)),
            whole((rows, width)), hbm,
        ],
        out_shape=[
            jax.ShapeDtypeStruct((rows, w), F32) for w in (width, width, width, 2 * width, width)
        ] + [jax.ShapeDtypeStruct(sent.shape, F32)],
        scratch_shapes=[pltpu.VMEM((pairs, rows, LANES), F32)] + ring_semaphores(members),
        compiler_params=pltpu.CompilerParams(
            collective_id=collective_id, has_side_effects=True, vmem_limit_bytes=VMEM_BYTES
        ),
        cost_estimate=pl.CostEstimate(
            flops=20_000_000_000, bytes_accessed=20_000_000, transcendentals=0
        ),
    )(
        queries, *key_values, *key_values, extra, x1, out_weight, gain_row, in_weight, live, sent
    )


def attention_back_kernel(
    members, near, q_ref, grad_ref, att_ref, lse_ref, *refs,
):
    k_refs, v_refs, refs = refs[:near], refs[near : 2 * near], refs[2 * near :]
    extra_ref, sent_ref, dqt_ref = refs[:3]
    dk_refs, dv_refs, refs = refs[3 : 3 + near], refs[3 + near : 3 + 2 * near], refs[3 + 2 * near :]
    landed_ref, packs, *sems = refs
    ring = Ring(sent_ref, landed_ref, members, 1, *sems)

    @pl.when(pl.program_id(0) == 0)
    def _():
        greet(ring.peers)
        ring.start()

    rows = q_ref.shape[0]
    count = k_refs[0].shape[0]
    tile = 256
    lane = lax.broadcasted_iota(jnp.int32, (1, LANES), 1)
    one_at = jnp.where(lane == HEAD, 1.0, 0.0).astype(F32)
    product = grad_ref[...] * att_ref[...]
    for head in range(2):
        mine = (lane < HEAD) == (head == 0)
        out_dot = jnp.sum(jnp.where(mine, product, 0.0), axis=1, keepdims=True)
        log_total = one_head(lse_ref[...], head, lane)
        queries = one_head(q_ref[...] * SCORE_SCALE, head, lane)
        grads = one_head(grad_ref[...], head, lane)
        query_pack = query_side(queries, one_at + in_parts(-log_total, lane, HEAD + 1), lane)
        dots = jnp.broadcast_to(-out_dot, grads.shape)
        grad_pack = query_side(grads, in_parts(dots, lane, HEAD + 1), lane)
        query_both = both_parts(queries, lane)
        grad_both = both_parts(grads, lane)
        packs[...] = jnp.zeros_like(packs)

        def step(part, index, carry):
            k_ref, v_ref, dk_ref, dv_ref = k_refs[part], v_refs[part], dk_refs[part], dv_refs[part]
            first = pl.multiple_of(index * tile, tile)
            extra = extra_ref[pl.ds(pl.multiple_of(part * count + first, tile), tile), :]
            keys = one_head(k_ref[pl.ds(first, tile), :], head, lane)
            values = one_head(v_ref[pl.ds(first, tile), :], head, lane)
            scores = lax.dot_general(
                key_side(keys, extra, lane), query_pack, NT, preferred_element_type=F32
            )
            prob = jnp.exp2(scores)
            score_grad = prob * lax.dot_general(
                key_side(values, extra, lane), grad_pack, NT, preferred_element_type=F32
            )
            value_grad = dot2(halves(prob), grad_both)
            parts = halves(score_grad)
            key_grad = dot2(parts, query_both) * math.log(2.0)
            value_grad = value_grad + pltpu.roll(value_grad, HEAD, 1)
            key_grad = key_grad + pltpu.roll(key_grad, HEAD, 1)
            if head == 0:
                dv_ref[pl.ds(first, tile), :] = value_grad
                dk_ref[pl.ds(first, tile), :] = key_grad
            else:
                dv_ref[pl.ds(first, tile), :] = jnp.where(
                    mine, value_grad, dv_ref[pl.ds(first, tile), :]
                )
                dk_ref[pl.ds(first, tile), :] = jnp.where(
                    mine, key_grad, dk_ref[pl.ds(first, tile), :]
                )
            key_both = both_parts(keys, lane)
            packs[...] += lax.dot_general(
                key_both, parts[0], TN, preferred_element_type=F32
            ) + lax.dot_general(key_both, parts[1], TN, preferred_element_type=F32)
            return carry

        for part in range(near):
            lax.fori_loop(0, count // tile, functools.partial(step, part), 0)
        dqt_ref[head * HEAD : (head + 1) * HEAD, :] = (
            packs[:HEAD, :] + packs[HEAD:, :]
        ) * HEAD ** (-0.5)

    @pl.when(pl.program_id(0) == pl.num_programs(0) - 1)
    def _():
        ring.wait_receives()
        ring.wait_sends()


def attention_back_block(
    queries, grad, attended, key_values, lse, extra, sent, collective_id
):
    rows, width = queries.shape
    near = len(key_values)
    pairs = width // LANES
    lanes_of = lambda height: pl.BlockSpec((height, LANES), lambda i: (0, i))
    values_of = pl.BlockSpec((rows, LANES), lambda i: (0, i + pairs))
    members = sent.shape[0]
    hbm = pl.BlockSpec(memory_space=pl.ANY)
    out = pl.pallas_call(
        functools.partial(attention_back_kernel, members, near),
        grid=(pairs,),
        in_specs=[
            *[lanes_of(rows)] * (4 + near), *[values_of] * near, whole(extra.shape), hbm,
        ],
        out_specs=[
            pl.BlockSpec((LANES, rows), lambda i: (i, 0)), *[lanes_of(rows)] * (2 * near), hbm,
        ],
        out_shape=[jax.ShapeDtypeStruct((width, rows), F32)]
        + [jax.ShapeDtypeStruct((rows, width), F32)] * (2 * near)
        + [jax.ShapeDtypeStruct(sent.shape, F32)],
        scratch_shapes=[pltpu.VMEM((LANES, rows), F32)] + ring_semaphores(members),
        compiler_params=pltpu.CompilerParams(
            collective_id=collective_id, has_side_effects=True, vmem_limit_bytes=VMEM_BYTES
        ),
        cost_estimate=pl.CostEstimate(
            flops=40_000_000_000, bytes_accessed=20_000_000, transcendentals=0
        ),
    )(queries, grad, attended, lse, *key_values, *key_values, extra, sent)
    return out[0], out[1 : 1 + near], out[1 + near : 1 + 2 * near], out[-1]


def project_back_kernel(near, dqt_ref, *refs):
    dk_refs, dv_refs, refs = refs[:near], refs[near : 2 * near], refs[2 * near :]
    (
        x_ref, gain_ref, weight_ref, cos_ref, sin_ref, upper_ref, dw_ref, gain_grad_ref, dx_ref,
    ) = refs
    width = x_ref.shape[1]
    unit, inverse = norm_stats(x_ref[...])
    gain_row = gain_ref[...]
    hidden = halves(unit * gain_row)
    lane = lax.broadcasted_iota(jnp.int32, (1, LANES), 1)
    cosine, sine = cos_ref[...], -sin_ref[...]
    hidden_grad = jnp.zeros(x_ref.shape, F32)
    for part in range(3):
        if part == 0:
            grad = dqt_ref[...].T
        else:
            pieces = dk_refs if part == 1 else dv_refs
            grad = pieces[0][...]
            for piece in pieces[1:]:
                grad = grad + piece[...]
        if part < 2:
            grad = jnp.concatenate(
                [
                    rotated(grad[:, i : i + LANES], cosine, sine, lane)
                    for i in range(0, width, LANES)
                ],
                axis=1,
            )
        grad = halves(grad)
        dw_ref[:, part * width : (part + 1) * width] = dot3(hidden, grad, TN)
        hidden_grad += dot3(grad, halves(weight_ref[:, part * width : (part + 1) * width]), NT)
    gain_grad_ref[...] = jnp.sum(hidden_grad * unit, axis=0, keepdims=True)
    dx_ref[...] = upper_ref[...] + norm_back(hidden_grad, gain_row, unit, inverse)


RIM = 8


def glu_back_kernel(
    dglu_ref, glu_in_ref, x2_ref, gain_ref, in_weight_ref, grad_ref, att_ref, out_weight_ref,
    dw_in_ref, gain_grad_ref, dx2_ref, dw_out_ref, datt_ref,
):
    width = x2_ref.shape[1]
    unit, inverse = norm_stats(x2_ref[...])
    gain_row = gain_ref[...]
    hidden = halves(unit * gain_row)
    dglu = dglu_ref[...]
    left, gate = glu_in_ref[:, :width], jax.nn.sigmoid(glu_in_ref[:, width:])
    left_grad = halves(dglu * gate)
    right_grad = halves(dglu * left * gate * (1.0 - gate))
    dw_in_ref[:, :width] = dot3(hidden, left_grad, TN)
    dw_in_ref[:, width:] = dot3(hidden, right_grad, TN)
    hidden_grad = dot3(left_grad, halves(in_weight_ref[:, :width]), NT) + dot3(
        right_grad, halves(in_weight_ref[:, width:]), NT
    )
    gain_grad_ref[...] = jnp.sum(hidden_grad * unit, axis=0, keepdims=True)
    dx2 = grad_ref[...] + norm_back(hidden_grad, gain_row, unit, inverse)
    dx2_ref[...] = dx2
    dx2 = halves(dx2)
    dw_out_ref[...] = dot3(halves(att_ref[...]), dx2, TN)
    datt_ref[...] = dot3(dx2, halves(out_weight_ref[...]), NT)


def side_by_side(values):
    high, low = halves(values)
    return jnp.concatenate([high, high, low], axis=1)


def one_below_other(values):
    high, low = halves(values)
    return jnp.concatenate([high, low, high], axis=0)


def product(left, right):
    return lax.dot_general(left, right, NN, preferred_element_type=F32)


class ExpertGrads:
    def __init__(self, inward_ref, outward_ref, ids, refs):
        self.inward_ref, self.outward_ref, self.ids = inward_ref, outward_ref, ids
        (
            self.w1t3, self.w23, self.ht3, self.gt3, self.h3, self.g3, self.dw1t, self.dw2,
            self.stage_one, self.stage_two, self.sems,
        ) = refs
        self.chunk = self.stage_one.shape[-1]
        self.count = len(ids)

    @staticmethod
    def scratch(width, chunk, count, rows):
        hidden = chunk * count
        return [
            pltpu.VMEM((hidden, 3 * width), BF16), pltpu.VMEM((hidden, 3 * width), BF16),
            pltpu.VMEM((3 * width, rows), BF16), pltpu.VMEM((3 * width, rows), BF16),
            pltpu.VMEM((3 * rows, width), BF16), pltpu.VMEM((3 * rows, width), BF16),
            pltpu.VMEM((hidden, width), F32), pltpu.VMEM((hidden, width), F32),
            pltpu.VMEM((2, width, chunk), F32), pltpu.VMEM((2, chunk, width), F32),
            pltpu.SemaphoreType.DMA((5,)),
        ]

    def load(self, index):
        first = self.ids[index] * self.chunk
        part, slot = pl.ds(pl.multiple_of(first, self.chunk), self.chunk), index % 2
        return [
            pltpu.make_async_copy(
                self.inward_ref.at[:, part], self.stage_one.at[slot], self.sems.at[2 * slot]
            ),
            pltpu.make_async_copy(
                self.outward_ref.at[part, :], self.stage_two.at[slot], self.sems.at[2 * slot + 1]
            ),
        ]

    def start_weights(self):
        for copy in self.load(0):
            copy.start()

    def finish_weights(self):
        for index in range(self.count):
            if index + 1 < self.count:
                for copy in self.load(index + 1):
                    copy.start()
            for copy in self.load(index):
                copy.wait()
            part, slot = pl.ds(index * self.chunk, self.chunk), index % 2
            self.w1t3[part, :] = side_by_side(self.stage_one[slot].T)
            self.w23[part, :] = side_by_side(self.stage_two[slot])

    def block(self, hidden, out_grad, first, hidden_grad=None, middle=None):
        width = hidden.shape[1]
        self.ht3[...] = one_below_other(hidden.T)
        self.gt3[...] = one_below_other(out_grad.T)
        self.h3[...] = one_below_other(hidden)
        self.g3[...] = one_below_other(out_grad)
        if hidden_grad is not None:
            hidden_grad[...] = jnp.zeros_like(hidden_grad)

        def step(index, carry):
            part = pl.ds(pl.multiple_of(index * self.chunk, self.chunk), self.chunk)
            weights = self.w1t3[part, :]
            pre = product(weights, self.ht3[...])
            gates = jax.nn.sigmoid(pre)
            two = product(side_by_side(pre * gates), self.g3[...])
            slope = gates * (1.0 + pre * (1.0 - gates))
            pre_grad = product(self.w23[part, :], self.gt3[...]) * slope
            one = product(side_by_side(pre_grad), self.h3[...])
            if first:
                self.dw2[part, :] = two
                self.dw1t[part, :] = one
            else:
                self.dw2[part, :] += two
                self.dw1t[part, :] += one
            if hidden_grad is not None:
                hidden_grad[...] += dot3(
                    halves(pre_grad), (weights[:, :width], weights[:, 2 * width :]), TN
                )
            return carry

        half = self.count // 2 if middle is not None else 0
        if middle is not None:
            lax.fori_loop(0, half, step, 0)
            middle()
        lax.fori_loop(half, self.count, step, 0)

    def store(self, dw1_of, dw2_of):
        pending = [[], []]
        for index in range(self.count):
            slot = index % 2
            for copy in pending[slot]:
                copy.wait()
            part = pl.ds(index * self.chunk, self.chunk)
            self.stage_one[slot] = self.dw1t[part, :].T
            pending[slot] = [
                pltpu.make_async_copy(
                    self.stage_one.at[slot], dw1_of(index), self.sems.at[2 * slot]
                ),
                pltpu.make_async_copy(
                    self.dw2.at[part, :], dw2_of(index), self.sems.at[2 * slot + 1]
                ),
            ]
            for copy in pending[slot]:
                copy.start()
        for copy in pending[0] + pending[1]:
            copy.wait()


class SmallSum:
    def __init__(self, rows, columns, refs):
        self.rows, self.columns = rows, columns
        self.row_buf, self.col_buf, *self.sems = refs
        b, s = lax.axis_index("batch"), lax.axis_index("seq")
        self.place = (b, s)
        self.row_peers = [(lax.rem(b + off, rows), s) for off in range(1, rows)]
        self.col_peers = [(b, lax.rem(s + off, columns)) for off in range(1, columns)]

    @staticmethod
    def scratch(rows, columns, shape):
        dma = pltpu.SemaphoreType.DMA
        return [
            pltpu.VMEM((rows,) + shape, F32), pltpu.VMEM((columns,) + shape, F32),
            dma((rows,)), dma((rows,)), dma((columns,)), dma((columns,)),
        ]

    def share(self, value, axis):
        buf, peers = (self.row_buf, self.row_peers) if axis == 0 else (self.col_buf, self.col_peers)
        send, recv = self.sems[2 * axis : 2 * axis + 2]
        mine = self.place[axis]
        buf[mine] = value
        self.copies = [
            remote(buf.at[mine], buf.at[mine], send.at[i], recv.at[mine], peer)
            for i, peer in enumerate(peers)
        ]
        for copy in self.copies:
            copy.start()

    def total(self, axis):
        buf, peers = (self.row_buf, self.row_peers) if axis == 0 else (self.col_buf, self.col_peers)
        send, recv = self.sems[2 * axis : 2 * axis + 2]
        for i, peer in enumerate(peers):
            other = peer[axis]
            remote(buf.at[other], buf.at[other], send.at[i], recv.at[other], peer).wait_recv()
        for copy in self.copies:
            copy.wait_send()
        total = buf[0]
        for i in range(1, buf.shape[0]):
            total = total + buf[i]
        return total


class Rims:
    def __init__(self, blocks_ref, step, refs):
        self.from_before, self.from_after, send, recv = refs
        b, s = lax.axis_index("batch"), lax.axis_index("seq")
        self.low, self.step = lax.rem(s, step), step
        base, rows = s - self.low, blocks_ref.shape[1]
        after = (b, base + lax.rem(self.low + 1, step))
        before = (b, base + lax.rem(self.low + step - 1, step))
        self.copies = [
            remote(
                blocks_ref.at[:, pl.ds(rows - RIM, RIM), :], self.from_before, send.at[0],
                recv.at[0], after,
            ),
            remote(
                blocks_ref.at[:, pl.ds(0, RIM), :], self.from_after, send.at[1], recv.at[1], before
            ),
        ]

    @staticmethod
    def scratch(parts, width):
        dma = pltpu.SemaphoreType.DMA
        return [
            pltpu.VMEM((parts, RIM, width), F32), pltpu.VMEM((parts, RIM, width), F32), dma((2,)),
            dma((2,)),
        ]

    def start(self):
        for copy in self.copies:
            copy.start()

    def finish(self):
        for copy in self.copies:
            copy.wait()
        before, after = self.from_before[...], self.from_after[...]
        none = jnp.zeros_like(before[:1])
        first, last = cast_one(self.low == 0), cast_one(self.low == self.step - 1)
        before_edge = jnp.concatenate([none, before[:-1]], axis=0)
        after_edge = jnp.concatenate([after[1:], none], axis=0)
        return (
            first * before_edge + (1.0 - first) * before,
            last * after_edge + (1.0 - last) * after,
        )


def cast_one(flag):
    return jnp.where(flag, 1.0, 0.0).astype(F32)


def pad_blocks(pad_ref, before, block_ref, after):
    rows = block_ref.shape[1]
    pad_ref[:, :RIM, :] = before
    pad_ref[:, RIM : RIM + rows, :] = block_ref[...]
    pad_ref[:, RIM + rows :, :] = after


def conv_stats(sums):
    count = sums[2:3]
    averaged = sums[0:1] / count
    return count, averaged, sums[1:2] / count - averaged * averaged


def conv_chain_kernel(
    step, row_count, columns, glu_ref, taps_ref, live_ref, gain_ref, bias_ref, weight_ref, x2_ref,
    sent_ref, conv_ref, sums_ref, x3_ref, before_ref, after_ref, landed_ref, pad_ref, mine, *refs,
):
    parts, rows, width = glu_ref.shape
    rims = Rims(glu_ref, step, refs[:4])
    small = SmallSum(row_count, columns, refs[4:10])
    ring = Ring(sent_ref, landed_ref, columns, 1, *refs[10:])
    greet(small.row_peers + small.col_peers)
    rims.start()
    ring.start()
    before, after = rims.finish()
    before_ref[...] = before
    after_ref[...] = after
    pad_blocks(pad_ref, before, glu_ref, after)
    mine[...] = jnp.zeros_like(mine)

    def part_step(part, carry):
        alive = live_ref[part]
        for first in range(0, width, LANES):
            columns_here = slice(first, first + LANES)
            total = jnp.zeros((rows, LANES), F32)
            for tap in range(KERNEL):
                total = total + pad_ref[part, 1 + tap : 1 + tap + rows, columns_here] * taps_ref[
                    tap : tap + 1, columns_here
                ]
            conv_ref[part, :, columns_here] = total
            kept = alive * total
            mine[0:1, columns_here] += jnp.sum(kept, axis=0, keepdims=True)
            mine[1:2, columns_here] += jnp.sum(kept * total, axis=0, keepdims=True)
            mine[2:3, columns_here] += jnp.sum(
                jnp.broadcast_to(alive, (rows, LANES)), axis=0, keepdims=True
            )
        return carry

    lax.fori_loop(0, parts, part_step, 0)
    small.share(mine[...], 0)
    small.share(small.total(0), 1)
    weight = halves(weight_ref[...])
    sums = small.total(1)
    sums_ref[...] = sums
    count, averaged, variance = conv_stats(sums)
    scale = lax.rsqrt(variance + EPSILON)
    conv = conv_ref[...].reshape(parts * rows, width)
    normed = (conv - averaged) * scale * gain_ref[...] + bias_ref[...]
    x3_ref[...] = x2_ref[...] + dot3(halves(swish(normed)), weight)
    ring.wait_receives()
    ring.wait_sends()


def conv_chain_back_kernel(
    step, row_count, columns, grad_ref, conv_ref, sums_ref, gain_ref, bias_ref, weight_ref,
    taps_ref, live_ref, glu_ref, glu_before_ref, glu_after_ref, dw_ref, out_sums_ref,
    taps_grad_ref, dglu_ref, pad_ref, glu_pad_ref, tap_sums, conv_grad, mine, *refs,
):
    parts, rows, width = glu_ref.shape
    rims = Rims(conv_grad, step, refs[:4])
    small = SmallSum(row_count, columns, refs[4:])
    greet(small.row_peers + small.col_peers)
    count, averaged, variance = conv_stats(sums_ref[...])
    scale = lax.rsqrt(variance + EPSILON)
    conv = conv_ref[...].reshape(parts * rows, width)
    unit = (conv - averaged) * scale
    gain_row = gain_ref[...]
    normed = unit * gain_row + bias_ref[...]
    grad = halves(grad_ref[...])
    normed_grad = dot3(grad, halves(weight_ref[...]), NT) * swish_slope(normed)
    mine[...] = jnp.zeros_like(mine)
    mine[0:1, :] = jnp.sum(normed_grad * unit, axis=0, keepdims=True)
    mine[1:2, :] = jnp.sum(normed_grad, axis=0, keepdims=True)
    small.share(mine[...], 0)
    dw_ref[...] = dot3(halves(swish(normed)), grad, TN)
    small.share(small.total(0), 1)
    pad_blocks(glu_pad_ref, glu_before_ref[...], glu_ref, glu_after_ref[...])
    tap_sums[...] = jnp.zeros_like(tap_sums)
    sums = small.total(1)
    out_sums_ref[...] = sums
    mean_grad = -scale * gain_row * sums[1:2]
    var_grad = -0.5 * scale * scale * gain_row * sums[0:1]
    fixed = (mean_grad - 2.0 * averaged * var_grad) / count
    slope = 2.0 * var_grad / count
    direct = (scale * gain_row * normed_grad).reshape(parts, rows, width)
    conv_grad[...] = direct + live_ref[...] * (
        fixed.reshape(1, 1, width) + conv_ref[...] * slope.reshape(1, 1, width)
    )
    rims.start()
    before, after = rims.finish()
    pad_blocks(pad_ref, before, conv_grad, after)

    def part_step(part, carry):
        alive = live_ref[part]
        for first in range(0, width, LANES):
            columns_here = slice(first, first + LANES)
            total = jnp.zeros((rows, LANES), F32)
            here = conv_grad[part, :, columns_here]
            for tap in range(KERNEL):
                start = KERNEL - tap
                total = total + pad_ref[part, start : start + rows, columns_here] * taps_ref[
                    tap : tap + 1, columns_here
                ]
                product_here = glu_pad_ref[part, 1 + tap : 1 + tap + rows, columns_here] * here
                tap_sums[tap, :, columns_here] += jnp.sum(
                    product_here.reshape(rows // 8, 8, LANES), axis=0
                )
            dglu_ref[part, :, columns_here] = total * alive
        return carry

    lax.fori_loop(0, parts, part_step, 0)
    for tap in range(KERNEL):
        taps_grad_ref[tap : tap + 1, :] = jnp.sum(tap_sums[tap], axis=0, keepdims=True)


def conv_chain(back, step, outs, args, extra_scratch, collective_id, ring=False):
    row_count, columns = lax.axis_size("batch"), lax.axis_size("seq")
    parts, rows, width = outs[0] if not back else outs[3]
    vmem, hbm = pl.BlockSpec(memory_space=pltpu.VMEM), pl.BlockSpec(memory_space=pl.ANY)
    padded = pltpu.VMEM((parts, rows + 2 * RIM, width), F32)
    scratch = [padded] * (2 if back else 1) + list(extra_scratch) + [pltpu.VMEM((8, width), F32)]
    scratch += Rims.scratch(parts, width) + SmallSum.scratch(row_count, columns, (8, width))
    if ring:
        scratch += ring_semaphores(columns)
    kernel = conv_chain_back_kernel if back else conv_chain_kernel
    hidden_last = [hbm] if ring else []
    return pl.pallas_call(
        functools.partial(kernel, step, row_count, columns),
        in_specs=[vmem] * (len(args) - len(hidden_last)) + hidden_last,
        out_specs=[vmem] * (len(outs) - len(hidden_last)) + hidden_last,
        out_shape=[jax.ShapeDtypeStruct(shape, F32) for shape in outs],
        scratch_shapes=scratch,
        compiler_params=pltpu.CompilerParams(
            collective_id=collective_id, has_side_effects=True, vmem_limit_bytes=PLAIN_BYTES
        ),
        cost_estimate=pl.CostEstimate(
            flops=2_000_000_000, bytes_accessed=30_000_000, transcendentals=0
        ),
    )(*args)


class Places:
    def __init__(self):
        b, s = lax.axis_index("batch"), lax.axis_index("seq")
        self.x, self.y, self.z, self.c = lax.rem(b, 2), b // 2, s // 2, lax.rem(s, 2)
        self.near = (b, s + 1 - 2 * self.c)
        self.across_x = (b + 1 - 2 * self.x, s)
        self.across_y = (b + 2 - 4 * self.y, s)
        self.line = [lax.rem(self.z + k, 4) for k in range(1, 4)]
        self.line_peers = [(b, other * 2 + self.c) for other in self.line]


def cut_of(width):
    cut = width // 256 * 128
    return pl.ds(0, cut), pl.ds(cut, width - cut)


class DenseScatter:
    def __init__(self, pieces, out_ref, refs):
        self.pieces, self.out_ref = pieces, out_ref
        self.buf0, self.buf1, self.buf2, self.acc0, self.acc1, self.send, self.recv, self.loads = refs

    @staticmethod
    def scratch(rows, width, pieces):
        block = lambda parts: pltpu.VMEM((rows // parts, width), F32)
        dma = pltpu.SemaphoreType.DMA
        return [
            block(2), block(4), block(8), block(2), block(4), dma((pieces + 4,)), dma((pieces + 4,)),
            dma((pieces,)),
        ]

    def start_cores(self):
        at = Places()
        half = self.buf0.shape[0]
        first = 0
        self.copies, self.local = [], []
        for i, piece in enumerate(self.pieces):
            columns = pl.ds(first, piece.shape[1])
            first += piece.shape[1]
            self.copies.append(
                remote(
                    piece.at[pl.ds((1 - at.c) * half, half), :], self.buf0.at[:, columns],
                    self.send.at[i], self.recv.at[i], at.near,
                )
            )
            self.local.append(
                pltpu.make_async_copy(
                    piece.at[pl.ds(at.c * half, half), :], self.acc0.at[:, columns],
                    self.loads.at[i],
                )
            )
        for copy in self.copies + self.local:
            copy.start()

    def start_first(self):
        for copy in self.copies + self.local:
            copy.wait()
        self.acc0[...] += self.buf0[...]
        at = Places()
        left, right = cut_of(self.acc0.shape[1])
        size, sem = self.buf1.shape[0], len(self.pieces)
        self.copies = [
            remote(
                self.acc0.at[pl.ds((1 - at.x) * size, size), left], self.buf1.at[:, left],
                self.send.at[sem], self.recv.at[sem], at.across_x,
            ),
            remote(
                self.acc0.at[pl.ds((1 - at.y) * size, size), right], self.buf1.at[:, right],
                self.send.at[sem + 1], self.recv.at[sem + 1], at.across_y,
            ),
        ]
        for copy in self.copies:
            copy.start()

    def start_second(self):
        for copy in self.copies:
            copy.wait()
        at = Places()
        left, right = cut_of(self.acc0.shape[1])
        size = self.buf1.shape[0]
        self.acc1[:, left] = self.acc0[pl.ds(at.x * size, size), left] + self.buf1[:, left]
        self.acc1[:, right] = self.acc0[pl.ds(at.y * size, size), right] + self.buf1[:, right]
        size, sem = self.buf2.shape[0], len(self.pieces) + 2
        self.copies = [
            remote(
                self.acc1.at[pl.ds((1 - at.y) * size, size), left], self.buf2.at[:, left],
                self.send.at[sem], self.recv.at[sem], at.across_y,
            ),
            remote(
                self.acc1.at[pl.ds((1 - at.x) * size, size), right], self.buf2.at[:, right],
                self.send.at[sem + 1], self.recv.at[sem + 1], at.across_x,
            ),
        ]
        for copy in self.copies:
            copy.start()

    def finish(self):
        for copy in self.copies:
            copy.wait()
        at = Places()
        left, right = cut_of(self.acc0.shape[1])
        size = self.buf2.shape[0]
        self.out_ref[:, left] = self.acc1[pl.ds(at.y * size, size), left] + self.buf2[:, left]
        self.out_ref[:, right] = self.acc1[pl.ds(at.x * size, size), right] + self.buf2[:, right]


class DenseGather:
    def __init__(self, a_ref, outs, refs):
        self.a_ref, self.outs = a_ref, outs
        (
            self.bufs, self.mine, self.eighth, self.acc1, self.acc0, self.send, self.recv,
            self.send_two, self.recv_two, self.send_three, self.recv_three, self.stores,
        ) = refs

    @staticmethod
    def scratch(rows, width, pieces):
        block = lambda parts: pltpu.VMEM((rows // parts, width), F32)
        dma = pltpu.SemaphoreType.DMA
        return [
            pltpu.VMEM((4, rows // 32, width), F32), block(32), block(8), block(4), block(2),
            dma((3,)), dma((4,)), dma((3,)), dma((4,)), dma((pieces + 4,)), dma((pieces + 4,)),
            dma((pieces,)),
        ]

    def start_line(self):
        at = Places()
        part = self.mine.shape[0]
        self.sends = [
            remote(
                self.a_ref.at[pl.ds(other * part, part), :], self.bufs.at[at.z],
                self.send.at[i], self.recv.at[at.z], at.line_peers[i],
            )
            for i, other in enumerate(at.line)
        ]
        for copy in self.sends:
            copy.start()
        self.bufs[at.z] = self.a_ref[pl.ds(at.z * part, part), :]

    def start_line_back(self):
        at = Places()
        part = self.mine.shape[0]
        for i, other in enumerate(at.line):
            remote(
                self.bufs.at[other], self.bufs.at[other], self.send.at[i], self.recv.at[other],
                at.line_peers[i],
            ).wait_recv()
        self.mine[...] = (self.bufs[0] + self.bufs[1]) + (self.bufs[2] + self.bufs[3])
        spread = [
            remote(
                self.mine, self.eighth.at[pl.ds(at.z * part, part), :], self.send_two.at[i],
                self.recv_two.at[at.z], at.line_peers[i],
            )
            for i, other in enumerate(at.line)
        ]
        for copy in spread:
            copy.start()
        self.sends += spread
        self.eighth[pl.ds(at.z * part, part), :] = self.mine[...]

    def swap(self, index, src, dst, mine, columns, peer):
        size = src.shape[0]
        out = remote(
            src.at[:, columns], dst.at[pl.ds(mine * size, size), columns],
            self.send_three.at[index], self.recv_three.at[index], peer,
        )
        out.start()
        dst[pl.ds(mine * size, size), columns] = src[:, columns]
        self.sends.append(out)
        return remote(
            src.at[:, columns], dst.at[pl.ds((1 - mine) * size, size), columns],
            self.send_three.at[index], self.recv_three.at[index], peer,
        )

    def start_first(self):
        at = Places()
        part = self.mine.shape[0]
        for i, other in enumerate(at.line):
            remote(
                self.mine, self.eighth.at[pl.ds(other * part, part), :], self.send_two.at[i],
                self.recv_two.at[other], at.line_peers[i],
            ).wait_recv()
        left, right = cut_of(self.eighth.shape[1])
        self.awaited = [
            self.swap(0, self.eighth, self.acc1, at.y, left, at.across_y),
            self.swap(1, self.eighth, self.acc1, at.x, right, at.across_x),
        ]

    def start_second(self):
        for copy in self.awaited:
            copy.wait_recv()
        at = Places()
        left, right = cut_of(self.eighth.shape[1])
        self.awaited = [
            self.swap(2, self.acc1, self.acc0, at.x, left, at.across_x),
            self.swap(3, self.acc1, self.acc0, at.y, right, at.across_y),
        ]

    def start_cores(self):
        for copy in self.awaited:
            copy.wait_recv()
        at = Places()
        half = self.acc0.shape[0]
        self.awaited, self.local = [], []
        first = 0
        for i, out in enumerate(self.outs):
            columns = pl.ds(first, out.shape[1])
            first += out.shape[1]
            rows, other_rows = pl.ds(at.c * half, half), pl.ds((1 - at.c) * half, half)
            index = 4 + i
            copy = remote(
                self.acc0.at[:, columns], out.at[rows, :], self.send_three.at[index],
                self.recv_three.at[index], at.near,
            )
            copy.start()
            self.sends.append(copy)
            self.awaited.append(
                remote(
                    self.acc0.at[:, columns], out.at[other_rows, :], self.send_three.at[index],
                    self.recv_three.at[index], at.near,
                )
            )
            store = pltpu.make_async_copy(
                self.acc0.at[:, columns], out.at[rows, :], self.stores.at[i]
            )
            store.start()
            self.local.append(store)

    def finish(self):
        for copy in self.awaited:
            copy.wait_recv()
        for copy in self.local:
            copy.wait()
        for copy in self.sends:
            copy.wait_send()


class Expert:
    def __init__(self, inward_ref, outward_ref, refs):
        self.inward_ref, self.outward_ref = inward_ref, outward_ref
        self.w13, self.w23, self.stage_one, self.stage_two, self.pre, self.sems = refs
        self.chunk = self.stage_one.shape[-1]
        self.count = self.w23.shape[0]

    @staticmethod
    def scratch(width, hidden, rows):
        chunk = min(512, hidden)
        count = hidden // chunk
        return [
            pltpu.VMEM((count, 3 * width, chunk), BF16), pltpu.VMEM((count, 3 * chunk, width), BF16),
            pltpu.VMEM((2, width, chunk), F32), pltpu.VMEM((2, chunk, width), F32),
            pltpu.VMEM((count, rows, chunk), F32), pltpu.SemaphoreType.DMA((4,)),
        ]

    def load(self, index):
        part, slot = pl.ds(index * self.chunk, self.chunk), index % 2
        return [
            pltpu.make_async_copy(
                self.inward_ref.at[:, part], self.stage_one.at[slot], self.sems.at[2 * slot]
            ),
            pltpu.make_async_copy(
                self.outward_ref.at[part, :], self.stage_two.at[slot], self.sems.at[2 * slot + 1]
            ),
        ]

    def start_weights(self):
        for copy in self.load(0):
            copy.start()

    def finish_weights(self):
        for index in range(self.count):
            if index + 1 < self.count:
                for copy in self.load(index + 1):
                    copy.start()
            for copy in self.load(index):
                copy.wait()
            self.w13[index] = one_below_other(self.stage_one[index % 2])
            self.w23[index] = one_below_other(self.stage_two[index % 2])

    def forward(self, hidden, out_ref):
        wide = side_by_side(hidden)
        out_ref[...] = jnp.zeros_like(out_ref)

        def step(index, carry):
            pre = product(wide, self.w13[index])
            self.pre[index] = pre
            out_ref[...] += product(side_by_side(swish(pre)), self.w23[index])
            return carry

        lax.fori_loop(0, self.count, step, 0)

    def backward(self, out_grad, hidden_grad):
        width = out_grad.shape[1]
        parts = halves(out_grad)
        hidden_grad[...] = jnp.zeros_like(hidden_grad)

        def step(index, carry):
            outward = self.w23[index]
            outward = outward[: self.chunk], outward[self.chunk : 2 * self.chunk]
            inward = self.w13[index]
            inward = inward[:width], inward[width : 2 * width]
            pre_grad = dot3(parts, outward, NT) * swish_slope(self.pre[index])
            hidden_grad[...] += dot3(halves(pre_grad), inward, NT)
            return carry

        lax.fori_loop(0, self.count, step, 0)


def pick_slots(slots, rows, sent, members):
    high, low = halves(rows)
    picked = product(slots, high) + product(slots, low)
    picked = picked.reshape(EXPERTS, sent.shape[1], rows.shape[1])
    groups = members // EXPERTS
    for expert in range(EXPERTS):
        for copy in range(groups):
            sent[expert * groups + copy] = picked[expert]


def put_slots(slots, returned, members):
    groups = members // EXPERTS
    pieces = []
    for expert in range(EXPERTS):
        piece = returned[expert * groups]
        for copy in range(1, groups):
            piece = piece + returned[expert * groups + copy]
        pieces.append(piece)
    high, low = halves(jnp.concatenate(pieces, axis=0))
    return lax.dot_general(slots, high, TN, preferred_element_type=F32) + lax.dot_general(
        slots, low, TN, preferred_element_type=F32
    )


def gate_of(hidden, router, off, chosen):
    logits = dot3(halves(hidden), router) + off
    weights = jnp.exp(logits - jnp.max(logits, axis=1, keepdims=True))
    prob = weights / jnp.sum(weights, axis=1, keepdims=True)
    return prob, jnp.sum(prob * chosen, axis=1, keepdims=True)


def mixture_kernel(
    members, parts, row_blocks, frames_ref, slots_ref, gain_ref, router_ref, off_ref, chosen_ref,
    inward_ref, outward_ref, out_ref, landed_ref, gate_ref, prob_ref, branch_ref, hidden_all_ref,
    sent, returned, hidden_sent, section, *rest,
):
    expert = Expert(inward_ref.at[0], outward_ref.at[0], rest[:6])
    seq_sems, back_sems, frame_sems, spread_sems = rest[6:9], rest[9:12], rest[12:15], rest[15:]
    step = members // parts
    to_experts = Ring(sent, landed_ref, members, 1, *seq_sems)
    back = Ring(sent, returned, members, 1, *back_sems)
    to_utterances = Ring(section, out_ref, parts, step, *frame_sems)
    spread = Spread(hidden_sent, hidden_all_ref, *spread_sems)
    expert.start_weights()
    pick_slots(slots_ref[...], frames_ref[...], sent, members)
    greet(to_experts.peers + spread.peers)
    to_experts.start()
    expert.finish_weights()
    to_experts.wait_receives()
    to_experts.wait_sends()
    rows = landed_ref[...].reshape(branch_ref.shape)
    unit, _ = norm_stats(rows)
    hidden = unit * gain_ref[...]
    hidden_sent[...] = hidden
    expert.forward(hidden, branch_ref)
    prob, gate = gate_of(hidden, halves(router_ref[...]), off_ref[...], chosen_ref[...])
    prob_ref[...] = prob
    gate_ref[...] = gate
    sent[...] = (0.5 * gate * branch_ref[...]).reshape(sent.shape)
    back.start()
    spread.start()
    back.wait_receives()
    spread.forward()
    x1 = frames_ref[...] + put_slots(slots_ref[...], returned, members)
    section[...] = x1.reshape(section.shape)
    to_utterances.start()
    to_utterances.wait_receives()
    spread.wait_receives()
    back.wait_sends()
    to_utterances.wait_sends()
    spread.wait_sends()


def mixture_block(
    frames, slots, gain_row, router, off, chosen, expert_in, expert_out, parts, capacity,
    collective_id,
):
    members, row_blocks = lax.axis_size("seq"), lax.axis_size("batch")
    rows, width = frames.shape
    count = members * capacity
    vmem = pl.BlockSpec(memory_space=pltpu.VMEM)
    hbm = pl.BlockSpec(memory_space=pl.ANY)
    dma = pltpu.SemaphoreType.DMA
    blocks = (parts, rows // parts, width)
    slot_blocks_shape = (members, capacity, width)
    outs = [
        blocks, slot_blocks_shape, (count, 1), (count, LANES), (count, width),
        (row_blocks, count, width),
    ]
    return pl.pallas_call(
        functools.partial(mixture_kernel, members, parts, row_blocks),
        in_specs=[vmem] * 6 + [hbm] * 2,
        out_specs=[vmem] * 5 + [hbm],
        out_shape=[jax.ShapeDtypeStruct(shape, F32) for shape in outs],
        scratch_shapes=[
            pltpu.VMEM(slot_blocks_shape, F32), pltpu.VMEM(slot_blocks_shape, F32),
            pltpu.VMEM((count, width), F32), pltpu.VMEM(blocks, F32),
        ]
        + Expert.scratch(width, expert_in.shape[2], count)
        + ring_semaphores(members)
        + ring_semaphores(members)
        + ring_semaphores(parts)
        + Spread.semaphores(),
        compiler_params=pltpu.CompilerParams(
            collective_id=collective_id, has_side_effects=True, vmem_limit_bytes=VMEM_BYTES
        ),
        cost_estimate=pl.CostEstimate(
            flops=60_000_000_000, bytes_accessed=20_000_000, transcendentals=0
        ),
    )(frames, slots, gain_row, router, off, chosen, expert_in, expert_out)


def mixture_both_kernel(
    members, parts, row_blocks, blocks_ref, slots_ref, drop_ref, grad_ref, grad_rows_a, grad_rows_b,
    gain_ref,
    last_gain_ref, router_ref, off_ref, chosen_ref, inward_ref, outward_ref, out_ref, plain_ref,
    last_rows_ref, hidden_all_ref, out_grad_all_ref, router_grad_ref, gain_grad_ref,
    last_gain_grad_ref, section, sent, landed, returned, hidden_sent, grad_sent, branch,
    hidden_grad, local, *rest,
):
    groups = members // EXPERTS
    expert = Expert(inward_ref.at[1], outward_ref.at[1], rest[:6])
    rest = rest[6:]
    in_sems, seq_sems, back_sems, out_sems = (rest[3 * i : 3 * i + 3] for i in range(4))
    spread_sems, grad_sems, rest = rest[12:15], rest[15:18], rest[18:]
    step = members // parts
    b, s = lax.axis_index("batch"), lax.axis_index("seq")
    to_frames = Ring(blocks_ref, section, parts, step, *in_sems)
    to_experts = Ring(sent, landed, members, 1, *seq_sems)
    back = Ring(sent, returned, members, 1, *back_sems)
    to_utterances = Ring(section, out_ref, parts, step, *out_sems)
    spread = Spread(hidden_sent, hidden_all_ref, *spread_sems)
    grad_spread = Spread(grad_sent, out_grad_all_ref, *grad_sems)
    greet(to_experts.peers + spread.peers)
    to_frames.start()
    expert.start_weights()
    expert.finish_weights()
    to_frames.wait_receives()
    x3 = section[...].reshape(plain_ref.shape)
    pick_slots(slots_ref[...], x3, sent, members)
    to_experts.start()
    drop = drop_ref[...]
    last_gain = last_gain_ref[...]
    out_grad = grad_ref[...]
    unit, inverse = norm_stats(x3)
    plain_ref[...] = drop * (unit * last_gain)
    last_gain_grad = jnp.sum(drop * out_grad * unit, axis=0, keepdims=True)
    local[...] = drop * norm_back(out_grad, last_gain, unit, inverse)
    to_experts.wait_receives()
    to_experts.wait_sends()
    rows = landed[...].reshape(branch.shape)
    unit_four, inverse_four = norm_stats(rows)
    gain = gain_ref[...]
    hidden = unit_four * gain
    hidden_sent[...] = hidden
    spread.start()
    router = halves(router_ref[...])
    chosen = chosen_ref[...]
    prob, gate = gate_of(hidden, router, off_ref[...], chosen)
    expert.forward(hidden, branch)
    whole_branch = branch[...]
    first_copy = 1.0
    if groups > 1:
        others, send, recv = rest
        base = s // groups * groups
        first_copy = cast_one(lax.rem(s, groups) == 0)
        copies = [
            remote(
                branch, others.at[off - 1], send.at[off - 1], recv.at[off - 1],
                (b, base + lax.rem(s + off, groups)),
            )
            for off in range(1, groups)
        ]
        for copy in copies:
            copy.start()
        for copy in copies:
            copy.wait()
        for off in range(1, groups):
            whole_branch = whole_branch + others[off - 1]
    unit_five, inverse_five = norm_stats(rows + 0.5 * gate * whole_branch)
    grad_rows = jnp.concatenate([grad_rows_a[...], grad_rows_b[...]], axis=1).reshape(branch.shape)
    last_rows_ref[...] = (first_copy * (unit_five * last_gain)).reshape(last_rows_ref.shape)
    last_gain_grad_ref[...] = last_gain_grad + first_copy * jnp.sum(
        grad_rows * unit_five, axis=0, keepdims=True
    )
    grad_four = norm_back(grad_rows, last_gain, unit_five, inverse_five)
    branch_grad = 0.5 * grad_four
    gate_grad = first_copy * jnp.sum(branch_grad * whole_branch, axis=1, keepdims=True)
    row_grad = branch_grad * gate
    grad_sent[...] = row_grad
    spread.forward()
    grad_spread.start()
    expert.backward(row_grad, hidden_grad)
    logit_grad = halves(gate_grad * gate * (chosen - prob))
    all_grad = hidden_grad[...] + dot3(logit_grad, router, NT)
    router_grad_ref[...] = dot3(logit_grad, halves(hidden), TN)
    gain_grad_ref[...] = jnp.sum(all_grad * unit_four, axis=0, keepdims=True)
    row_back = first_copy * grad_four + norm_back(all_grad, gain, unit_four, inverse_four)
    sent[...] = row_back.reshape(sent.shape)
    back.start()
    to_frames.wait_sends()
    back.wait_receives()
    grad_spread.forward()
    back_grad = local[...] + put_slots(slots_ref[...], returned, members)
    section[...] = back_grad.reshape(section.shape)
    to_utterances.start()
    to_utterances.wait_receives()
    spread.wait_receives()
    grad_spread.wait_receives()
    back.wait_sends()
    to_utterances.wait_sends()
    spread.wait_sends()
    grad_spread.wait_sends()


def mixture_both_block(
    blocks, slots, drop, out_grad, grad_rows_a, grad_rows_b, gain_row, last_gain_row, router, off, chosen,
    expert_in, expert_out, capacity, collective_id,
):
    members, row_blocks = lax.axis_size("seq"), lax.axis_size("batch")
    groups = members // EXPERTS
    parts, frame_rows, width = blocks.shape
    rows, count = parts * frame_rows, members * capacity
    vmem = pl.BlockSpec(memory_space=pltpu.VMEM)
    hbm = pl.BlockSpec(memory_space=pl.ANY)
    dma = pltpu.SemaphoreType.DMA
    slot_shape = (members, capacity, width)
    outs = [
        blocks.shape, (rows, width), slot_shape, (row_blocks, count, width),
        (row_blocks, count, width), (LANES, width), (1, width), (1, width),
    ]
    scratch = (
        [
            pltpu.VMEM(blocks.shape, F32), pltpu.VMEM(slot_shape, F32), pltpu.VMEM(slot_shape, F32),
            pltpu.VMEM(slot_shape, F32), pltpu.VMEM((count, width), F32),
            pltpu.VMEM((count, width), F32), pltpu.VMEM((count, width), F32),
            pltpu.VMEM((count, width), F32), pltpu.VMEM((rows, width), F32),
        ]
        + Expert.scratch(width, expert_in.shape[2], count)
        + ring_semaphores(parts)
        + ring_semaphores(members)
        + ring_semaphores(members)
        + ring_semaphores(parts)
        + Spread.semaphores() + [dma]
        + Spread.semaphores() + [dma]
    )
    if groups > 1:
        scratch += [pltpu.VMEM((groups - 1, count, width), F32), dma((groups,)), dma((groups,))]
    return pl.pallas_call(
        functools.partial(mixture_both_kernel, members, parts, row_blocks),
        in_specs=[hbm] + [vmem] * 10 + [hbm] * 2,
        out_specs=[vmem] * 3 + [hbm] * 2 + [vmem] * 3,
        out_shape=[jax.ShapeDtypeStruct(shape, F32) for shape in outs],
        scratch_shapes=scratch,
        compiler_params=pltpu.CompilerParams(
            collective_id=collective_id, has_side_effects=True, vmem_limit_bytes=58 * 1024 * 1024
        ),
        cost_estimate=pl.CostEstimate(
            flops=90_000_000_000, bytes_accessed=30_000_000, transcendentals=0
        ),
    )(
        blocks, slots, drop, out_grad, grad_rows_a, grad_rows_b, gain_row, last_gain_row, router, off, chosen,
        expert_in, expert_out,
    )


def grad_chunks(hidden, row_blocks):
    if square_mesh():
        return hidden // row_blocks, 2
    chunk = min(512, hidden)
    return chunk, hidden // chunk


def return_kernel(
    members, parts, row_blocks, pieces, chunks, blocks_ref, slots_ref, inward_ref, outward_ref,
    hidden_ref, out_grad_ref, *rest,
):
    dense, rest = rest[:pieces], rest[pieces:]
    grad_ref, landed_ref, dw1_ref, dw2_ref = rest[:4]
    rest = rest[4:]
    if pieces:
        dense_out, rest = rest[0], rest[1:]
    sent, buf_one, buf_two, load_sem = rest[:4]
    frame_sems, seq_sems = rest[4:7], rest[7:10]
    b = lax.axis_index("batch")
    ids = [b, row_blocks - 1 - b] if pieces else list(range(chunks))
    grads = ExpertGrads(inward_ref.at[1], outward_ref.at[1], ids, rest[10:21])
    step = members // parts
    frame_ring = Ring(blocks_ref, grad_ref, parts, step, *frame_sems)
    seq_ring = Ring(sent, landed_ref, members, 1, *seq_sems)
    peers = list(seq_ring.peers)
    if pieces:
        scatter = DenseScatter(dense, dense_out, rest[21:])
        at = Places()
        peers += [at.across_x, at.across_y]

    def load_rows(index):
        slot = index % 2
        return [
            pltpu.make_async_copy(hidden_ref.at[index], buf_one.at[slot], load_sem.at[2 * slot]),
            pltpu.make_async_copy(
                out_grad_ref.at[index], buf_two.at[slot], load_sem.at[2 * slot + 1]
            ),
        ]

    greet(peers)
    frame_ring.start()
    if pieces:
        scatter.start_cores()
    grads.start_weights()
    for load in load_rows(0):
        load.start()
    grads.finish_weights()
    if pieces:
        scatter.start_first()
    for index in range(row_blocks):
        if index + 1 < row_blocks:
            for load in load_rows(index + 1):
                load.start()
        for load in load_rows(index):
            load.wait()
        grads.block(buf_one[index % 2], buf_two[index % 2], index == 0)
        if index == 0:
            frame_ring.wait_receives()
            flat = grad_ref[...].reshape(slots_ref.shape[1], grad_ref.shape[-1])
            pick_slots(slots_ref[...], flat, sent, members)
            seq_ring.start()
        if pieces and index == 1:
            scatter.start_second()
        if pieces and index == 2:
            scatter.finish()
    grads.store(lambda index: dw1_ref.at[index], lambda index: dw2_ref.at[index])
    seq_ring.wait_receives()
    seq_ring.wait_sends()
    frame_ring.wait_sends()


def return_block(
    blocks, slots, expert_in, expert_out, hidden_all, out_grad_all, dense, capacity, collective_id
):
    members, row_blocks = lax.axis_size("seq"), hidden_all.shape[0]
    parts, frame_rows, width = blocks.shape
    count = hidden_all.shape[1]
    chunk, chunks = grad_chunks(expert_in.shape[2], row_blocks)
    vmem = pl.BlockSpec(memory_space=pltpu.VMEM)
    hbm = pl.BlockSpec(memory_space=pl.ANY)
    dma = pltpu.SemaphoreType.DMA
    dense_width = sum(piece.shape[1] for piece in dense)
    outs = [
        blocks.shape, (members, capacity, width), (chunks, width, chunk), (chunks, chunk, width),
    ]
    out_specs = [vmem, hbm, hbm, hbm]
    scratch = (
        [
            pltpu.VMEM((members, capacity, width), F32), pltpu.VMEM((2, count, width), F32),
            pltpu.VMEM((2, count, width), F32), dma((4,)),
        ]
        + ring_semaphores(parts)
        + ring_semaphores(members)
        + ExpertGrads.scratch(width, chunk, chunks, count)
    )
    if dense:
        outs.append((width // 8, dense_width))
        out_specs.append(vmem)
        scratch += DenseScatter.scratch(width, dense_width, len(dense))
    return pl.pallas_call(
        functools.partial(return_kernel, members, parts, row_blocks, len(dense), chunks),
        in_specs=[hbm, vmem] + [hbm] * (4 + len(dense)),
        out_specs=out_specs,
        out_shape=[jax.ShapeDtypeStruct(shape, F32) for shape in outs],
        scratch_shapes=scratch,
        compiler_params=pltpu.CompilerParams(
            collective_id=collective_id, has_side_effects=True, vmem_limit_bytes=60 * 1024 * 1024
        ),
        cost_estimate=pl.CostEstimate(
            flops=60_000_000_000, bytes_accessed=40_000_000, transcendentals=0
        ),
    )(blocks, slots, expert_in, expert_out, hidden_all, out_grad_all, *dense)


def back_chunk(hidden, rows):
    return min(512 if rows <= 512 else 256, hidden)


def expert_back_kernel(
    row_blocks, columns, widths, grad_ref, rows_ref, gain_ref, gate_ref, prob_ref, chosen_ref,
    router_ref, branch_ref, router_two_ref, gain_two_ref, gain_three_ref, gain_four_ref,
    gain_five_ref, taps_grad_ref, slots_ref, upper_ref, inward_ref, outward_ref, hidden_ref,
    quarter_one, quarter_two, *rest,
):
    if widths:
        dense_ref, rest = rest[0], rest[1:]
    frames_grad_ref, landed_ref, dw1_ref, dw2_ref, small_out_ref = rest[:5]
    rest = rest[5:]
    dense_outs, rest = rest[: len(widths)], rest[len(widths) :]
    sent, back_rows, returned, buf_one, buf_two, small_mine, send_b, recv_b, load_sem = rest[:9]
    ring_sems, small_refs, local_sems, rest = rest[9:12], rest[12:18], rest[18], rest[19:]
    hidden_width = inward_ref.shape[2]
    chunk = back_chunk(hidden_width, grad_ref.shape[0])
    grads = ExpertGrads(
        inward_ref.at[0], outward_ref.at[0], list(range(hidden_width // chunk)), rest[:11]
    )
    rest = rest[11:]
    ring = Ring(back_rows, returned, columns, 1, *ring_sems)
    spread = Spread(sent, landed_ref, send_b, recv_b)
    small = SmallSum(row_blocks, columns, small_refs)
    grads.start_weights()
    b = lax.axis_index("batch")
    size = quarter_one.shape[2]

    def place_of(which, index):
        part = pl.ds(pl.multiple_of(index * size, size), size)
        return dw1_ref.at[1, :, part] if which == 0 else dw2_ref.at[1, part, :]

    ids = [b, row_blocks - 1 - b] if widths else list(range(quarter_one.shape[0]))
    local = [
        pltpu.make_async_copy(
            (quarter_one, quarter_two)[j].at[i], place_of(j, index), local_sems.at[2 * i + j]
        )
        for i, index in enumerate(ids)
        for j in range(2)
    ]
    greet(small.row_peers + ring.peers)
    branch_grad = 0.5 * grad_ref[...]
    gate = gate_ref[...]
    sent[...] = branch_grad * gate
    spread.start()
    if widths:
        dense = DenseGather(dense_ref, dense_outs, rest[:12])
        dense.start_line()
        send_n, recv_n = rest[12:]
        at = Places()
        quarters, into = [], []
        for i, peer in enumerate((at.across_x, at.across_y)):
            for j in range(2):
                src = (quarter_one, quarter_two)[j].at[0]
                sems = send_n.at[2 * i + j], recv_n.at[2 * i + j]
                quarters.append(remote(src, place_of(j, b), *sems, peer))
                into.append(remote(src, place_of(j, peer[0]), *sems, peer))
        for copy in quarters[::2]:
            copy.start()
    for copy in local:
        copy.start()
    grads.finish_weights()
    unit, inverse = norm_stats(rows_ref[...])
    gain_row = gain_ref[...]
    hidden = unit * gain_row
    grads.block(hidden, sent[...], True, buf_one)
    gate_grad = jnp.sum(branch_grad * branch_ref[...], axis=1, keepdims=True)
    logit_grad = halves(gate_grad * gate * (chosen_ref[...] - prob_ref[...]))
    hidden_grad = buf_one[...] + dot3(logit_grad, halves(router_ref[...]), NT)
    router_grad = dot3(logit_grad, halves(hidden), TN)
    small_mine[...] = jnp.zeros_like(small_mine)
    small_mine[:EXPERTS, :] = router_grad[:EXPERTS, :]
    small_mine[EXPERTS : 2 * EXPERTS, :] = router_two_ref[:EXPERTS, :]
    gain_one = jnp.sum(hidden_grad * unit, axis=0, keepdims=True)
    gains = (gain_one, gain_two_ref, gain_three_ref, gain_four_ref, gain_five_ref)
    for i, gain in enumerate(gains):
        small_mine[2 * EXPERTS + i : 2 * EXPERTS + i + 1, :] = gain[...]
    small_mine[3 * EXPERTS : 3 * EXPERTS + KERNEL, :] = taps_grad_ref[:KERNEL, :]
    extra = norm_back(hidden_grad, gain_row, unit, inverse)
    back_rows[...] = extra.reshape(back_rows.shape)
    ring.start()
    small.share(small_mine[...], 0)
    if widths:
        dense.start_line_back()
    spread.forward()
    if widths:
        for copy in quarters[1::2]:
            copy.start()

    def first_middle():
        small.share(small.total(0), 1)
        if widths:
            dense.start_first()

    def second_middle():
        small_out_ref[...] = small.total(1)
        if widths:
            dense.start_second()

    def third_middle():
        if widths:
            dense.start_cores()
        ring.wait_receives()
        frames_grad_ref[...] = upper_ref[...] + put_slots(slots_ref[...], returned, columns)

    middles = [first_middle, second_middle, third_middle]
    for k in range(1, row_blocks):
        load = pltpu.make_async_copy(hidden_ref.at[k], buf_one, load_sem.at[0])
        load.start()
        spread.wait_receive(k)
        load_two = pltpu.make_async_copy(landed_ref.at[k], buf_two, load_sem.at[1])
        load_two.start()
        load.wait()
        load_two.wait()
        middle = middles[k - 1] if k <= len(middles) else None
        grads.block(buf_one[...], buf_two[...], False, None, middle)
    chunk_of = lambda index: pl.ds(index * chunk, chunk)
    grads.store(
        lambda index: dw1_ref.at[0, :, chunk_of(index)],
        lambda index: dw2_ref.at[0, chunk_of(index), :],
    )
    if widths:
        dense.finish()
        for copy in into:
            copy.wait_recv()
        for copy in quarters:
            copy.wait_send()
    for copy in local:
        copy.wait()
    ring.wait_sends()
    spread.wait_sends()


def expert_back_block(
    grad, rows, gain_row, gate, prob, chosen, router, branch, small_parts, slots, upper, expert_in,
    expert_out, hidden_all, quarters, dense, widths, collective_id,
):
    row_blocks, columns = lax.axis_size("batch"), lax.axis_size("seq")
    count, width = grad.shape
    capacity = count // columns
    hidden = expert_in.shape[2]
    chunk = back_chunk(hidden, count)
    vmem = pl.BlockSpec(memory_space=pltpu.VMEM)
    hbm = pl.BlockSpec(memory_space=pl.ANY)
    dma = pltpu.SemaphoreType.DMA
    small_shape = (5 * EXPERTS, width)
    outs = [
        upper.shape, (row_blocks, count, width), expert_in.shape, expert_out.shape, small_shape,
    ]
    outs += [(width, w) for w in widths]
    scratch = (
        [
            pltpu.VMEM((count, width), F32), pltpu.VMEM((columns, capacity, width), F32),
            pltpu.VMEM((columns, capacity, width), F32),
            pltpu.VMEM((count, width), F32), pltpu.VMEM((count, width), F32),
            pltpu.VMEM(small_shape, F32), *Spread.semaphores(),
            dma((2,)),
        ]
        + ring_semaphores(columns)
        + SmallSum.scratch(row_blocks, columns, small_shape)
        + [dma((2 * quarters[0].shape[0],))]
        + ExpertGrads.scratch(width, chunk, hidden // chunk, count)
    )
    if widths:
        scratch += DenseGather.scratch(width, sum(widths), len(widths))
        scratch += [dma((4,)), dma((4,))]
    out = pl.pallas_call(
        functools.partial(expert_back_kernel, row_blocks, columns, widths),
        in_specs=[vmem] * (10 + len(small_parts)) + [hbm] * 5 + [vmem] * len(dense),
        out_specs=[vmem] + [hbm] * 3 + [vmem] + [hbm] * len(widths),
        out_shape=[jax.ShapeDtypeStruct(shape, F32) for shape in outs],
        scratch_shapes=scratch,
        compiler_params=pltpu.CompilerParams(
            collective_id=collective_id, has_side_effects=True, vmem_limit_bytes=61 * 1024 * 1024
        ),
        cost_estimate=pl.CostEstimate(
            flops=60_000_000_000, bytes_accessed=40_000_000, transcendentals=0
        ),
    )(
        grad, rows, gain_row, gate, prob, chosen, router, branch, *small_parts, slots, upper,
        expert_in, expert_out, hidden_all, *quarters, *dense,
    )
    return out[0], out[2], out[3], out[4], out[5:]


def per_device(
    frames, out_grad, lengths, routing, norm_gains, routers, expert_in, expert_out,
    attn_qkv, attn_out, conv_in, depthwise, bn_gain, bn_bias, conv_out, running_mean, running_var,
):
    utter_count, frame_rows, width = frames.shape
    members = lax.axis_size("seq")
    step = members // utter_count
    groups = members // EXPERTS
    capacity = utter_count * frame_rows // EXPERTS
    place = lax.axis_index("seq")
    expert = place // groups
    first_copy = (place % groups == 0).astype(jnp.float32)
    row_ids = jnp.arange(frame_rows, dtype=jnp.int32)
    live_here = (place * frame_rows + row_ids)[None, :] < lengths[:, None]
    flat_frames = frames.reshape(-1, width)
    flat_grad = out_grad.reshape(-1, width)
    kept_one, slots_one = slot_matrix(routing[..., 0].reshape(-1), live_here.reshape(-1), capacity)
    kept_two, slots_two = slot_matrix(routing[..., 1].reshape(-1), live_here.reshape(-1), capacity)

    rows = utter_count * frame_rows
    block_shape = (utter_count, frame_rows, width)
    gain_rows = norm_gains.reshape(5, 1, width)
    lane = jnp.arange(LANES, dtype=jnp.int32)[None, :]
    chosen = (lane == expert).astype(F32)
    off = jnp.where(lane < EXPERTS, 0.0, NEGATIVE_FILL)
    wide_routers = jnp.pad(routers, ((0, 0), (0, 0), (0, LANES - EXPERTS)))
    section_one, rows_one, gate_one, prob_one, branch_one, hidden_one_all = mixture_block(
        flat_frames, slots_one, gain_rows[0], wide_routers[0], off, chosen, expert_in, expert_out,
        utter_count, capacity, 2,
    )
    section_one = section_one.reshape(rows, width)
    rows_one = rows_one.reshape(-1, width)

    utter = place // step
    low = place % step
    length = lax.dynamic_index_in_dim(lengths, utter, keepdims=False)
    parts = jnp.arange(utter_count, dtype=jnp.int32)

    def positions_of(offset):
        other = (low + offset) % step
        return ((parts * step + other)[:, None] * frame_rows + row_ids[None, :]).reshape(-1)

    positions = positions_of(0)
    live = (positions < length).astype(jnp.float32)[:, None]
    half = HEAD // 2
    frequency = 10000.0 ** (-jnp.arange(half, dtype=F32) / half)
    angles = positions.astype(F32)[:, None] * frequency[None, :]
    cosine, sine = jnp.cos(angles), jnp.sin(angles)
    cosine = jnp.concatenate([cosine] * (LANES // half), axis=1)
    sine = jnp.concatenate([-sine, sine] * (LANES // HEAD), axis=1)
    usable = jnp.concatenate([positions_of(i) for i in range(step)]) < length
    extra = jnp.where(
        lane == HEAD,
        jnp.where(usable, 0.0, NEGATIVE_FILL)[:, None],
        ((lane > HEAD) & (lane < HEAD + 4)).astype(F32),
    )
    queries, key_values = plain_call(
        project_kernel, [(rows, width), (rows, 2 * width)],
        [section_one, gain_rows[1], attn_qkv, cosine, sine], flops=2_500_000_000,
    )
    key_values = near_gather(key_values, step)
    half = capacity // 2
    out_blocks = slot_blocks(slots_two, flat_grad, capacity, groups)
    attended, log_total, section_two, glu_in, glu, grad_rows_a = attention_block(
        queries, key_values, extra, section_one, attn_out, gain_rows[2], conv_in, live,
        out_blocks[:, :half], 3,
    )
    glu = glu.reshape(block_shape)
    taps = jnp.concatenate([depthwise, jnp.zeros((1, width), F32)], axis=0)
    live_blocks = live.reshape(utter_count, frame_rows, 1)
    bn_rows = (bn_gain.reshape(1, width), bn_bias.reshape(1, width))
    rim_shape = (utter_count, RIM, width)
    convolved, sums, section_three, glu_before, glu_after, grad_rows_b = conv_chain(
        False, step,
        [
            block_shape, (8, width), (rows, width), rim_shape, rim_shape,
            (members, capacity - half, width),
        ],
        [glu, taps, live_blocks, *bn_rows, conv_out, section_two, out_blocks[:, half:]], [], 4, True,
    )
    frame_count = sums[2]
    averaged = sums[0] / frame_count
    variance = sums[1] / frame_count - averaged * averaged

    (
        grad_three, layer_plain, last_rows, hidden_two_all, out_grad_two_all, router_two, gain_four,
        gain_five,
    ) = mixture_both_block(
        section_three.reshape(block_shape), slots_two, 1.0 - kept_two.astype(F32)[:, None],
        flat_grad, grad_rows_a, grad_rows_b, gain_rows[3], gain_rows[4], wide_routers[1], off, chosen,
        expert_in, expert_out, capacity, 6,
    )

    grad_three = grad_three.reshape(rows, width)
    conv_out_grad, parts_sum, depthwise_grad, glu_grad = conv_chain(
        True, step, [(width, width), (8, width), (KERNEL + 1, width), block_shape],
        [
            grad_three, convolved, sums, *bn_rows, conv_out, taps, live_blocks, glu, glu_before,
            glu_after,
        ],
        [pltpu.VMEM((KERNEL, 8, width), F32), pltpu.VMEM(block_shape, F32)], 5,
    )
    bn_gain_grad, bn_bias_grad = parts_sum[0], parts_sum[1]
    conv_in_grad, gain_three, grad_two, attn_out_grad, attended_grad = plain_call(
        glu_back_kernel,
        [(width, 2 * width), (1, width), (rows, width), (width, width), (rows, width)],
        [
            glu_grad.reshape(rows, width), glu_in, section_two, gain_rows[2], conv_in, grad_three,
            attended, attn_out,
        ],
        flops=5_000_000_000,
    )
    query_grad, key_grads, value_grads, last_back = attention_back_block(
        queries, attended_grad, attended, key_values, log_total, extra, last_rows, 9
    )
    layer_out = fold_back(slots_two, last_back, capacity, groups) + layer_plain
    key_grads, value_grads = near_back(key_grads, step), near_back(value_grads, step)
    qkv_grad, gain_two, grad_one = plain_call(
        functools.partial(project_back_kernel, step),
        [(width, 3 * width), (1, width), (rows, width)],
        [
            query_grad, *key_grads, *value_grads, section_one, gain_rows[1], attn_qkv, cosine, sine,
            grad_two,
        ],
        flops=5_000_000_000,
    )

    pieces = (qkv_grad, attn_out_grad, conv_in_grad, conv_out_grad)
    in_kernel = square_mesh()
    grad_one, grad_rows, inward_two, outward_two, *dense = return_block(
        grad_one.reshape(block_shape), slots_one, expert_in, expert_out, hidden_two_all,
        out_grad_two_all, pieces if in_kernel else (), capacity, 11,
    )
    grad_one = grad_one.reshape(rows, width)
    frames_grad, expert_in_grad, expert_out_grad, small, dense = expert_back_block(
        grad_rows.reshape(-1, width), rows_one, gain_rows[0], gate_one, prob_one, chosen,
        wide_routers[0], branch_one,
        (router_two, gain_two, gain_three, gain_four, gain_five, depthwise_grad), slots_one, grad_one,
        expert_in, expert_out, hidden_one_all, (inward_two, outward_two), dense,
        tuple(p.shape[1] for p in pieces) if in_kernel else (), 13,
    )
    if not in_kernel:
        dense = lax.psum(pieces, ("batch", "seq"))
    qkv_grad, attn_out_grad, conv_in_grad, conv_out_grad = dense
    first = 2 * EXPERTS
    routers_grad = small[:first].reshape(2, EXPERTS, width).transpose(0, 2, 1)
    gains_grad = small[first : first + 5]
    depthwise_grad = small[first + EXPERTS : first + EXPERTS + KERNEL]
    new_mean = (1.0 - MOMENTUM) * running_mean + MOMENTUM * averaged
    new_var = (1.0 - MOMENTUM) * running_var + MOMENTUM * variance * frame_count / (
        frame_count - 1.0
    )
    return (
        layer_out.reshape(frames.shape), frames_grad.reshape(frames.shape), gains_grad, routers_grad,
        expert_in_grad, expert_out_grad,
        qkv_grad, attn_out_grad, conv_in_grad, depthwise_grad, bn_gain_grad, bn_bias_grad,
        conv_out_grad, new_mean, new_var,
    )


def solution(mesh):
    frame_spec = P("batch", "seq", None)
    in_specs = (
        frame_spec, frame_spec, P("batch"), frame_spec, P(), P(),
        P(None, None, "seq"), P(None, "seq", None),
    ) + (P(),) * 9
    out_specs = (
        frame_spec, frame_spec, P(), P(), P(None, None, "seq"), P(None, "seq", None),
    ) + (P(),) * 9
    return jax.shard_map(
        per_device, mesh=mesh, in_specs=in_specs, out_specs=out_specs, check_vma=False
    )
```

```python
import functools
import math

import jax
import jax.numpy as jnp
from jax import lax
from jax.experimental import pallas as pl
from jax.experimental.pallas import tpu as pltpu
from jax.sharding import PartitionSpec as P

HEADS = 8
EXPERTS = 8
KERNEL = 15
HEAD = 64
EPSILON = 1e-05
MOMENTUM = 0.1
NEGATIVE_FILL = -1e30
HIGH = lax.Precision.HIGH
MESH = pl.DeviceIdType.MESH
F32 = jnp.float32
BF16 = jnp.bfloat16
LANES = 128
SCORE_SCALE = HEAD ** (-0.5) / math.log(2.0)
VMEM_BYTES = 52 * 1024 * 1024
PLAIN_BYTES = 36 * 1024 * 1024


def mm(left_side, right_side):
    return jnp.dot(left_side, right_side, precision=HIGH, preferred_element_type=jnp.float32)


def mm_tn(left_side, right_side):
    return lax.dot_general(
        left_side, right_side, (((0,), (0,)), ((), ())), precision=HIGH,
        preferred_element_type=jnp.float32,
    )


def mm_nt(left_side, right_side):
    return lax.dot_general(
        left_side, right_side, (((1,), (1,)), ((), ())), precision=HIGH,
        preferred_element_type=jnp.float32,
    )


def einsum_high(pattern, left_side, right_side):
    return jnp.einsum(
        pattern, left_side, right_side, precision=HIGH, preferred_element_type=jnp.float32
    )


def norm_stats(values):
    centered = values - jnp.mean(values, axis=-1, keepdims=True)
    inverse = lax.rsqrt(jnp.mean(centered * centered, axis=-1, keepdims=True) + EPSILON)
    return centered * inverse, inverse


def norm_back(grad, gain_row, unit, inverse):
    scaled = grad * gain_row
    return inverse * (
        scaled
        - jnp.mean(scaled, axis=-1, keepdims=True)
        - unit * jnp.mean(scaled * unit, axis=-1, keepdims=True)
    )


def swish(values):
    return values * jax.nn.sigmoid(values)


def swish_slope(values):
    gate = jax.nn.sigmoid(values)
    return gate * (1.0 + values * (1.0 - gate))


def remote(src, dst, send, recv, peer):
    return pltpu.make_async_remote_copy(
        src_ref=src, dst_ref=dst, send_sem=send, recv_sem=recv, device_id=peer, device_id_type=MESH
    )


def greet(peers):
    barrier = pltpu.get_barrier_semaphore()
    for peer in peers:
        pl.semaphore_signal(barrier, inc=1, device_id=peer, device_id_type=MESH)
    pl.semaphore_wait(barrier, len(peers))


class Ring:
    def __init__(self, src, dst, members, step, send, recv, local):
        b, s = lax.axis_index("batch"), lax.axis_index("seq")
        me, low = s // step, lax.rem(s, step)
        others = [lax.rem(me + off, members) for off in range(1, members)]
        self.peers = [(b, other * step + low) for other in others]
        self.own = pltpu.make_async_copy(src.at[me], dst.at[me], local)
        self.sends = [
            remote(src.at[other], dst.at[me], send.at[i], recv.at[me], self.peers[i])
            for i, other in enumerate(others)
        ]
        self.receives = [
            remote(src.at[other], dst.at[other], send.at[i], recv.at[other], self.peers[i])
            for i, other in enumerate(others)
        ]

    def start(self):
        for send in self.sends:
            send.start()
        self.own.start()

    def wait_receives(self):
        self.own.wait()
        for receive in self.receives:
            receive.wait_recv()

    def wait_sends(self):
        for send in self.sends:
            send.wait_send()


def ring_semaphores(members):
    dma = pltpu.SemaphoreType.DMA
    return [dma((members,)), dma((members,)), dma]


def square_mesh():
    return (lax.axis_size("batch"), lax.axis_size("seq")) == (4, 8)


class Spread:
    def __init__(self, src, dst, send, recv, local=None):
        b, s = lax.axis_index("batch"), lax.axis_index("seq")
        count = lax.axis_size("batch")
        self.square = square_mesh()
        if self.square:
            x, y = lax.rem(b, 2), b // 2
            across_x, across_y = (b + 1 - 2 * x, s), (b + 2 - 4 * y, s)
            half = src.shape[0] // 2
            low, high = pl.ds(0, half), pl.ds(half, half)
            self.peers = [across_x, across_y]
            plan = [
                (src.at[low], 1, low, across_x), (src.at[high], 2, high, across_y),
                (src.at[high], 1, high, across_x), (src.at[low], 2, low, across_y),
                (dst.at[1, low], 3, low, across_y), (dst.at[2, high], 3, high, across_x),
            ]
            self.copies = [
                remote(rows, dst.at[piece, part], send.at[i], recv.at[i], peer)
                for i, (rows, piece, part, peer) in enumerate(plan)
            ]
            self.needs = {1: (2,), 2: (3,), 3: (4, 5)}
            self.first = 4
        else:
            self.peers = [(lax.rem(b + k, count), s) for k in range(1, count)]
            self.copies = [
                remote(src, dst.at[k], send.at[k - 1], recv.at[k - 1], self.peers[k - 1])
                for k in range(1, count)
            ]
            self.needs = {k: (k - 1,) for k in range(1, count)}
            self.first = count - 1
        self.own = None if local is None else pltpu.make_async_copy(src, dst.at[0], local)

    @staticmethod
    def semaphores():
        count = 6 if square_mesh() else max(lax.axis_size("batch") - 1, 1)
        return [pltpu.SemaphoreType.DMA((count,)), pltpu.SemaphoreType.DMA((count,))]

    def start(self):
        for copy in self.copies[: self.first]:
            copy.start()
        if self.own is not None:
            self.own.start()

    def forward(self):
        if self.square:
            for i in range(2):
                self.copies[i].wait_recv()
                self.copies[4 + i].start()

    def wait_receive(self, piece):
        for i in self.needs[piece]:
            self.copies[i].wait_recv()

    def wait_receives(self):
        for piece in self.needs:
            self.wait_receive(piece)
        if self.own is not None:
            self.own.wait()

    def wait_sends(self):
        for copy in self.copies:
            copy.wait_send()


def near_pairs(step, shift):
    count = lax.axis_size("seq")
    return [(i, i // step * step + (i % step + shift) % step) for i in range(count)]


def near_gather(rows, step):
    return [rows] + [
        lax.ppermute(rows, "seq", near_pairs(step, step - shift)) for shift in range(1, step)
    ]


def near_back(pieces, step):
    return [pieces[0]] + [
        lax.ppermute(pieces[shift], "seq", near_pairs(step, shift)) for shift in range(1, step)
    ]


def slot_matrix(routes, live_flat, capacity):
    experts = jnp.arange(EXPERTS, dtype=jnp.int32)
    match = (routes[:, None] == experts[None, :]) & live_flat[:, None]
    rank = jnp.cumsum(match.astype(jnp.int32), axis=0) - 1
    rank = jnp.sum(jnp.where(match, rank, 0), axis=-1)
    kept = live_flat & (rank < capacity)
    slot = jnp.where(kept, routes * capacity + rank, -1)
    slots = jnp.arange(EXPERTS * capacity, dtype=jnp.int32)
    return kept, (slots[:, None] == slot[None, :]).astype(jnp.bfloat16)


def split_two(values):
    high = lax.reduce_precision(values, exponent_bits=8, mantissa_bits=7)
    return high.astype(jnp.bfloat16), (values - high).astype(jnp.bfloat16)


def pick(matrix, rows):
    width = rows.shape[-1]
    both = jnp.concatenate(split_two(rows), axis=-1)
    out = jnp.dot(matrix, both, preferred_element_type=jnp.float32)
    return out[:, :width] + out[:, width:]


def put(matrix, rows):
    width = rows.shape[-1]
    both = jnp.concatenate(split_two(rows), axis=-1)
    out = lax.dot_general(
        matrix, both, (((0,), (0,)), ((), ())), preferred_element_type=jnp.float32
    )
    return out[:, :width] + out[:, width:]


def slot_blocks(matrix, rows, capacity, groups):
    slots = pick(matrix, rows).reshape(EXPERTS, 1, capacity, -1)
    copies = jnp.broadcast_to(slots, (EXPERTS, groups, capacity, slots.shape[-1]))
    return copies.reshape(EXPERTS * groups, capacity, -1)


def fold_back(matrix, out, capacity, groups):
    out = out.reshape(EXPERTS, groups, capacity, -1)
    total = out[:, 0]
    for i in range(1, groups):
        total = total + out[:, i]
    return put(matrix, total.reshape(EXPERTS * capacity, -1))


def whole(shape):
    rank = len(shape)
    return pl.BlockSpec(shape, lambda *ids: (0,) * rank)


def plain_call(kernel, outs, args, scratch=(), flops=0):
    moved = sum(math.prod(a.shape) * 4 for a in args) + sum(math.prod(o) * 4 for o in outs)
    return pl.pallas_call(
        kernel,
        out_shape=[jax.ShapeDtypeStruct(o, F32) for o in outs],
        scratch_shapes=list(scratch),
        compiler_params=pltpu.CompilerParams(vmem_limit_bytes=PLAIN_BYTES),
        cost_estimate=pl.CostEstimate(flops=flops, bytes_accessed=moved, transcendentals=0),
    )(*args)


def halves(values):
    high = values.astype(BF16)
    return high, (values - high.astype(F32)).astype(BF16)


NN = (((1,), (0,)), ((), ()))
NT = (((1,), (1,)), ((), ()))
TN = (((0,), (0,)), ((), ()))


def dot3(left, right, dims=NN):
    left_high, left_low = left
    right_high, right_low = right
    return (
        lax.dot_general(left_high, right_high, dims, preferred_element_type=F32)
        + lax.dot_general(left_high, right_low, dims, preferred_element_type=F32)
        + lax.dot_general(left_low, right_high, dims, preferred_element_type=F32)
    )


def dot2(left, right, dims=NN):
    left_high, left_low = left
    return lax.dot_general(left_high, right, dims, preferred_element_type=F32) + lax.dot_general(
        left_low, right, dims, preferred_element_type=F32
    )


def rotated(values, cosine, sine, lane):
    ahead = pltpu.roll(values, LANES - HEAD // 2, 1)
    behind = pltpu.roll(values, HEAD // 2, 1)
    other = jnp.where(lane % HEAD < HEAD // 2, ahead, behind)
    return values * cosine + other * sine


def project_kernel(x_ref, gain_ref, weight_ref, cos_ref, sin_ref, q_ref, kv_ref):
    width = x_ref.shape[1]
    unit, _ = norm_stats(x_ref[...])
    hidden = halves(unit * gain_ref[...])
    lane = lax.broadcasted_iota(jnp.int32, (1, LANES), 1)
    cosine, sine = cos_ref[...], sin_ref[...]
    for part in range(3):
        out = dot3(hidden, halves(weight_ref[:, part * width : (part + 1) * width]))
        for first in range(0, width, LANES):
            piece = out[:, first : first + LANES]
            if part < 2:
                piece = rotated(piece, cosine, sine, lane)
            if part == 0:
                q_ref[:, first : first + LANES] = piece
            else:
                start = (part - 1) * width + first
                kv_ref[:, start : start + LANES] = piece


def one_head(values, head, lane):
    return jnp.where((lane < HEAD) == (head == 0), values, pltpu.roll(values, HEAD, 1))


def high_low(values):
    high = values.astype(BF16).astype(F32)
    return high, values - high


def query_side(values, extra, lane):
    high, low = high_low(values)
    return jnp.concatenate([high, jnp.where(lane < HEAD, low, extra)], axis=1).astype(BF16)


def key_side(values, extra, lane):
    high, low = high_low(values)
    first = jnp.where(lane < HEAD, high, low)
    return jnp.concatenate([first, jnp.where(lane < HEAD, high, extra)], axis=1).astype(BF16)


def both_parts(values, lane):
    high, low = high_low(values)
    return jnp.where(lane < HEAD, high, low).astype(BF16)


def in_parts(column, lane, first):
    high, rest = high_low(column)
    middle, low = high_low(rest)
    return jnp.where(
        lane == first,
        high,
        jnp.where(lane == first + 1, middle, jnp.where(lane == first + 2, low, 0.0)),
    )


def attention_kernel(
    members, near, q_ref, *refs,
):
    k_refs, v_refs, refs = refs[:near], refs[near : 2 * near], refs[2 * near :]
    (
        extra_ref, x_ref, out_weight_ref, gain_ref, in_weight_ref, live_ref, sent_ref, att_ref,
        lse_ref, x2_ref, glu_in_ref, glu_ref, landed_ref, att_all, *sems,
    ) = refs
    pair = pl.program_id(0)
    ring = Ring(sent_ref, landed_ref, members, 1, *sems)

    @pl.when(pair == 0)
    def _():
        greet(ring.peers)
        ring.start()

    rows = q_ref.shape[0]
    width = x_ref.shape[1]
    tile = min(256, rows)
    lane = lax.broadcasted_iota(jnp.int32, (1, LANES), 1)
    one_at = jnp.where(lane == HEAD, 1.0, 0.0).astype(F32)
    ones_column = jnp.where(lane == 0, 1.0, 0.0).astype(F32)
    keys = jnp.concatenate([k_ref[...] for k_ref in k_refs], axis=0)
    values = jnp.concatenate([v_ref[...] for v_ref in v_refs], axis=0)
    keys_count = keys.shape[0]
    outs = []
    for head in range(2):
        key_pack = key_side(one_head(keys, head, lane), extra_ref[...], lane)
        value_high, value_low = high_low(one_head(values, head, lane))
        value_pack = jnp.concatenate(
            [
                jnp.where(lane < HEAD, value_high, value_low),
                jnp.broadcast_to(ones_column, (keys_count, LANES)),
            ],
            axis=1,
        ).astype(BF16)
        per_tile = []
        for first in range(0, rows, tile):
            queries = one_head(q_ref[first : first + tile, :] * SCORE_SCALE, head, lane)
            query_pack = query_side(queries, one_at, lane)
            scores = lax.dot_general(query_pack, key_pack, NT, preferred_element_type=F32)
            top = jnp.max(scores, axis=1, keepdims=True)
            weights = halves(jnp.exp2(scores - top))
            summed = dot2(weights, value_pack)
            total = summed[:, LANES : LANES + 1]
            mixed = summed[:, :LANES]
            mixed = (mixed + pltpu.roll(mixed, HEAD, 1)) / total
            log_total = jnp.broadcast_to(top + jnp.log2(total), mixed.shape)
            per_tile.append((mixed, log_total))
        outs.append(per_tile)
    for index, first in enumerate(range(0, rows, tile)):
        (mixed_a, log_a), (mixed_b, log_b) = outs[0][index], outs[1][index]
        mixed = jnp.where(lane < HEAD, mixed_a, mixed_b)
        att_ref[first : first + tile, :] = mixed
        lse_ref[first : first + tile, :] = jnp.where(lane < HEAD, log_a, log_b)
        att_all[pair, first : first + tile, :] = mixed

    @pl.when(pair == pl.num_programs(0) - 1)
    def _():
        pairs = att_all.shape[0]
        attended = jnp.concatenate([att_all[i] for i in range(pairs)], axis=1)
        x2 = x_ref[...] + dot3(halves(attended), halves(out_weight_ref[...]))
        x2_ref[...] = x2
        unit, _ = norm_stats(x2)
        hidden = halves(unit * gain_ref[...])
        left = dot3(hidden, halves(in_weight_ref[:, :width]))
        right = dot3(hidden, halves(in_weight_ref[:, width:]))
        glu_in_ref[:, :width] = left
        glu_in_ref[:, width:] = right
        glu_ref[...] = left * jax.nn.sigmoid(right) * live_ref[...]
        ring.wait_receives()
        ring.wait_sends()


def attention_block(
    queries, key_values, extra, x1, out_weight, gain_row, in_weight, live, sent, collective_id
):
    rows, width = queries.shape
    near = len(key_values)
    pairs = width // LANES
    lanes_of = lambda height: pl.BlockSpec((height, LANES), lambda i: (0, i))
    values_of = pl.BlockSpec((rows, LANES), lambda i: (0, i + pairs))
    members = sent.shape[0]
    hbm = pl.BlockSpec(memory_space=pl.ANY)
    return pl.pallas_call(
        functools.partial(attention_kernel, members, near),
        grid=(pairs,),
        in_specs=[
            *[lanes_of(rows)] * (1 + near), *[values_of] * near, whole(extra.shape), whole(x1.shape),
            whole(out_weight.shape), whole(gain_row.shape), whole(in_weight.shape), whole(live.shape),
            hbm,
        ],
        out_specs=[
            lanes_of(rows), lanes_of(rows), whole((rows, width)), whole((rows, 2 * width)),
            whole((rows, width)), hbm,
        ],
        out_shape=[
            jax.ShapeDtypeStruct((rows, w), F32) for w in (width, width, width, 2 * width, width)
        ] + [jax.ShapeDtypeStruct(sent.shape, F32)],
        scratch_shapes=[pltpu.VMEM((pairs, rows, LANES), F32)] + ring_semaphores(members),
        compiler_params=pltpu.CompilerParams(
            collective_id=collective_id, has_side_effects=True, vmem_limit_bytes=VMEM_BYTES
        ),
        cost_estimate=pl.CostEstimate(
            flops=20_000_000_000, bytes_accessed=20_000_000, transcendentals=0
        ),
    )(
        queries, *key_values, *key_values, extra, x1, out_weight, gain_row, in_weight, live, sent
    )


def attention_back_kernel(
    members, near, q_ref, grad_ref, att_ref, lse_ref, *refs,
):
    k_refs, v_refs, refs = refs[:near], refs[near : 2 * near], refs[2 * near :]
    extra_ref, sent_ref, dqt_ref = refs[:3]
    dk_refs, dv_refs, refs = refs[3 : 3 + near], refs[3 + near : 3 + 2 * near], refs[3 + 2 * near :]
    landed_ref, packs, *sems = refs
    ring = Ring(sent_ref, landed_ref, members, 1, *sems)

    @pl.when(pl.program_id(0) == 0)
    def _():
        greet(ring.peers)
        ring.start()

    rows = q_ref.shape[0]
    count = k_refs[0].shape[0]
    tile = 256
    lane = lax.broadcasted_iota(jnp.int32, (1, LANES), 1)
    one_at = jnp.where(lane == HEAD, 1.0, 0.0).astype(F32)
    product = grad_ref[...] * att_ref[...]
    for head in range(2):
        mine = (lane < HEAD) == (head == 0)
        out_dot = jnp.sum(jnp.where(mine, product, 0.0), axis=1, keepdims=True)
        log_total = one_head(lse_ref[...], head, lane)
        queries = one_head(q_ref[...] * SCORE_SCALE, head, lane)
        grads = one_head(grad_ref[...], head, lane)
        query_pack = query_side(queries, one_at + in_parts(-log_total, lane, HEAD + 1), lane)
        dots = jnp.broadcast_to(-out_dot, grads.shape)
        grad_pack = query_side(grads, in_parts(dots, lane, HEAD + 1), lane)
        query_both = both_parts(queries, lane)
        grad_both = both_parts(grads, lane)
        packs[...] = jnp.zeros_like(packs)

        def step(part, index, carry):
            k_ref, v_ref, dk_ref, dv_ref = k_refs[part], v_refs[part], dk_refs[part], dv_refs[part]
            first = pl.multiple_of(index * tile, tile)
            extra = extra_ref[pl.ds(pl.multiple_of(part * count + first, tile), tile), :]
            keys = one_head(k_ref[pl.ds(first, tile), :], head, lane)
            values = one_head(v_ref[pl.ds(first, tile), :], head, lane)
            scores = lax.dot_general(
                key_side(keys, extra, lane), query_pack, NT, preferred_element_type=F32
            )
            prob = jnp.exp2(scores)
            score_grad = prob * lax.dot_general(
                key_side(values, extra, lane), grad_pack, NT, preferred_element_type=F32
            )
            value_grad = dot2(halves(prob), grad_both)
            parts = halves(score_grad)
            key_grad = dot2(parts, query_both) * math.log(2.0)
            value_grad = value_grad + pltpu.roll(value_grad, HEAD, 1)
            key_grad = key_grad + pltpu.roll(key_grad, HEAD, 1)
            if head == 0:
                dv_ref[pl.ds(first, tile), :] = value_grad
                dk_ref[pl.ds(first, tile), :] = key_grad
            else:
                dv_ref[pl.ds(first, tile), :] = jnp.where(
                    mine, value_grad, dv_ref[pl.ds(first, tile), :]
                )
                dk_ref[pl.ds(first, tile), :] = jnp.where(
                    mine, key_grad, dk_ref[pl.ds(first, tile), :]
                )
            key_both = both_parts(keys, lane)
            packs[...] += lax.dot_general(
                key_both, parts[0], TN, preferred_element_type=F32
            ) + lax.dot_general(key_both, parts[1], TN, preferred_element_type=F32)
            return carry

        for part in range(near):
            lax.fori_loop(0, count // tile, functools.partial(step, part), 0)
        dqt_ref[head * HEAD : (head + 1) * HEAD, :] = (
            packs[:HEAD, :] + packs[HEAD:, :]
        ) * HEAD ** (-0.5)

    @pl.when(pl.program_id(0) == pl.num_programs(0) - 1)
    def _():
        ring.wait_receives()
        ring.wait_sends()


def attention_back_block(
    queries, grad, attended, key_values, lse, extra, sent, collective_id
):
    rows, width = queries.shape
    near = len(key_values)
    pairs = width // LANES
    lanes_of = lambda height: pl.BlockSpec((height, LANES), lambda i: (0, i))
    values_of = pl.BlockSpec((rows, LANES), lambda i: (0, i + pairs))
    members = sent.shape[0]
    hbm = pl.BlockSpec(memory_space=pl.ANY)
    out = pl.pallas_call(
        functools.partial(attention_back_kernel, members, near),
        grid=(pairs,),
        in_specs=[
            *[lanes_of(rows)] * (4 + near), *[values_of] * near, whole(extra.shape), hbm,
        ],
        out_specs=[
            pl.BlockSpec((LANES, rows), lambda i: (i, 0)), *[lanes_of(rows)] * (2 * near), hbm,
        ],
        out_shape=[jax.ShapeDtypeStruct((width, rows), F32)]
        + [jax.ShapeDtypeStruct((rows, width), F32)] * (2 * near)
        + [jax.ShapeDtypeStruct(sent.shape, F32)],
        scratch_shapes=[pltpu.VMEM((LANES, rows), F32)] + ring_semaphores(members),
        compiler_params=pltpu.CompilerParams(
            collective_id=collective_id, has_side_effects=True, vmem_limit_bytes=VMEM_BYTES
        ),
        cost_estimate=pl.CostEstimate(
            flops=40_000_000_000, bytes_accessed=20_000_000, transcendentals=0
        ),
    )(queries, grad, attended, lse, *key_values, *key_values, extra, sent)
    return out[0], out[1 : 1 + near], out[1 + near : 1 + 2 * near], out[-1]


def project_back_kernel(near, dqt_ref, *refs):
    dk_refs, dv_refs, refs = refs[:near], refs[near : 2 * near], refs[2 * near :]
    (
        x_ref, gain_ref, weight_ref, cos_ref, sin_ref, upper_ref, dw_ref, gain_grad_ref, dx_ref,
    ) = refs
    width = x_ref.shape[1]
    unit, inverse = norm_stats(x_ref[...])
    gain_row = gain_ref[...]
    hidden = halves(unit * gain_row)
    lane = lax.broadcasted_iota(jnp.int32, (1, LANES), 1)
    cosine, sine = cos_ref[...], -sin_ref[...]
    hidden_grad = jnp.zeros(x_ref.shape, F32)
    for part in range(3):
        if part == 0:
            grad = dqt_ref[...].T
        else:
            pieces = dk_refs if part == 1 else dv_refs
            grad = pieces[0][...]
            for piece in pieces[1:]:
                grad = grad + piece[...]
        if part < 2:
            grad = jnp.concatenate(
                [
                    rotated(grad[:, i : i + LANES], cosine, sine, lane)
                    for i in range(0, width, LANES)
                ],
                axis=1,
            )
        grad = halves(grad)
        dw_ref[:, part * width : (part + 1) * width] = dot3(hidden, grad, TN)
        hidden_grad += dot3(grad, halves(weight_ref[:, part * width : (part + 1) * width]), NT)
    gain_grad_ref[...] = jnp.sum(hidden_grad * unit, axis=0, keepdims=True)
    dx_ref[...] = upper_ref[...] + norm_back(hidden_grad, gain_row, unit, inverse)


RIM = 8


def glu_back_kernel(
    dglu_ref, glu_in_ref, x2_ref, gain_ref, in_weight_ref, grad_ref, att_ref, out_weight_ref,
    dw_in_ref, gain_grad_ref, dx2_ref, dw_out_ref, datt_ref,
):
    width = x2_ref.shape[1]
    unit, inverse = norm_stats(x2_ref[...])
    gain_row = gain_ref[...]
    hidden = halves(unit * gain_row)
    dglu = dglu_ref[...]
    left, gate = glu_in_ref[:, :width], jax.nn.sigmoid(glu_in_ref[:, width:])
    left_grad = halves(dglu * gate)
    right_grad = halves(dglu * left * gate * (1.0 - gate))
    dw_in_ref[:, :width] = dot3(hidden, left_grad, TN)
    dw_in_ref[:, width:] = dot3(hidden, right_grad, TN)
    hidden_grad = dot3(left_grad, halves(in_weight_ref[:, :width]), NT) + dot3(
        right_grad, halves(in_weight_ref[:, width:]), NT
    )
    gain_grad_ref[...] = jnp.sum(hidden_grad * unit, axis=0, keepdims=True)
    dx2 = grad_ref[...] + norm_back(hidden_grad, gain_row, unit, inverse)
    dx2_ref[...] = dx2
    dx2 = halves(dx2)
    dw_out_ref[...] = dot3(halves(att_ref[...]), dx2, TN)
    datt_ref[...] = dot3(dx2, halves(out_weight_ref[...]), NT)


def side_by_side(values):
    high, low = halves(values)
    return jnp.concatenate([high, high, low], axis=1)


def one_below_other(values):
    high, low = halves(values)
    return jnp.concatenate([high, low, high], axis=0)


def product(left, right):
    return lax.dot_general(left, right, NN, preferred_element_type=F32)


class ExpertGrads:
    def __init__(self, inward_ref, outward_ref, ids, refs):
        self.inward_ref, self.outward_ref, self.ids = inward_ref, outward_ref, ids
        (
            self.w1t3, self.w23, self.ht3, self.gt3, self.h3, self.g3, self.dw1t, self.dw2,
            self.stage_one, self.stage_two, self.sems,
        ) = refs
        self.chunk = self.stage_one.shape[-1]
        self.count = len(ids)

    @staticmethod
    def scratch(width, chunk, count, rows):
        hidden = chunk * count
        return [
            pltpu.VMEM((hidden, 3 * width), BF16), pltpu.VMEM((hidden, 3 * width), BF16),
            pltpu.VMEM((3 * width, rows), BF16), pltpu.VMEM((3 * width, rows), BF16),
            pltpu.VMEM((3 * rows, width), BF16), pltpu.VMEM((3 * rows, width), BF16),
            pltpu.VMEM((hidden, width), F32), pltpu.VMEM((hidden, width), F32),
            pltpu.VMEM((2, width, chunk), F32), pltpu.VMEM((chunk, width), F32),
            pltpu.SemaphoreType.DMA((5,)),
        ]

    def part_of(self, index):
        return pl.ds(pl.multiple_of(self.ids[index] * self.chunk, self.chunk), self.chunk)

    def load_one(self, index):
        slot = index % 2
        return pltpu.make_async_copy(
            self.inward_ref.at[:, self.part_of(index)], self.stage_one.at[slot], self.sems.at[slot]
        )

    def load_two(self, index):
        return pltpu.make_async_copy(
            self.outward_ref.at[self.part_of(index), :], self.stage_two, self.sems.at[2]
        )

    def start_weights(self):
        self.load_one(0).start()
        self.load_two(0).start()

    def finish_weights(self):
        for index in range(self.count):
            more = index + 1 < self.count
            if more:
                self.load_one(index + 1).start()
            part = pl.ds(index * self.chunk, self.chunk)
            self.load_two(index).wait()
            self.w23[part, :] = side_by_side(self.stage_two[...])
            if more:
                self.load_two(index + 1).start()
            self.load_one(index).wait()
            self.w1t3[part, :] = side_by_side(self.stage_one[index % 2].T)

    def block(self, hidden, out_grad, first, hidden_grad=None, middle=None):
        width = hidden.shape[1]
        self.ht3[...] = one_below_other(hidden.T)
        self.gt3[...] = one_below_other(out_grad.T)
        self.h3[...] = one_below_other(hidden)
        self.g3[...] = one_below_other(out_grad)
        if hidden_grad is not None:
            hidden_grad[...] = jnp.zeros_like(hidden_grad)

        steps = self.count // 2 if self.count % 2 == 0 and self.chunk > 256 else self.count
        span = self.count * self.chunk // steps

        def step(index, carry):
            part = pl.ds(pl.multiple_of(index * span, span), span)
            weights = self.w1t3[part, :]
            pre = product(weights, self.ht3[...])
            gates = jax.nn.sigmoid(pre)
            two = product(side_by_side(pre * gates), self.g3[...])
            slope = gates * (1.0 + pre * (1.0 - gates))
            pre_grad = product(self.w23[part, :], self.gt3[...]) * slope
            one = product(side_by_side(pre_grad), self.h3[...])
            if first:
                self.dw2[part, :] = two
                self.dw1t[part, :] = one
            else:
                self.dw2[part, :] += two
                self.dw1t[part, :] += one
            if hidden_grad is not None:
                hidden_grad[...] += dot3(
                    halves(pre_grad), (weights[:, :width], weights[:, 2 * width :]), TN
                )
            return carry

        half = steps // 2 if middle is not None else 0
        if middle is not None:
            lax.fori_loop(0, half, step, 0)
            middle()
        lax.fori_loop(half, steps, step, 0)

    def store(self, dw1_of, dw2_of):
        pending = [[], []]
        for index in range(self.count):
            slot = index % 2
            for copy in pending[slot]:
                copy.wait()
            part = pl.ds(index * self.chunk, self.chunk)
            self.stage_one[slot] = self.dw1t[part, :].T
            pending[slot] = [
                pltpu.make_async_copy(
                    self.stage_one.at[slot], dw1_of(index), self.sems.at[2 * slot]
                ),
                pltpu.make_async_copy(
                    self.dw2.at[part, :], dw2_of(index), self.sems.at[2 * slot + 1]
                ),
            ]
            for copy in pending[slot]:
                copy.start()
        for copy in pending[0] + pending[1]:
            copy.wait()


class SmallSum:
    def __init__(self, rows, columns, refs):
        self.rows, self.columns = rows, columns
        self.row_buf, self.col_buf, *self.sems = refs
        b, s = lax.axis_index("batch"), lax.axis_index("seq")
        self.place = (b, s)
        self.row_peers = [(lax.rem(b + off, rows), s) for off in range(1, rows)]
        self.col_peers = [(b, lax.rem(s + off, columns)) for off in range(1, columns)]

    @staticmethod
    def scratch(rows, columns, shape):
        dma = pltpu.SemaphoreType.DMA
        return [
            pltpu.VMEM((rows,) + shape, F32), pltpu.VMEM((columns,) + shape, F32),
            dma((rows,)), dma((rows,)), dma((columns,)), dma((columns,)),
        ]

    def share(self, value, axis):
        buf, peers = (self.row_buf, self.row_peers) if axis == 0 else (self.col_buf, self.col_peers)
        send, recv = self.sems[2 * axis : 2 * axis + 2]
        mine = self.place[axis]
        buf[mine] = value
        self.copies = [
            remote(buf.at[mine], buf.at[mine], send.at[i], recv.at[mine], peer)
            for i, peer in enumerate(peers)
        ]
        for copy in self.copies:
            copy.start()

    def total(self, axis):
        buf, peers = (self.row_buf, self.row_peers) if axis == 0 else (self.col_buf, self.col_peers)
        send, recv = self.sems[2 * axis : 2 * axis + 2]
        for i, peer in enumerate(peers):
            other = peer[axis]
            remote(buf.at[other], buf.at[other], send.at[i], recv.at[other], peer).wait_recv()
        for copy in self.copies:
            copy.wait_send()
        total = buf[0]
        for i in range(1, buf.shape[0]):
            total = total + buf[i]
        return total


class Rims:
    def __init__(self, blocks_ref, step, refs):
        self.from_before, self.from_after, send, recv = refs
        b, s = lax.axis_index("batch"), lax.axis_index("seq")
        self.low, self.step = lax.rem(s, step), step
        base, rows = s - self.low, blocks_ref.shape[1]
        after = (b, base + lax.rem(self.low + 1, step))
        before = (b, base + lax.rem(self.low + step - 1, step))
        self.copies = [
            remote(
                blocks_ref.at[:, pl.ds(rows - RIM, RIM), :], self.from_before, send.at[0],
                recv.at[0], after,
            ),
            remote(
                blocks_ref.at[:, pl.ds(0, RIM), :], self.from_after, send.at[1], recv.at[1], before
            ),
        ]

    @staticmethod
    def scratch(parts, width):
        dma = pltpu.SemaphoreType.DMA
        return [
            pltpu.VMEM((parts, RIM, width), F32), pltpu.VMEM((parts, RIM, width), F32), dma((2,)),
            dma((2,)),
        ]

    def start(self):
        for copy in self.copies:
            copy.start()

    def finish(self):
        for copy in self.copies:
            copy.wait()
        before, after = self.from_before[...], self.from_after[...]
        none = jnp.zeros_like(before[:1])
        first, last = cast_one(self.low == 0), cast_one(self.low == self.step - 1)
        before_edge = jnp.concatenate([none, before[:-1]], axis=0)
        after_edge = jnp.concatenate([after[1:], none], axis=0)
        return (
            first * before_edge + (1.0 - first) * before,
            last * after_edge + (1.0 - last) * after,
        )


def cast_one(flag):
    return jnp.where(flag, 1.0, 0.0).astype(F32)


def pad_blocks(pad_ref, before, block_ref, after):
    rows = block_ref.shape[1]
    pad_ref[:, :RIM, :] = before
    pad_ref[:, RIM : RIM + rows, :] = block_ref[...]
    pad_ref[:, RIM + rows :, :] = after


def conv_stats(sums):
    count = sums[2:3]
    averaged = sums[0:1] / count
    return count, averaged, sums[1:2] / count - averaged * averaged


def conv_chain_kernel(
    step, row_count, columns, glu_ref, taps_ref, live_ref, gain_ref, bias_ref, weight_ref, x2_ref,
    sent_ref, conv_ref, sums_ref, x3_ref, before_ref, after_ref, landed_ref, pad_ref, mine, *refs,
):
    parts, rows, width = glu_ref.shape
    rims = Rims(glu_ref, step, refs[:4])
    small = SmallSum(row_count, columns, refs[4:10])
    ring = Ring(sent_ref, landed_ref, columns, 1, *refs[10:])
    greet(small.row_peers + small.col_peers)
    rims.start()
    ring.start()
    before, after = rims.finish()
    before_ref[...] = before
    after_ref[...] = after
    pad_blocks(pad_ref, before, glu_ref, after)
    mine[...] = jnp.zeros_like(mine)

    def part_step(part, carry):
        alive = live_ref[part]
        for first in range(0, width, LANES):
            columns_here = slice(first, first + LANES)
            total = jnp.zeros((rows, LANES), F32)
            for tap in range(KERNEL):
                total = total + pad_ref[part, 1 + tap : 1 + tap + rows, columns_here] * taps_ref[
                    tap : tap + 1, columns_here
                ]
            conv_ref[part, :, columns_here] = total
            kept = alive * total
            mine[0:1, columns_here] += jnp.sum(kept, axis=0, keepdims=True)
            mine[1:2, columns_here] += jnp.sum(kept * total, axis=0, keepdims=True)
            mine[2:3, columns_here] += jnp.sum(
                jnp.broadcast_to(alive, (rows, LANES)), axis=0, keepdims=True
            )
        return carry

    lax.fori_loop(0, parts, part_step, 0)
    small.share(mine[...], 0)
    small.share(small.total(0), 1)
    weight = halves(weight_ref[...])
    sums = small.total(1)
    sums_ref[...] = sums
    count, averaged, variance = conv_stats(sums)
    scale = lax.rsqrt(variance + EPSILON)
    conv = conv_ref[...].reshape(parts * rows, width)
    normed = (conv - averaged) * scale * gain_ref[...] + bias_ref[...]
    x3_ref[...] = x2_ref[...] + dot3(halves(swish(normed)), weight)
    ring.wait_receives()
    ring.wait_sends()


def conv_chain_back_kernel(
    step, row_count, columns, grad_ref, conv_ref, sums_ref, gain_ref, bias_ref, weight_ref,
    taps_ref, live_ref, glu_ref, glu_before_ref, glu_after_ref, dw_ref, out_sums_ref,
    taps_grad_ref, dglu_ref, pad_ref, glu_pad_ref, tap_sums, conv_grad, mine, *refs,
):
    parts, rows, width = glu_ref.shape
    rims = Rims(conv_grad, step, refs[:4])
    small = SmallSum(row_count, columns, refs[4:])
    greet(small.row_peers + small.col_peers)
    count, averaged, variance = conv_stats(sums_ref[...])
    scale = lax.rsqrt(variance + EPSILON)
    conv = conv_ref[...].reshape(parts * rows, width)
    unit = (conv - averaged) * scale
    gain_row = gain_ref[...]
    normed = unit * gain_row + bias_ref[...]
    grad = halves(grad_ref[...])
    normed_grad = dot3(grad, halves(weight_ref[...]), NT) * swish_slope(normed)
    mine[...] = jnp.zeros_like(mine)
    mine[0:1, :] = jnp.sum(normed_grad * unit, axis=0, keepdims=True)
    mine[1:2, :] = jnp.sum(normed_grad, axis=0, keepdims=True)
    small.share(mine[...], 0)
    dw_ref[...] = dot3(halves(swish(normed)), grad, TN)
    small.share(small.total(0), 1)
    pad_blocks(glu_pad_ref, glu_before_ref[...], glu_ref, glu_after_ref[...])
    tap_sums[...] = jnp.zeros_like(tap_sums)
    sums = small.total(1)
    out_sums_ref[...] = sums
    mean_grad = -scale * gain_row * sums[1:2]
    var_grad = -0.5 * scale * scale * gain_row * sums[0:1]
    fixed = (mean_grad - 2.0 * averaged * var_grad) / count
    slope = 2.0 * var_grad / count
    direct = (scale * gain_row * normed_grad).reshape(parts, rows, width)
    conv_grad[...] = direct + live_ref[...] * (
        fixed.reshape(1, 1, width) + conv_ref[...] * slope.reshape(1, 1, width)
    )
    rims.start()
    before, after = rims.finish()
    pad_blocks(pad_ref, before, conv_grad, after)

    def part_step(part, carry):
        alive = live_ref[part]
        for first in range(0, width, LANES):
            columns_here = slice(first, first + LANES)
            total = jnp.zeros((rows, LANES), F32)
            here = conv_grad[part, :, columns_here]
            for tap in range(KERNEL):
                start = KERNEL - tap
                total = total + pad_ref[part, start : start + rows, columns_here] * taps_ref[
                    tap : tap + 1, columns_here
                ]
                product_here = glu_pad_ref[part, 1 + tap : 1 + tap + rows, columns_here] * here
                tap_sums[tap, :, columns_here] += jnp.sum(
                    product_here.reshape(rows // 8, 8, LANES), axis=0
                )
            dglu_ref[part, :, columns_here] = total * alive
        return carry

    lax.fori_loop(0, parts, part_step, 0)
    for tap in range(KERNEL):
        taps_grad_ref[tap : tap + 1, :] = jnp.sum(tap_sums[tap], axis=0, keepdims=True)


def conv_chain(back, step, outs, args, extra_scratch, collective_id, ring=False):
    row_count, columns = lax.axis_size("batch"), lax.axis_size("seq")
    parts, rows, width = outs[0] if not back else outs[3]
    vmem, hbm = pl.BlockSpec(memory_space=pltpu.VMEM), pl.BlockSpec(memory_space=pl.ANY)
    padded = pltpu.VMEM((parts, rows + 2 * RIM, width), F32)
    scratch = [padded] * (2 if back else 1) + list(extra_scratch) + [pltpu.VMEM((8, width), F32)]
    scratch += Rims.scratch(parts, width) + SmallSum.scratch(row_count, columns, (8, width))
    if ring:
        scratch += ring_semaphores(columns)
    kernel = conv_chain_back_kernel if back else conv_chain_kernel
    hidden_last = [hbm] if ring else []
    return pl.pallas_call(
        functools.partial(kernel, step, row_count, columns),
        in_specs=[vmem] * (len(args) - len(hidden_last)) + hidden_last,
        out_specs=[vmem] * (len(outs) - len(hidden_last)) + hidden_last,
        out_shape=[jax.ShapeDtypeStruct(shape, F32) for shape in outs],
        scratch_shapes=scratch,
        compiler_params=pltpu.CompilerParams(
            collective_id=collective_id, has_side_effects=True, vmem_limit_bytes=PLAIN_BYTES
        ),
        cost_estimate=pl.CostEstimate(
            flops=2_000_000_000, bytes_accessed=30_000_000, transcendentals=0
        ),
    )(*args)


class Places:
    def __init__(self):
        b, s = lax.axis_index("batch"), lax.axis_index("seq")
        self.x, self.y, self.z, self.c = lax.rem(b, 2), b // 2, s // 2, lax.rem(s, 2)
        self.near = (b, s + 1 - 2 * self.c)
        self.across_x = (b + 1 - 2 * self.x, s)
        self.across_y = (b + 2 - 4 * self.y, s)
        self.line = [lax.rem(self.z + k, 4) for k in range(1, 4)]
        self.line_peers = [(b, other * 2 + self.c) for other in self.line]


def cut_of(width):
    cut = width // 256 * 128
    return pl.ds(0, cut), pl.ds(cut, width - cut)


class DenseScatter:
    def __init__(self, pieces, out_ref, refs):
        self.pieces, self.out_ref = pieces, out_ref
        self.buf0, self.buf1, self.buf2, self.acc0, self.acc1, self.send, self.recv, self.loads = refs

    @staticmethod
    def scratch(rows, width, pieces):
        block = lambda parts: pltpu.VMEM((rows // parts, width), F32)
        dma = pltpu.SemaphoreType.DMA
        return [
            block(2), block(4), block(8), block(2), block(4), dma((pieces + 4,)), dma((pieces + 4,)),
            dma((pieces,)),
        ]

    def start_cores(self):
        at = Places()
        half = self.buf0.shape[0]
        first = 0
        self.copies, self.local = [], []
        for i, piece in enumerate(self.pieces):
            columns = pl.ds(first, piece.shape[1])
            first += piece.shape[1]
            self.copies.append(
                remote(
                    piece.at[pl.ds((1 - at.c) * half, half), :], self.buf0.at[:, columns],
                    self.send.at[i], self.recv.at[i], at.near,
                )
            )
            self.local.append(
                pltpu.make_async_copy(
                    piece.at[pl.ds(at.c * half, half), :], self.acc0.at[:, columns],
                    self.loads.at[i],
                )
            )
        for copy in self.copies + self.local:
            copy.start()

    def start_first(self):
        for copy in self.copies + self.local:
            copy.wait()
        self.acc0[...] += self.buf0[...]
        at = Places()
        left, right = cut_of(self.acc0.shape[1])
        size, sem = self.buf1.shape[0], len(self.pieces)
        self.copies = [
            remote(
                self.acc0.at[pl.ds((1 - at.x) * size, size), left], self.buf1.at[:, left],
                self.send.at[sem], self.recv.at[sem], at.across_x,
            ),
            remote(
                self.acc0.at[pl.ds((1 - at.y) * size, size), right], self.buf1.at[:, right],
                self.send.at[sem + 1], self.recv.at[sem + 1], at.across_y,
            ),
        ]
        for copy in self.copies:
            copy.start()

    def start_second(self):
        for copy in self.copies:
            copy.wait()
        at = Places()
        left, right = cut_of(self.acc0.shape[1])
        size = self.buf1.shape[0]
        self.acc1[:, left] = self.acc0[pl.ds(at.x * size, size), left] + self.buf1[:, left]
        self.acc1[:, right] = self.acc0[pl.ds(at.y * size, size), right] + self.buf1[:, right]
        size, sem = self.buf2.shape[0], len(self.pieces) + 2
        self.copies = [
            remote(
                self.acc1.at[pl.ds((1 - at.y) * size, size), left], self.buf2.at[:, left],
                self.send.at[sem], self.recv.at[sem], at.across_y,
            ),
            remote(
                self.acc1.at[pl.ds((1 - at.x) * size, size), right], self.buf2.at[:, right],
                self.send.at[sem + 1], self.recv.at[sem + 1], at.across_x,
            ),
        ]
        for copy in self.copies:
            copy.start()

    def finish(self):
        for copy in self.copies:
            copy.wait()
        at = Places()
        left, right = cut_of(self.acc0.shape[1])
        size = self.buf2.shape[0]
        self.out_ref[:, left] = self.acc1[pl.ds(at.y * size, size), left] + self.buf2[:, left]
        self.out_ref[:, right] = self.acc1[pl.ds(at.x * size, size), right] + self.buf2[:, right]


class DenseGather:
    def __init__(self, a_ref, outs, refs):
        self.a_ref, self.outs = a_ref, outs
        (
            self.bufs, self.mine, self.eighth, self.acc1, self.acc0, self.send, self.recv,
            self.send_two, self.recv_two, self.send_three, self.recv_three, self.stores,
        ) = refs

    @staticmethod
    def scratch(rows, width, pieces):
        block = lambda parts: pltpu.VMEM((rows // parts, width), F32)
        dma = pltpu.SemaphoreType.DMA
        return [
            pltpu.VMEM((4, rows // 32, width), F32), block(32), block(8), block(4), block(2),
            dma((3,)), dma((4,)), dma((3,)), dma((4,)), dma((pieces + 4,)), dma((pieces + 4,)),
            dma((pieces,)),
        ]

    def start_line(self):
        at = Places()
        part = self.mine.shape[0]
        self.sends = [
            remote(
                self.a_ref.at[pl.ds(other * part, part), :], self.bufs.at[at.z],
                self.send.at[i], self.recv.at[at.z], at.line_peers[i],
            )
            for i, other in enumerate(at.line)
        ]
        for copy in self.sends:
            copy.start()
        self.bufs[at.z] = self.a_ref[pl.ds(at.z * part, part), :]

    def start_line_back(self):
        at = Places()
        part = self.mine.shape[0]
        for i, other in enumerate(at.line):
            remote(
                self.bufs.at[other], self.bufs.at[other], self.send.at[i], self.recv.at[other],
                at.line_peers[i],
            ).wait_recv()
        self.mine[...] = (self.bufs[0] + self.bufs[1]) + (self.bufs[2] + self.bufs[3])
        spread = [
            remote(
                self.mine, self.eighth.at[pl.ds(at.z * part, part), :], self.send_two.at[i],
                self.recv_two.at[at.z], at.line_peers[i],
            )
            for i, other in enumerate(at.line)
        ]
        for copy in spread:
            copy.start()
        self.sends += spread
        self.eighth[pl.ds(at.z * part, part), :] = self.mine[...]

    def swap(self, index, src, dst, mine, columns, peer):
        size = src.shape[0]
        out = remote(
            src.at[:, columns], dst.at[pl.ds(mine * size, size), columns],
            self.send_three.at[index], self.recv_three.at[index], peer,
        )
        out.start()
        dst[pl.ds(mine * size, size), columns] = src[:, columns]
        self.sends.append(out)
        return remote(
            src.at[:, columns], dst.at[pl.ds((1 - mine) * size, size), columns],
            self.send_three.at[index], self.recv_three.at[index], peer,
        )

    def start_first(self):
        at = Places()
        part = self.mine.shape[0]
        for i, other in enumerate(at.line):
            remote(
                self.mine, self.eighth.at[pl.ds(other * part, part), :], self.send_two.at[i],
                self.recv_two.at[other], at.line_peers[i],
            ).wait_recv()
        left, right = cut_of(self.eighth.shape[1])
        self.awaited = [
            self.swap(0, self.eighth, self.acc1, at.y, left, at.across_y),
            self.swap(1, self.eighth, self.acc1, at.x, right, at.across_x),
        ]

    def start_second(self):
        for copy in self.awaited:
            copy.wait_recv()
        at = Places()
        left, right = cut_of(self.eighth.shape[1])
        self.awaited = [
            self.swap(2, self.acc1, self.acc0, at.x, left, at.across_x),
            self.swap(3, self.acc1, self.acc0, at.y, right, at.across_y),
        ]

    def start_cores(self):
        for copy in self.awaited:
            copy.wait_recv()
        at = Places()
        half = self.acc0.shape[0]
        self.awaited, self.local = [], []
        first = 0
        for i, out in enumerate(self.outs):
            columns = pl.ds(first, out.shape[1])
            first += out.shape[1]
            rows, other_rows = pl.ds(at.c * half, half), pl.ds((1 - at.c) * half, half)
            index = 4 + i
            copy = remote(
                self.acc0.at[:, columns], out.at[rows, :], self.send_three.at[index],
                self.recv_three.at[index], at.near,
            )
            copy.start()
            self.sends.append(copy)
            self.awaited.append(
                remote(
                    self.acc0.at[:, columns], out.at[other_rows, :], self.send_three.at[index],
                    self.recv_three.at[index], at.near,
                )
            )
            store = pltpu.make_async_copy(
                self.acc0.at[:, columns], out.at[rows, :], self.stores.at[i]
            )
            store.start()
            self.local.append(store)

    def finish(self):
        for copy in self.awaited:
            copy.wait_recv()
        for copy in self.local:
            copy.wait()
        for copy in self.sends:
            copy.wait_send()


class Expert:
    def __init__(self, inward_ref, outward_ref, refs):
        self.inward_ref, self.outward_ref = inward_ref, outward_ref
        self.w13, self.w23, self.stage_one, self.stage_two, self.pre, self.sems = refs
        self.chunk = self.stage_one.shape[-1]
        self.count = self.w23.shape[0]

    @staticmethod
    def scratch(width, hidden, rows):
        chunk = min(512, hidden)
        count = hidden // chunk
        return [
            pltpu.VMEM((count, 3 * width, chunk), BF16), pltpu.VMEM((count, 3 * chunk, width), BF16),
            pltpu.VMEM((2, width, chunk), F32), pltpu.VMEM((2, chunk, width), F32),
            pltpu.VMEM((count, rows, chunk), F32), pltpu.SemaphoreType.DMA((4,)),
        ]

    def load(self, index):
        part, slot = pl.ds(index * self.chunk, self.chunk), index % 2
        return [
            pltpu.make_async_copy(
                self.inward_ref.at[:, part], self.stage_one.at[slot], self.sems.at[2 * slot]
            ),
            pltpu.make_async_copy(
                self.outward_ref.at[part, :], self.stage_two.at[slot], self.sems.at[2 * slot + 1]
            ),
        ]

    def start_weights(self):
        for copy in self.load(0):
            copy.start()

    def finish_weights(self):
        for index in range(self.count):
            if index + 1 < self.count:
                for copy in self.load(index + 1):
                    copy.start()
            for copy in self.load(index):
                copy.wait()
            self.w13[index] = one_below_other(self.stage_one[index % 2])
            self.w23[index] = one_below_other(self.stage_two[index % 2])

    def forward(self, hidden, out_ref):
        wide = side_by_side(hidden)
        out_ref[...] = jnp.zeros_like(out_ref)

        def step(index, carry):
            pre = product(wide, self.w13[index])
            self.pre[index] = pre
            out_ref[...] += product(side_by_side(swish(pre)), self.w23[index])
            return carry

        lax.fori_loop(0, self.count, step, 0)

    def backward(self, out_grad, hidden_grad):
        width = out_grad.shape[1]
        parts = halves(out_grad)
        hidden_grad[...] = jnp.zeros_like(hidden_grad)

        def step(index, carry):
            outward = self.w23[index]
            outward = outward[: self.chunk], outward[self.chunk : 2 * self.chunk]
            inward = self.w13[index]
            inward = inward[:width], inward[width : 2 * width]
            pre_grad = dot3(parts, outward, NT) * swish_slope(self.pre[index])
            hidden_grad[...] += dot3(halves(pre_grad), inward, NT)
            return carry

        lax.fori_loop(0, self.count, step, 0)


def pick_slots(slots, rows, sent, members):
    high, low = halves(rows)
    picked = product(slots, high) + product(slots, low)
    picked = picked.reshape(EXPERTS, sent.shape[1], rows.shape[1])
    groups = members // EXPERTS
    for expert in range(EXPERTS):
        for copy in range(groups):
            sent[expert * groups + copy] = picked[expert]


def put_slots(slots, returned, members):
    groups = members // EXPERTS
    pieces = []
    for expert in range(EXPERTS):
        piece = returned[expert * groups]
        for copy in range(1, groups):
            piece = piece + returned[expert * groups + copy]
        pieces.append(piece)
    high, low = halves(jnp.concatenate(pieces, axis=0))
    return lax.dot_general(slots, high, TN, preferred_element_type=F32) + lax.dot_general(
        slots, low, TN, preferred_element_type=F32
    )


def gate_of(hidden, router, off, chosen):
    logits = dot3(halves(hidden), router) + off
    weights = jnp.exp(logits - jnp.max(logits, axis=1, keepdims=True))
    prob = weights / jnp.sum(weights, axis=1, keepdims=True)
    return prob, jnp.sum(prob * chosen, axis=1, keepdims=True)


def mixture_kernel(
    members, parts, row_blocks, frames_ref, slots_ref, gain_ref, router_ref, off_ref, chosen_ref,
    inward_ref, outward_ref, out_ref, landed_ref, gate_ref, prob_ref, branch_ref, hidden_all_ref,
    sent, returned, hidden_sent, section, *rest,
):
    expert = Expert(inward_ref.at[0], outward_ref.at[0], rest[:6])
    seq_sems, back_sems, frame_sems, spread_sems = rest[6:9], rest[9:12], rest[12:15], rest[15:]
    step = members // parts
    to_experts = Ring(sent, landed_ref, members, 1, *seq_sems)
    back = Ring(sent, returned, members, 1, *back_sems)
    to_utterances = Ring(section, out_ref, parts, step, *frame_sems)
    spread = Spread(hidden_sent, hidden_all_ref, *spread_sems)
    expert.start_weights()
    pick_slots(slots_ref[...], frames_ref[...], sent, members)
    greet(to_experts.peers + spread.peers)
    to_experts.start()
    expert.finish_weights()
    to_experts.wait_receives()
    to_experts.wait_sends()
    rows = landed_ref[...].reshape(branch_ref.shape)
    unit, _ = norm_stats(rows)
    hidden = unit * gain_ref[...]
    hidden_sent[...] = hidden
    expert.forward(hidden, branch_ref)
    prob, gate = gate_of(hidden, halves(router_ref[...]), off_ref[...], chosen_ref[...])
    prob_ref[...] = prob
    gate_ref[...] = gate
    sent[...] = (0.5 * gate * branch_ref[...]).reshape(sent.shape)
    back.start()
    spread.start()
    back.wait_receives()
    spread.forward()
    x1 = frames_ref[...] + put_slots(slots_ref[...], returned, members)
    section[...] = x1.reshape(section.shape)
    to_utterances.start()
    to_utterances.wait_receives()
    spread.wait_receives()
    back.wait_sends()
    to_utterances.wait_sends()
    spread.wait_sends()


def mixture_block(
    frames, slots, gain_row, router, off, chosen, expert_in, expert_out, parts, capacity,
    collective_id,
):
    members, row_blocks = lax.axis_size("seq"), lax.axis_size("batch")
    rows, width = frames.shape
    count = members * capacity
    vmem = pl.BlockSpec(memory_space=pltpu.VMEM)
    hbm = pl.BlockSpec(memory_space=pl.ANY)
    dma = pltpu.SemaphoreType.DMA
    blocks = (parts, rows // parts, width)
    slot_blocks_shape = (members, capacity, width)
    outs = [
        blocks, slot_blocks_shape, (count, 1), (count, LANES), (count, width),
        (row_blocks, count, width),
    ]
    return pl.pallas_call(
        functools.partial(mixture_kernel, members, parts, row_blocks),
        in_specs=[vmem] * 6 + [hbm] * 2,
        out_specs=[vmem] * 5 + [hbm],
        out_shape=[jax.ShapeDtypeStruct(shape, F32) for shape in outs],
        scratch_shapes=[
            pltpu.VMEM(slot_blocks_shape, F32), pltpu.VMEM(slot_blocks_shape, F32),
            pltpu.VMEM((count, width), F32), pltpu.VMEM(blocks, F32),
        ]
        + Expert.scratch(width, expert_in.shape[2], count)
        + ring_semaphores(members)
        + ring_semaphores(members)
        + ring_semaphores(parts)
        + Spread.semaphores(),
        compiler_params=pltpu.CompilerParams(
            collective_id=collective_id, has_side_effects=True, vmem_limit_bytes=VMEM_BYTES
        ),
        cost_estimate=pl.CostEstimate(
            flops=60_000_000_000, bytes_accessed=20_000_000, transcendentals=0
        ),
    )(frames, slots, gain_row, router, off, chosen, expert_in, expert_out)


def mixture_both_kernel(
    members, parts, row_blocks, blocks_ref, slots_ref, drop_ref, grad_ref, grad_rows_a, grad_rows_b,
    gain_ref,
    last_gain_ref, router_ref, off_ref, chosen_ref, inward_ref, outward_ref, out_ref, plain_ref,
    last_rows_ref, hidden_all_ref, out_grad_all_ref, router_grad_ref, gain_grad_ref,
    last_gain_grad_ref, section, sent, landed, returned, hidden_sent, grad_sent, branch,
    hidden_grad, local, *rest,
):
    groups = members // EXPERTS
    expert = Expert(inward_ref.at[1], outward_ref.at[1], rest[:6])
    rest = rest[6:]
    in_sems, seq_sems, back_sems, out_sems = (rest[3 * i : 3 * i + 3] for i in range(4))
    spread_sems, grad_sems, rest = rest[12:15], rest[15:18], rest[18:]
    step = members // parts
    b, s = lax.axis_index("batch"), lax.axis_index("seq")
    to_frames = Ring(blocks_ref, section, parts, step, *in_sems)
    to_experts = Ring(sent, landed, members, 1, *seq_sems)
    back = Ring(sent, returned, members, 1, *back_sems)
    to_utterances = Ring(section, out_ref, parts, step, *out_sems)
    spread = Spread(hidden_sent, hidden_all_ref, *spread_sems)
    grad_spread = Spread(grad_sent, out_grad_all_ref, *grad_sems)
    greet(to_experts.peers + spread.peers)
    to_frames.start()
    expert.start_weights()
    expert.finish_weights()
    to_frames.wait_receives()
    x3 = section[...].reshape(plain_ref.shape)
    pick_slots(slots_ref[...], x3, sent, members)
    to_experts.start()
    drop = drop_ref[...]
    last_gain = last_gain_ref[...]
    out_grad = grad_ref[...]
    unit, inverse = norm_stats(x3)
    plain_ref[...] = drop * (unit * last_gain)
    last_gain_grad = jnp.sum(drop * out_grad * unit, axis=0, keepdims=True)
    local[...] = drop * norm_back(out_grad, last_gain, unit, inverse)
    to_experts.wait_receives()
    to_experts.wait_sends()
    rows = landed[...].reshape(branch.shape)
    unit_four, inverse_four = norm_stats(rows)
    gain = gain_ref[...]
    hidden = unit_four * gain
    hidden_sent[...] = hidden
    spread.start()
    router = halves(router_ref[...])
    chosen = chosen_ref[...]
    prob, gate = gate_of(hidden, router, off_ref[...], chosen)
    expert.forward(hidden, branch)
    whole_branch = branch[...]
    first_copy = 1.0
    if groups > 1:
        others, send, recv = rest
        base = s // groups * groups
        first_copy = cast_one(lax.rem(s, groups) == 0)
        copies = [
            remote(
                branch, others.at[off - 1], send.at[off - 1], recv.at[off - 1],
                (b, base + lax.rem(s + off, groups)),
            )
            for off in range(1, groups)
        ]
        for copy in copies:
            copy.start()
        for copy in copies:
            copy.wait()
        for off in range(1, groups):
            whole_branch = whole_branch + others[off - 1]
    unit_five, inverse_five = norm_stats(rows + 0.5 * gate * whole_branch)
    grad_rows = jnp.concatenate([grad_rows_a[...], grad_rows_b[...]], axis=1).reshape(branch.shape)
    last_rows_ref[...] = (first_copy * (unit_five * last_gain)).reshape(last_rows_ref.shape)
    last_gain_grad_ref[...] = last_gain_grad + first_copy * jnp.sum(
        grad_rows * unit_five, axis=0, keepdims=True
    )
    grad_four = norm_back(grad_rows, last_gain, unit_five, inverse_five)
    branch_grad = 0.5 * grad_four
    gate_grad = first_copy * jnp.sum(branch_grad * whole_branch, axis=1, keepdims=True)
    row_grad = branch_grad * gate
    grad_sent[...] = row_grad
    spread.forward()
    grad_spread.start()
    expert.backward(row_grad, hidden_grad)
    logit_grad = halves(gate_grad * gate * (chosen - prob))
    all_grad = hidden_grad[...] + dot3(logit_grad, router, NT)
    router_grad_ref[...] = dot3(logit_grad, halves(hidden), TN)
    gain_grad_ref[...] = jnp.sum(all_grad * unit_four, axis=0, keepdims=True)
    row_back = first_copy * grad_four + norm_back(all_grad, gain, unit_four, inverse_four)
    sent[...] = row_back.reshape(sent.shape)
    back.start()
    to_frames.wait_sends()
    back.wait_receives()
    grad_spread.forward()
    back_grad = local[...] + put_slots(slots_ref[...], returned, members)
    section[...] = back_grad.reshape(section.shape)
    to_utterances.start()
    to_utterances.wait_receives()
    spread.wait_receives()
    grad_spread.wait_receives()
    back.wait_sends()
    to_utterances.wait_sends()
    spread.wait_sends()
    grad_spread.wait_sends()


def mixture_both_block(
    blocks, slots, drop, out_grad, grad_rows_a, grad_rows_b, gain_row, last_gain_row, router, off, chosen,
    expert_in, expert_out, capacity, collective_id,
):
    members, row_blocks = lax.axis_size("seq"), lax.axis_size("batch")
    groups = members // EXPERTS
    parts, frame_rows, width = blocks.shape
    rows, count = parts * frame_rows, members * capacity
    vmem = pl.BlockSpec(memory_space=pltpu.VMEM)
    hbm = pl.BlockSpec(memory_space=pl.ANY)
    dma = pltpu.SemaphoreType.DMA
    slot_shape = (members, capacity, width)
    outs = [
        blocks.shape, (rows, width), slot_shape, (row_blocks, count, width),
        (row_blocks, count, width), (LANES, width), (1, width), (1, width),
    ]
    scratch = (
        [
            pltpu.VMEM(blocks.shape, F32), pltpu.VMEM(slot_shape, F32), pltpu.VMEM(slot_shape, F32),
            pltpu.VMEM(slot_shape, F32), pltpu.VMEM((count, width), F32),
            pltpu.VMEM((count, width), F32), pltpu.VMEM((count, width), F32),
            pltpu.VMEM((count, width), F32), pltpu.VMEM((rows, width), F32),
        ]
        + Expert.scratch(width, expert_in.shape[2], count)
        + ring_semaphores(parts)
        + ring_semaphores(members)
        + ring_semaphores(members)
        + ring_semaphores(parts)
        + Spread.semaphores() + [dma]
        + Spread.semaphores() + [dma]
    )
    if groups > 1:
        scratch += [pltpu.VMEM((groups - 1, count, width), F32), dma((groups,)), dma((groups,))]
    return pl.pallas_call(
        functools.partial(mixture_both_kernel, members, parts, row_blocks),
        in_specs=[hbm] + [vmem] * 10 + [hbm] * 2,
        out_specs=[vmem] * 3 + [hbm] * 2 + [vmem] * 3,
        out_shape=[jax.ShapeDtypeStruct(shape, F32) for shape in outs],
        scratch_shapes=scratch,
        compiler_params=pltpu.CompilerParams(
            collective_id=collective_id, has_side_effects=True, vmem_limit_bytes=58 * 1024 * 1024
        ),
        cost_estimate=pl.CostEstimate(
            flops=90_000_000_000, bytes_accessed=30_000_000, transcendentals=0
        ),
    )(
        blocks, slots, drop, out_grad, grad_rows_a, grad_rows_b, gain_row, last_gain_row, router, off, chosen,
        expert_in, expert_out,
    )


def grad_chunks(hidden, row_blocks):
    if square_mesh():
        return hidden // row_blocks, 2
    chunk = min(512, hidden)
    return chunk, hidden // chunk


def return_kernel(
    members, parts, row_blocks, pieces, chunks, blocks_ref, slots_ref, inward_ref, outward_ref,
    hidden_ref, out_grad_ref, *rest,
):
    dense, rest = rest[:pieces], rest[pieces:]
    grad_ref, landed_ref, dw1_ref, dw2_ref = rest[:4]
    rest = rest[4:]
    if pieces:
        dense_out, rest = rest[0], rest[1:]
    sent, buf_one, buf_two, load_sem = rest[:4]
    frame_sems, seq_sems = rest[4:7], rest[7:10]
    b = lax.axis_index("batch")
    ids = [b, row_blocks - 1 - b] if pieces else list(range(chunks))
    grads = ExpertGrads(inward_ref.at[1], outward_ref.at[1], ids, rest[10:21])
    step = members // parts
    frame_ring = Ring(blocks_ref, grad_ref, parts, step, *frame_sems)
    seq_ring = Ring(sent, landed_ref, members, 1, *seq_sems)
    peers = list(seq_ring.peers)
    if pieces:
        scatter = DenseScatter(dense, dense_out, rest[21:])
        at = Places()
        peers += [at.across_x, at.across_y]

    def load_rows(index):
        slot = index % 2
        return [
            pltpu.make_async_copy(hidden_ref.at[index], buf_one.at[slot], load_sem.at[2 * slot]),
            pltpu.make_async_copy(
                out_grad_ref.at[index], buf_two.at[slot], load_sem.at[2 * slot + 1]
            ),
        ]

    greet(peers)
    frame_ring.start()
    if pieces:
        scatter.start_cores()
    grads.start_weights()
    for load in load_rows(0):
        load.start()
    grads.finish_weights()
    if pieces:
        scatter.start_first()
    for index in range(row_blocks):
        if index + 1 < row_blocks:
            for load in load_rows(index + 1):
                load.start()
        for load in load_rows(index):
            load.wait()
        grads.block(buf_one[index % 2], buf_two[index % 2], index == 0)
        if index == 0:
            frame_ring.wait_receives()
            flat = grad_ref[...].reshape(slots_ref.shape[1], grad_ref.shape[-1])
            pick_slots(slots_ref[...], flat, sent, members)
            seq_ring.start()
        if pieces and index == 1:
            scatter.start_second()
        if pieces and index == 2:
            scatter.finish()
    grads.store(lambda index: dw1_ref.at[index], lambda index: dw2_ref.at[index])
    seq_ring.wait_receives()
    seq_ring.wait_sends()
    frame_ring.wait_sends()


def return_block(
    blocks, slots, expert_in, expert_out, hidden_all, out_grad_all, dense, capacity, collective_id
):
    members, row_blocks = lax.axis_size("seq"), hidden_all.shape[0]
    parts, frame_rows, width = blocks.shape
    count = hidden_all.shape[1]
    chunk, chunks = grad_chunks(expert_in.shape[2], row_blocks)
    vmem = pl.BlockSpec(memory_space=pltpu.VMEM)
    hbm = pl.BlockSpec(memory_space=pl.ANY)
    dma = pltpu.SemaphoreType.DMA
    dense_width = sum(piece.shape[1] for piece in dense)
    outs = [
        blocks.shape, (members, capacity, width), (chunks, width, chunk), (chunks, chunk, width),
    ]
    out_specs = [vmem, hbm, hbm, hbm]
    scratch = (
        [
            pltpu.VMEM((members, capacity, width), F32), pltpu.VMEM((2, count, width), F32),
            pltpu.VMEM((2, count, width), F32), dma((4,)),
        ]
        + ring_semaphores(parts)
        + ring_semaphores(members)
        + ExpertGrads.scratch(width, chunk, chunks, count)
    )
    if dense:
        outs.append((width // 8, dense_width))
        out_specs.append(vmem)
        scratch += DenseScatter.scratch(width, dense_width, len(dense))
    return pl.pallas_call(
        functools.partial(return_kernel, members, parts, row_blocks, len(dense), chunks),
        in_specs=[hbm, vmem] + [hbm] * (4 + len(dense)),
        out_specs=out_specs,
        out_shape=[jax.ShapeDtypeStruct(shape, F32) for shape in outs],
        scratch_shapes=scratch,
        compiler_params=pltpu.CompilerParams(
            collective_id=collective_id, has_side_effects=True, vmem_limit_bytes=60 * 1024 * 1024
        ),
        cost_estimate=pl.CostEstimate(
            flops=60_000_000_000, bytes_accessed=40_000_000, transcendentals=0
        ),
    )(blocks, slots, expert_in, expert_out, hidden_all, out_grad_all, *dense)


def back_chunk(hidden, rows):
    return min(512 if rows <= 512 else 256, hidden)


def expert_back_kernel(
    row_blocks, columns, widths, grad_ref, rows_ref, gain_ref, gate_ref, prob_ref, chosen_ref,
    router_ref, router_two_ref, gain_two_ref, gain_three_ref, gain_four_ref,
    gain_five_ref, taps_grad_ref, slots_ref, branch_ref, upper_ref, inward_ref, outward_ref, hidden_ref,
    quarter_one, quarter_two, *rest,
):
    if widths:
        dense_ref, rest = rest[0], rest[1:]
    frames_grad_ref, landed_ref, dw1_ref, dw2_ref, small_out_ref = rest[:5]
    rest = rest[5:]
    dense_outs, rest = rest[: len(widths)], rest[len(widths) :]
    sent, back_rows, returned, buf_one, buf_two, small_mine, send_b, recv_b, load_sem = rest[:9]
    ring_sems, small_refs, local_sems, rest = rest[9:12], rest[12:18], rest[18], rest[19:]
    hidden_width = inward_ref.shape[2]
    chunk = back_chunk(hidden_width, grad_ref.shape[0])
    grads = ExpertGrads(
        inward_ref.at[0], outward_ref.at[0], list(range(hidden_width // chunk)), rest[:11]
    )
    rest = rest[11:]
    ring = Ring(back_rows, returned, columns, 1, *ring_sems)
    spread = Spread(sent, landed_ref, send_b, recv_b)
    small = SmallSum(row_blocks, columns, small_refs)
    grads.start_weights()
    b = lax.axis_index("batch")
    size = quarter_one.shape[2]

    def place_of(which, index):
        part = pl.ds(pl.multiple_of(index * size, size), size)
        return dw1_ref.at[1, :, part] if which == 0 else dw2_ref.at[1, part, :]

    ids = [b, row_blocks - 1 - b] if widths else list(range(quarter_one.shape[0]))
    local = [
        pltpu.make_async_copy(
            (quarter_one, quarter_two)[j].at[i], place_of(j, index), local_sems.at[2 * i + j]
        )
        for i, index in enumerate(ids)
        for j in range(2)
    ]
    greet(small.row_peers + ring.peers)
    upper_load = pltpu.make_async_copy(upper_ref, frames_grad_ref, load_sem.at[2])
    upper_load.start()
    branch_load = pltpu.make_async_copy(branch_ref, buf_two, load_sem.at[1])
    branch_load.start()
    gate = gate_ref[...]
    sent[...] = 0.5 * grad_ref[...] * gate
    spread.start()
    if widths:
        dense = DenseGather(dense_ref, dense_outs, rest[:12])
        dense.start_line()
        send_n, recv_n = rest[12:]
        at = Places()
        quarters, into = [], []
        for i, peer in enumerate((at.across_x, at.across_y)):
            for j in range(2):
                src = (quarter_one, quarter_two)[j].at[0]
                sems = send_n.at[2 * i + j], recv_n.at[2 * i + j]
                quarters.append(remote(src, place_of(j, b), *sems, peer))
                into.append(remote(src, place_of(j, peer[0]), *sems, peer))
        for copy in quarters[::2]:
            copy.start()
    for copy in local:
        copy.start()
    grads.finish_weights()
    gain_row = gain_ref[...]
    grads.block(norm_stats(rows_ref[...])[0] * gain_row, sent[...], True, buf_one)
    unit, inverse = norm_stats(rows_ref[...])
    hidden = unit * gain_row
    branch_load.wait()
    gate_grad = jnp.sum(0.5 * grad_ref[...] * buf_two[...], axis=1, keepdims=True)
    logit_grad = halves(gate_grad * gate * (chosen_ref[...] - prob_ref[...]))
    hidden_grad = buf_one[...] + dot3(logit_grad, halves(router_ref[...]), NT)
    router_grad = dot3(logit_grad, halves(hidden), TN)
    small_mine[...] = jnp.zeros_like(small_mine)
    small_mine[:EXPERTS, :] = router_grad[:EXPERTS, :]
    small_mine[EXPERTS : 2 * EXPERTS, :] = router_two_ref[:EXPERTS, :]
    gain_one = jnp.sum(hidden_grad * unit, axis=0, keepdims=True)
    gains = (gain_one, gain_two_ref, gain_three_ref, gain_four_ref, gain_five_ref)
    for i, gain in enumerate(gains):
        small_mine[2 * EXPERTS + i : 2 * EXPERTS + i + 1, :] = gain[...]
    small_mine[3 * EXPERTS : 3 * EXPERTS + KERNEL, :] = taps_grad_ref[:KERNEL, :]
    extra = norm_back(hidden_grad, gain_row, unit, inverse)
    back_rows[...] = extra.reshape(back_rows.shape)
    ring.start()
    small.share(small_mine[...], 0)
    if widths:
        dense.start_line_back()
    spread.forward()
    if widths:
        for copy in quarters[1::2]:
            copy.start()

    def first_middle():
        small.share(small.total(0), 1)
        if widths:
            dense.start_first()

    def second_middle():
        small_out_ref[...] = small.total(1)
        if widths:
            dense.start_second()

    def third_middle():
        if widths:
            dense.start_cores()
        ring.wait_receives()
        upper_load.wait()
        frames_grad_ref[...] += put_slots(slots_ref[...], returned, columns)

    middles = [first_middle, second_middle, third_middle]
    for k in range(1, row_blocks):
        load = pltpu.make_async_copy(hidden_ref.at[k], buf_one, load_sem.at[0])
        load.start()
        spread.wait_receive(k)
        load_two = pltpu.make_async_copy(landed_ref.at[k], buf_two, load_sem.at[1])
        load_two.start()
        load.wait()
        load_two.wait()
        middle = middles[k - 1] if k <= len(middles) else None
        grads.block(buf_one[...], buf_two[...], False, None, middle)
    chunk_of = lambda index: pl.ds(index * chunk, chunk)
    grads.store(
        lambda index: dw1_ref.at[0, :, chunk_of(index)],
        lambda index: dw2_ref.at[0, chunk_of(index), :],
    )
    if widths:
        dense.finish()
        for copy in into:
            copy.wait_recv()
        for copy in quarters:
            copy.wait_send()
    for copy in local:
        copy.wait()
    ring.wait_sends()
    spread.wait_sends()


def expert_back_block(
    grad, rows, gain_row, gate, prob, chosen, router, branch, small_parts, slots, upper, expert_in,
    expert_out, hidden_all, quarters, dense, widths, collective_id,
):
    row_blocks, columns = lax.axis_size("batch"), lax.axis_size("seq")
    count, width = grad.shape
    capacity = count // columns
    hidden = expert_in.shape[2]
    chunk = back_chunk(hidden, count)
    vmem = pl.BlockSpec(memory_space=pltpu.VMEM)
    hbm = pl.BlockSpec(memory_space=pl.ANY)
    dma = pltpu.SemaphoreType.DMA
    small_shape = (5 * EXPERTS, width)
    outs = [
        upper.shape, (row_blocks, count, width), expert_in.shape, expert_out.shape, small_shape,
    ]
    outs += [(width, w) for w in widths]
    scratch = (
        [
            pltpu.VMEM((count, width), F32), pltpu.VMEM((columns, capacity, width), F32),
            pltpu.VMEM((columns, capacity, width), F32),
            pltpu.VMEM((count, width), F32), pltpu.VMEM((count, width), F32),
            pltpu.VMEM(small_shape, F32), *Spread.semaphores(),
            dma((3,)),
        ]
        + ring_semaphores(columns)
        + SmallSum.scratch(row_blocks, columns, small_shape)
        + [dma((2 * quarters[0].shape[0],))]
        + ExpertGrads.scratch(width, chunk, hidden // chunk, count)
    )
    if widths:
        scratch += DenseGather.scratch(width, sum(widths), len(widths))
        scratch += [dma((4,)), dma((4,))]
    out = pl.pallas_call(
        functools.partial(expert_back_kernel, row_blocks, columns, widths),
        in_specs=[vmem] * (8 + len(small_parts)) + [hbm] * 7 + [vmem] * len(dense),
        out_specs=[vmem] + [hbm] * 3 + [vmem] + [hbm] * len(widths),
        out_shape=[jax.ShapeDtypeStruct(shape, F32) for shape in outs],
        scratch_shapes=scratch,
        compiler_params=pltpu.CompilerParams(
            collective_id=collective_id, has_side_effects=True, vmem_limit_bytes=62 * 1024 * 1024
        ),
        cost_estimate=pl.CostEstimate(
            flops=60_000_000_000, bytes_accessed=40_000_000, transcendentals=0
        ),
    )(
        grad, rows, gain_row, gate, prob, chosen, router, *small_parts, slots, branch, upper,
        expert_in, expert_out, hidden_all, *quarters, *dense,
    )
    return out[0], out[2], out[3], out[4], out[5:]


def per_device(
    frames, out_grad, lengths, routing, norm_gains, routers, expert_in, expert_out,
    attn_qkv, attn_out, conv_in, depthwise, bn_gain, bn_bias, conv_out, running_mean, running_var,
):
    utter_count, frame_rows, width = frames.shape
    members = lax.axis_size("seq")
    step = members // utter_count
    groups = members // EXPERTS
    capacity = utter_count * frame_rows // EXPERTS
    place = lax.axis_index("seq")
    expert = place // groups
    first_copy = (place % groups == 0).astype(jnp.float32)
    row_ids = jnp.arange(frame_rows, dtype=jnp.int32)
    live_here = (place * frame_rows + row_ids)[None, :] < lengths[:, None]
    flat_frames = frames.reshape(-1, width)
    flat_grad = out_grad.reshape(-1, width)
    kept_one, slots_one = slot_matrix(routing[..., 0].reshape(-1), live_here.reshape(-1), capacity)
    kept_two, slots_two = slot_matrix(routing[..., 1].reshape(-1), live_here.reshape(-1), capacity)

    rows = utter_count * frame_rows
    block_shape = (utter_count, frame_rows, width)
    gain_rows = norm_gains.reshape(5, 1, width)
    lane = jnp.arange(LANES, dtype=jnp.int32)[None, :]
    chosen = (lane == expert).astype(F32)
    off = jnp.where(lane < EXPERTS, 0.0, NEGATIVE_FILL)
    wide_routers = jnp.pad(routers, ((0, 0), (0, 0), (0, LANES - EXPERTS)))
    section_one, rows_one, gate_one, prob_one, branch_one, hidden_one_all = mixture_block(
        flat_frames, slots_one, gain_rows[0], wide_routers[0], off, chosen, expert_in, expert_out,
        utter_count, capacity, 2,
    )
    section_one = section_one.reshape(rows, width)
    rows_one = rows_one.reshape(-1, width)

    utter = place // step
    low = place % step
    length = lax.dynamic_index_in_dim(lengths, utter, keepdims=False)
    parts = jnp.arange(utter_count, dtype=jnp.int32)

    def positions_of(offset):
        other = (low + offset) % step
        return ((parts * step + other)[:, None] * frame_rows + row_ids[None, :]).reshape(-1)

    positions = positions_of(0)
    live = (positions < length).astype(jnp.float32)[:, None]
    half = HEAD // 2
    frequency = 10000.0 ** (-jnp.arange(half, dtype=F32) / half)
    angles = positions.astype(F32)[:, None] * frequency[None, :]
    cosine, sine = jnp.cos(angles), jnp.sin(angles)
    cosine = jnp.concatenate([cosine] * (LANES // half), axis=1)
    sine = jnp.concatenate([-sine, sine] * (LANES // HEAD), axis=1)
    usable = jnp.concatenate([positions_of(i) for i in range(step)]) < length
    extra = jnp.where(
        lane == HEAD,
        jnp.where(usable, 0.0, NEGATIVE_FILL)[:, None],
        ((lane > HEAD) & (lane < HEAD + 4)).astype(F32),
    )
    queries, key_values = plain_call(
        project_kernel, [(rows, width), (rows, 2 * width)],
        [section_one, gain_rows[1], attn_qkv, cosine, sine], flops=2_500_000_000,
    )
    key_values = near_gather(key_values, step)
    half = capacity // 2
    out_blocks = slot_blocks(slots_two, flat_grad, capacity, groups)
    attended, log_total, section_two, glu_in, glu, grad_rows_a = attention_block(
        queries, key_values, extra, section_one, attn_out, gain_rows[2], conv_in, live,
        out_blocks[:, :half], 3,
    )
    glu = glu.reshape(block_shape)
    taps = jnp.concatenate([depthwise, jnp.zeros((1, width), F32)], axis=0)
    live_blocks = live.reshape(utter_count, frame_rows, 1)
    bn_rows = (bn_gain.reshape(1, width), bn_bias.reshape(1, width))
    rim_shape = (utter_count, RIM, width)
    convolved, sums, section_three, glu_before, glu_after, grad_rows_b = conv_chain(
        False, step,
        [
            block_shape, (8, width), (rows, width), rim_shape, rim_shape,
            (members, capacity - half, width),
        ],
        [glu, taps, live_blocks, *bn_rows, conv_out, section_two, out_blocks[:, half:]], [], 4, True,
    )
    frame_count = sums[2]
    averaged = sums[0] / frame_count
    variance = sums[1] / frame_count - averaged * averaged

    (
        grad_three, layer_plain, last_rows, hidden_two_all, out_grad_two_all, router_two, gain_four,
        gain_five,
    ) = mixture_both_block(
        section_three.reshape(block_shape), slots_two, 1.0 - kept_two.astype(F32)[:, None],
        flat_grad, grad_rows_a, grad_rows_b, gain_rows[3], gain_rows[4], wide_routers[1], off, chosen,
        expert_in, expert_out, capacity, 6,
    )

    grad_three = grad_three.reshape(rows, width)
    conv_out_grad, parts_sum, depthwise_grad, glu_grad = conv_chain(
        True, step, [(width, width), (8, width), (KERNEL + 1, width), block_shape],
        [
            grad_three, convolved, sums, *bn_rows, conv_out, taps, live_blocks, glu, glu_before,
            glu_after,
        ],
        [pltpu.VMEM((KERNEL, 8, width), F32), pltpu.VMEM(block_shape, F32)], 5,
    )
    bn_gain_grad, bn_bias_grad = parts_sum[0], parts_sum[1]
    conv_in_grad, gain_three, grad_two, attn_out_grad, attended_grad = plain_call(
        glu_back_kernel,
        [(width, 2 * width), (1, width), (rows, width), (width, width), (rows, width)],
        [
            glu_grad.reshape(rows, width), glu_in, section_two, gain_rows[2], conv_in, grad_three,
            attended, attn_out,
        ],
        flops=5_000_000_000,
    )
    query_grad, key_grads, value_grads, last_back = attention_back_block(
        queries, attended_grad, attended, key_values, log_total, extra, last_rows, 9
    )
    layer_out = fold_back(slots_two, last_back, capacity, groups) + layer_plain
    key_grads, value_grads = near_back(key_grads, step), near_back(value_grads, step)
    qkv_grad, gain_two, grad_one = plain_call(
        functools.partial(project_back_kernel, step),
        [(width, 3 * width), (1, width), (rows, width)],
        [
            query_grad, *key_grads, *value_grads, section_one, gain_rows[1], attn_qkv, cosine, sine,
            grad_two,
        ],
        flops=5_000_000_000,
    )

    pieces = (qkv_grad, attn_out_grad, conv_in_grad, conv_out_grad)
    in_kernel = square_mesh()
    grad_one, grad_rows, inward_two, outward_two, *dense = return_block(
        grad_one.reshape(block_shape), slots_one, expert_in, expert_out, hidden_two_all,
        out_grad_two_all, pieces if in_kernel else (), capacity, 11,
    )
    grad_one = grad_one.reshape(rows, width)
    frames_grad, expert_in_grad, expert_out_grad, small, dense = expert_back_block(
        grad_rows.reshape(-1, width), rows_one, gain_rows[0], gate_one, prob_one, chosen,
        wide_routers[0], branch_one,
        (router_two, gain_two, gain_three, gain_four, gain_five, depthwise_grad), slots_one, grad_one,
        expert_in, expert_out, hidden_one_all, (inward_two, outward_two), dense,
        tuple(p.shape[1] for p in pieces) if in_kernel else (), 13,
    )
    if not in_kernel:
        dense = lax.psum(pieces, ("batch", "seq"))
    qkv_grad, attn_out_grad, conv_in_grad, conv_out_grad = dense
    first = 2 * EXPERTS
    routers_grad = small[:first].reshape(2, EXPERTS, width).transpose(0, 2, 1)
    gains_grad = small[first : first + 5]
    depthwise_grad = small[first + EXPERTS : first + EXPERTS + KERNEL]
    new_mean = (1.0 - MOMENTUM) * running_mean + MOMENTUM * averaged
    new_var = (1.0 - MOMENTUM) * running_var + MOMENTUM * variance * frame_count / (
        frame_count - 1.0
    )
    return (
        layer_out.reshape(frames.shape), frames_grad.reshape(frames.shape), gains_grad, routers_grad,
        expert_in_grad, expert_out_grad,
        qkv_grad, attn_out_grad, conv_in_grad, depthwise_grad, bn_gain_grad, bn_bias_grad,
        conv_out_grad, new_mean, new_var,
    )


def solution(mesh):
    frame_spec = P("batch", "seq", None)
    in_specs = (
        frame_spec, frame_spec, P("batch"), frame_spec, P(), P(),
        P(None, None, "seq"), P(None, "seq", None),
    ) + (P(),) * 9
    out_specs = (
        frame_spec, frame_spec, P(), P(), P(None, None, "seq"), P(None, "seq", None),
    ) + (P(),) * 9
    return jax.shard_map(
        per_device, mesh=mesh, in_specs=in_specs, out_specs=out_specs, check_vma=False
    )
```
